128 devices in a mesh: lat: 8 (over z, core), lon: 16 (over x, y).
Axes of the slice: x: 4, y: 4, z: 4, core: 2. Of those that a mesh axis runs over, the one named last changes fastest.
Arguments:
- sea_height: float32 [512, 4096], P('lat', 'lon'), may hold values from -7.5 to 10
- trans_u: float32 [512, 4096], P('lat', 'lon'), may hold values from -3 to 3
- trans_v: float32 [512, 4096], P('lat', 'lon'), may hold values from -3 to 3
- depth: float32 [512, 4096], P('lat', 'lon'), may hold values from 0.2 to 1
- sea_mask: int32 [512, 4096], P('lat', 'lon'), may hold values 0 or 1
- freshwater_flux: float32 [512, 4096], P('lat', 'lon'), may hold values from -2 to 6
- love_factor: float32 [1024], replicated, may hold values from 0.5 to 10.8
Outputs:
- height_out: float32 [512, 4096], P('lat', 'lon')
- trans_u_out: float32 [512, 4096], P('lat', 'lon')
- trans_v_out: float32 [512, 4096], P('lat', 'lon')
- sal_height: float32 [512, 4096], P('lat', 'lon')
The draws below stay inside these ranges and needn't reach their ends.
All inputs are finite; a program needn't handle non-finite values. No bound on the sum of `sea_mask` on one device may be relied on, other than what follows from the above.
Results may differ from the reference program's by a relative error of at most 0.0003.
Values sent between devices are 32-bit elements; how exact they have to be, the bound alone decides.
No kernel may reach another device: no remote copies, remote signals or barrier semaphores. Data moves between devices by JAX's collectives and lax.ppermute only.
A program may use at most 128 MiB of HBM per device.

```python
import math
import jax
import jax.numpy as jnp
from jax import lax

NLON = 4096
DEG = 1024
ITERS = 4
NLAT = 512


def draw_sea_height(key, part):
    key = jax.random.fold_in(key, 11)
    key_phase, key_rough = jax.random.split(key)
    phases = jax.random.uniform(key_phase, (3,), jnp.float32, 0.0, 2.0 * math.pi)
    row_pos = jnp.arange(NLAT).astype(jnp.float32)[:, None] / NLAT
    col_pos = jnp.arange(NLON).astype(jnp.float32)[None, :] / NLON
    smooth = 0.5 * jnp.sin(6.0 * math.pi * col_pos + phases[0]) * jnp.cos(2.0 * math.pi * row_pos + phases[1])
    smooth = smooth + 0.3 * jnp.sin(14.0 * math.pi * col_pos + phases[2])
    rough_part = 2.5 * jnp.clip(jax.random.normal(key_rough, (NLAT, NLON), jnp.float32), -3.0, 3.0)
    mean_level = 1.5
    return mean_level + smooth + rough_part


def draw_freshwater_flux(key, part):
    key = jax.random.fold_in(key, 23)
    lat_ramp = 1.0 + 2.0 * jnp.arange(NLAT).astype(jnp.float32)[:, None] / (NLAT - 1)
    noise = 0.6 + 0.4 * jnp.clip(jax.random.normal(key, (NLAT, NLON), jnp.float32), -3.0, 3.0)
    return lat_ramp * noise


def draw_love_factor(key, part):
    key = jax.random.fold_in(key, 37)
    degree_list = jnp.arange(DEG).astype(jnp.float32)
    profile = 7.2 - 6.2 * 16.0 / (16.0 + degree_list)
    spread = jax.random.uniform(key, (DEG,), jnp.float32, 0.5, 1.5)
    return profile * spread


def plant(array, stream_key, smallest, largest):
    shape = array.shape
    spot = [jax.random.randint(jax.random.fold_in(stream_key, axis), (), 0, shape[axis]) for axis in range(len(shape))]
    array = array.at[tuple(spot)].set(smallest)
    longest = shape.index(max(shape))
    spot[longest] = (spot[longest] + 1) % shape[longest]
    return array.at[tuple(spot)].set(largest)


def steps_of(stream_key, extent, shards, low, high):
    gain, own = 1.0, jax.random.fold_in(stream_key, 6)
    for dim, parts in shards:
        heights = jnp.exp(jax.random.uniform(jax.random.fold_in(own, dim), (parts,), jnp.float32, low / len(shards), high / len(shards)))
        gain = gain * jnp.repeat(heights, extent[dim] // parts).reshape([-1 if axis == dim else 1 for axis in range(len(extent))])
    return gain


def normal_values(stream_key, shape, scale, most, cuts=(), kind=jnp.bfloat16):
    drawn = scale * jax.random.normal(stream_key, shape, jnp.float32)
    if cuts:
        drawn = drawn * steps_of(stream_key, shape, cuts, -0.22, 0.18)
    return jnp.clip(drawn, -most, most).astype(kind)


def setup_inputs(seed: int = 0) -> dict:
    seeds = jax.random.split(jax.random.key(seed), 8)
    sea_height = draw_sea_height(jax.random.fold_in(seeds[7], 71), 0)
    trans_u = normal_values(seeds[1], (NLAT, NLON), 0.5, 3.0, ((0, 8), (1, 16)), jnp.float32)
    trans_v = normal_values(seeds[2], (NLAT, NLON), 0.5, 3.0, ((0, 8), (1, 16)), jnp.float32)
    depth = jnp.clip(jnp.exp(math.log(1.0) - 1.609438 * jax.random.uniform(seeds[3], (NLAT, NLON), jnp.float32) ** steps_of(seeds[3], (NLAT, NLON), ((0, 8), (1, 16)), -0.2, 0.2)), 0.2, 1.0)
    sea_mask = plant((jax.random.randint(seeds[4], (NLAT, NLON), 0, 4) < 3).astype(jnp.int32), jax.random.fold_in(seeds[4], 1), 0, 1)
    freshwater_flux = draw_freshwater_flux(jax.random.fold_in(seeds[7], 71), 0)
    love_factor = draw_love_factor(jax.random.fold_in(seeds[7], 71), 0)
    return {"sea_height": sea_height, "trans_u": trans_u, "trans_v": trans_v, "depth": depth, "sea_mask": sea_mask, "freshwater_flux": freshwater_flux, "love_factor": love_factor}


step_time = 0.5
sal_ratio = 3.0 * 1035.0 / 5517.0

def seed_table(degrees):
    order_ids = jnp.arange(degrees, dtype=jnp.int32)
    order_f = order_ids.astype(jnp.float32)
    terms = jnp.where(order_ids > 0, jnp.log((2.0 * order_f + 1.0) / jnp.maximum(2.0 * order_f, 1.0)), 0.0 * order_f)
    values = 0.5 * math.log(2.0) + 0.5 * jnp.cumsum(terms)
    return jnp.where(order_ids == 0, 0.0 * order_f, values)

def advance(previous, current, orders, sine_lat, degree_next):
    degree_f = orders + degree_next
    factor_a = jnp.sqrt((4.0 * degree_f * degree_f - 1.0) / (degree_f * degree_f - orders * orders))
    below = degree_f - 1.0
    factor_b = jnp.sqrt((below * below - orders * orders) / (4.0 * below * below - 1.0))
    return (current, factor_a * (sine_lat * current - factor_b * previous))

def shift_north(values):
    return jnp.concatenate([values[1:], jnp.zeros_like(values[:1])], axis=0)

def shift_south(values):
    return jnp.concatenate([jnp.zeros_like(values[:1]), values[:-1]], axis=0)

def fourier_tables(width_lon, degrees):
    products = jnp.arange(width_lon, dtype=jnp.int32)[:, None] * jnp.arange(degrees, dtype=jnp.int32)[None, :] % width_lon
    angles = products.astype(jnp.float32) * (2.0 * math.pi / width_lon)
    return (jnp.cos(angles), jnp.sin(angles))

def reference(sea_height, trans_u, trans_v, depth, sea_mask, freshwater_flux, love_factor):
    spacing = 2.0 * math.pi / NLON
    sea_cells = sea_mask.astype(jnp.float32)
    latitude = (jnp.arange(NLAT).astype(jnp.float32) + 0.5 - NLAT / 2) * spacing
    center_cos = jnp.cos(latitude)[:, None]
    north_cos = jnp.cos(latitude + spacing / 2)[:, None]
    mean_flux = jnp.sum(sea_cells * center_cos * freshwater_flux) / jnp.sum(sea_cells * center_cos)
    forcing = sea_cells * (freshwater_flux - mean_flux)
    height, flux_u, flux_v = (sea_height, trans_u, trans_v)
    for repeat in range(ITERS):
        north_flux = flux_v * north_cos
        divergence = (flux_u - jnp.roll(flux_u, 1, axis=1)) / center_cos + (north_flux - shift_south(north_flux)) / center_cos
        height = height - step_time * divergence + step_time * forcing
        flux_u = sea_cells * jnp.roll(sea_cells, -1, axis=1) * (flux_u - step_time * 0.5 * (depth + jnp.roll(depth, -1, axis=1)) * (jnp.roll(height, -1, axis=1) - height) / center_cos)
        flux_v = sea_cells * shift_north(sea_cells) * (flux_v - step_time * 0.5 * (depth + shift_north(depth)) * (shift_north(height) - height))
    sea_mass = sea_cells * sea_height
    cos_table, sin_table = fourier_tables(NLON, DEG)
    cos_part = jnp.dot(sea_mass, cos_table, precision=lax.Precision.HIGHEST, preferred_element_type=jnp.float32)
    sin_part = jnp.dot(sea_mass, sin_table, precision=lax.Precision.HIGHEST, preferred_element_type=jnp.float32)
    orders = jnp.arange(DEG, dtype=jnp.int32).astype(jnp.float32)[None, :]
    sine_lat = jnp.sin(latitude)[:, None]
    seed_values = jnp.exp(seed_table(DEG)[None, :] + orders * jnp.log(center_cos))
    weights = center_cos * (spacing * spacing / (4.0 * math.pi))
    weighted_cos = cos_part * weights
    weighted_sin = sin_part * weights

    def analyse(loop_state, degree):
        previous, current = loop_state
        in_range = (orders[0] + degree.astype(jnp.float32) <= DEG - 1).astype(jnp.float32)
        cos_row = lax.optimization_barrier(jnp.sum(weighted_cos * current, axis=0)) * in_range
        sin_row = lax.optimization_barrier(jnp.sum(weighted_sin * current, axis=0)) * in_range
        previous, current = advance(previous, current, orders, sine_lat, (degree + 1).astype(jnp.float32))
        return ((previous, current), (cos_row, sin_row))
    degree_ids = jnp.arange(DEG, dtype=jnp.int32)
    final_state, coefs = lax.scan(analyse, (jnp.zeros_like(seed_values), seed_values), degree_ids)
    coef_cos, coef_sin = coefs
    degree_list = degree_ids.astype(jnp.float32)
    degree_gain = jnp.concatenate([sal_ratio * love_factor / (2.0 * degree_list + 1.0), jnp.zeros((DEG,), jnp.float32)])

    def synthesise(loop_state, inputs):
        previous, current, amp_cos, amp_sin = loop_state
        degree, cos_row, sin_row = inputs
        scaled = lax.dynamic_slice_in_dim(degree_gain, degree, DEG)
        amp_cos = amp_cos + (scaled * cos_row)[None, :] * current
        amp_sin = amp_sin + (scaled * sin_row)[None, :] * current
        previous, current = advance(previous, current, orders, sine_lat, (degree + 1).astype(jnp.float32))
        return ((previous, current, amp_cos, amp_sin), None)
    zero_state = jnp.zeros_like(seed_values)
    final_synth, unused = lax.scan(synthesise, (zero_state, seed_values, zero_state, zero_state), (degree_ids, coef_cos, coef_sin))
    amp_cos, amp_sin = (final_synth[2], final_synth[3])
    sal_field = jnp.dot(amp_cos, cos_table.T, precision=lax.Precision.HIGHEST, preferred_element_type=jnp.float32)
    sal_field = sal_field + jnp.dot(amp_sin, sin_table.T, precision=lax.Precision.HIGHEST, preferred_element_type=jnp.float32)
    sal_height = sea_cells * sal_field
    return (height, flux_u, flux_v, sal_height)
```

```python
import math

import jax
import jax.numpy as jnp
import ml_dtypes
import numpy as np
from jax import lax
from jax.experimental import pallas as pl
from jax.experimental.pallas import tpu as pltpu
from jax.sharding import PartitionSpec as P

ITERS = 4
NLON = 4096
NLAT = 512
DEG = 1024
LATS = 8
LONS = 16
DEVS = LATS * LONS
ROWS = NLAT // LATS
COLS = NLON // LONS
HALF = NLAT // 2
ORDERS = DEG // DEVS
WIDE = 4
FIELDS = 6
PAD_ROWS = ROWS + 2 * WIDE
PAD_COLS = COLS + 128
STRIP = FIELDS * WIDE
CHUNK = 128
CHUNKS = DEG // CHUNK

step_time = 0.5
sal_ratio = 3.0 * 1035.0 / 5517.0
spacing = 2.0 * math.pi / NLON

f32 = jnp.float32
bf16 = jnp.bfloat16


def split_table(values):
    high = values.astype(ml_dtypes.bfloat16)
    low = (values - high.astype(np.float64)).astype(ml_dtypes.bfloat16)
    return high, low


def wave_tables():
    order = (np.arange(DEVS)[:, None] + DEVS * np.arange(ORDERS)[None, :]).reshape(-1)
    angle = (order[:, None] * np.arange(COLS)[None, :] % NLON) * (2.0 * math.pi / NLON)
    cos_high, cos_low = split_table(np.cos(angle))
    sin_high, sin_low = split_table(np.sin(angle))
    return np.stack([cos_high, sin_high, cos_low, sin_low])


def phase_tables():
    angle = np.arange(LONS) * (2.0 * math.pi / LONS)
    return np.stack([np.cos(angle), np.sin(angle)]).astype(np.float32)


def latitude_of(rows):
    return (rows + 0.5 - NLAT / 2) * spacing


def row_tables():
    local = np.concatenate([np.arange(ROWS + WIDE), np.arange(-WIDE, 0)])
    latitude = latitude_of(np.arange(LATS)[:, None] * ROWS + local[None, :])
    both = np.stack([1.0 / np.cos(latitude), np.cos(latitude + spacing / 2)], axis=1)
    return np.broadcast_to(both[..., None], both.shape + (128,)).astype(np.float32)


def area_table():
    latitude = latitude_of(np.arange(NLAT)).reshape(LATS, ROWS, 1)
    return np.broadcast_to(np.cos(latitude), (LATS, ROWS, 128)).astype(np.float32)


def north_tables():
    latitude = latitude_of(np.arange(HALF, NLAT))
    weight = np.cos(latitude) * spacing * spacing / (4.0 * math.pi)
    table = np.stack([np.sin(latitude), np.log(np.cos(latitude)), weight])
    return np.broadcast_to(table[:, None, :], (3, 8, HALF)).astype(np.float32)


def seed_table():
    order = np.arange(1, DEG)
    grown = 0.5 * math.log(2.0) + 0.5 * np.cumsum(np.log((2.0 * order + 1.0) / (2.0 * order)))
    return np.concatenate([[0.0], grown]).reshape(ORDERS, DEVS).astype(np.float32)


def iota(shape, dim):
    return lax.broadcasted_iota(jnp.int32, shape, dim)


def halves(values):
    high = values.astype(bf16)
    low = (values - high.astype(f32)).astype(bf16)
    return high, low


def dot_nt(left, right):
    return lax.dot_general(left, right, (((1,), (1,)), ((), ())), preferred_element_type=f32)


def dot_nn(left, right):
    return lax.dot_general(left, right, (((1,), (0,)), ((), ())), preferred_element_type=f32)


def row_order(lat_index):
    row = iota((ROWS, ROWS), 0)
    col = iota((ROWS, ROWS), 1)
    south = lat_index < LATS // 2
    return jnp.where(south, (row + col == ROWS - 1).astype(f32), (row == col).astype(f32))


def reorder(matrix, values):
    return lax.dot_general(
        matrix,
        values,
        (((1,), (0,)), ((), ())),
        precision=lax.Precision.HIGHEST,
        preferred_element_type=f32,
    )


def forward_kernel(
    height, flux_u, flux_v, depth, mask, flux, wave, phase, area, message, strip_north, strip_south
):
    lat_index = lax.axis_index("lat")
    lon_index = lax.axis_index("lon")
    sea = mask[...].astype(f32)
    for slot, ref in enumerate((height, flux_u, flux_v, depth, None, flux)):
        values = sea if ref is None else ref[...]
        strip_north[slot * WIDE : (slot + 1) * WIDE, :] = values[ROWS - WIDE :, :]
        strip_south[slot * WIDE : (slot + 1) * WIDE, :] = values[:WIDE, :]

    mass = reorder(row_order(lat_index), sea * height[...])
    mass_high, mass_low = halves(mass)
    zero = jnp.zeros_like(mass_high)

    def sides(part):
        return (
            jnp.concatenate([part, zero, zero, part], axis=0),
            jnp.concatenate([zero, part, -part, zero], axis=0),
        )

    high_cos, high_sin = sides(mass_high)
    low_cos, low_sin = sides(mass_low)
    spectrum = (
        dot_nt(wave[0], high_cos)
        + dot_nt(wave[1], high_sin)
        + dot_nt(wave[0], low_cos)
        + dot_nt(wave[1], low_sin)
        + dot_nt(wave[2], high_cos)
        + dot_nt(wave[3], high_sin)
    )
    for device in range(DEVS):
        turn = (device % LONS) * lon_index % LONS
        part = spectrum[device * ORDERS : (device + 1) * ORDERS, :]
        message[device] = phase[0, turn] * part[:, :128] + phase[1, turn] * part[:, 128:]

    band = area[lat_index]
    area_cells = sea * jnp.concatenate([band, band], axis=1)
    flux_sum = jnp.sum(area_cells * flux[...])
    area_sum = jnp.sum(area_cells)
    row = iota((8, 128), 0)
    lane = iota((8, 128), 1)
    first = message[0]
    first = jnp.where((row == 0) & (lane >= 64), area_sum, first)
    message[0] = jnp.where((row == 0) & (lane == 64), flux_sum, first)


def table_kernel(north, seeds, high, low):
    device = lax.axis_index("lat") * LONS + lax.axis_index("lon")
    lane = iota((8, CHUNK), 1)
    row = iota((8, CHUNK), 0)
    seed_log = jnp.sum(jnp.where(lane == device, seeds[...], 0.0), axis=1, keepdims=True)
    order = (device + DEVS * row).astype(f32)
    sine = north[0]
    current = jnp.exp(seed_log + order[:, :1] * north[1])

    def one_chunk(chunk, state):
        previous, current = state
        step = (chunk * CHUNK + lane).astype(f32)
        below = order + step
        degree = below + 1.0
        factor_a = jnp.sqrt(
            (4.0 * degree * degree - 1.0) / ((step + 1.0) * (2.0 * order + step + 1.0))
        )
        factor_b = jnp.sqrt(
            step * (2.0 * order + step) / jnp.maximum(4.0 * below * below - 1.0, 1.0)
        )
        factor_c = factor_a * factor_b
        for pair in range(CHUNK // 2):
            kept = []
            for offset in range(2 * pair, 2 * pair + 2):
                kept.append(current)
                scaled = factor_a[:, offset : offset + 1] * sine
                behind = factor_c[:, offset : offset + 1] * previous
                previous, current = current, scaled * current - behind
            table_high, table_low = halves(jnp.concatenate(kept, axis=0))
            place = pl.ds(pl.multiple_of(chunk * (CHUNK * ORDERS) + 16 * pair, 16), 16)
            high[place, :] = table_high
            low[place, :] = table_low
        return previous, current

    lax.fori_loop(0, CHUNKS, one_chunk, (jnp.zeros_like(current), current))


def legendre_kernel(received, high, low, love, north, message, rows_scratch, gain_scratch, total):
    chunk = pl.program_id(0)
    device = lax.axis_index("lat") * LONS + lax.axis_index("lon")
    lane = iota((8, 128), 1)
    row = iota((8, 128), 0)
    left = lane < 64
    span = CHUNK * ORDERS

    @pl.when(chunk == 0)
    def _():
        bands = []
        for lat in range(LATS):
            band = received[lat * LONS]
            for lon in range(1, LONS):
                band = band + received[lat * LONS + lon]
            bands.append(band)
        whole = bands[0]
        for band in bands[1:]:
            whole = whole + band
        total[32:40, 0:128] = whole
        even = [bands[4 + part] + bands[3 - part] for part in range(4)]
        odd = [bands[4 + part] - bands[3 - part] for part in range(4)]

        def arrange(parts):
            cos_parts = []
            sin_parts = []
            for first, second in ((parts[0], parts[1]), (parts[2], parts[3])):
                cos_parts.append(jnp.where(left, first, pltpu.roll(second, 64, 1)))
                sin_parts.append(jnp.where(left, pltpu.roll(first, 64, 1), second))
            weight = north[2]
            return [
                jnp.concatenate(cos_parts, axis=1) * weight,
                jnp.concatenate(sin_parts, axis=1) * weight,
            ]

        rows = jnp.concatenate(arrange(even) + arrange(odd), axis=0)
        rows_high, rows_low = halves(rows)
        rows_scratch[0:32, :] = rows_high
        rows_scratch[32:64, :] = rows_low
        total[0:32, :] = jnp.zeros((32, HALF), f32)

        degree = (128 * row + lane).astype(f32)
        gain = sal_ratio * love[...] / (2.0 * degree + 1.0)
        turned = pltpu.roll(gain, (128 - device) % 128, 1)
        above = jnp.concatenate([turned[1:], jnp.zeros((1, 128), f32)], axis=0)
        shifted = jnp.where(lane + device < 128, turned, above)
        padded = jnp.concatenate([shifted, jnp.zeros((8, 128), f32)], axis=0)
        blocks = jnp.concatenate([padded[c : c + 8] for c in range(CHUNKS)], axis=0)
        blocks_high, blocks_low = halves(blocks)
        spread = (iota((CHUNK, span), 1) // ORDERS == iota((CHUNK, span), 0)).astype(f32).astype(bf16)
        wide = dot_nn(blocks_high, spread) + dot_nn(blocks_low, spread)
        gain_scratch[...] = wide.reshape(CHUNKS, ORDERS, span)

    rows_high = rows_scratch[0:32, :]
    both = dot_nt(rows_scratch[...], high[...])
    coefs = both[:32] + both[32:] + dot_nt(rows_high, low[...])
    gain = gain_scratch[chunk]
    column = iota((ORDERS, span), 1)
    gain = jnp.where(column % ORDERS == iota((ORDERS, span), 0), gain, 0.0)
    is_even = (column // ORDERS) % 2 == 0
    gain_even = jnp.where(is_even, gain, 0.0)
    gain_odd = gain - gain_even
    coefs = coefs * jnp.concatenate([gain_even, gain_even, gain_odd, gain_odd], axis=0)
    coefs_high, coefs_low = halves(coefs)
    both = dot_nn(jnp.concatenate([coefs_high, coefs_low], axis=0), high[...])
    total[0:32, :] += both[:32] + both[32:] + dot_nn(coefs_high, low[...])

    @pl.when(chunk == CHUNKS - 1)
    def _():
        sums = total[32:40, 0:128]
        flux_sum = jnp.sum(jnp.where((row == 0) & (lane == 64), sums, 0.0))
        area_sum = jnp.sum(jnp.where((row == 0) & (lane == 65), sums, 0.0))
        mean = jnp.full((8, 128), flux_sum, f32) / jnp.full((8, 128), area_sum, f32)
        slot = (device == 0) & (row == 0) & (lane >= 64)
        cos_even, sin_even = total[0:8, :], total[8:16, :]
        cos_odd, sin_odd = total[16:24, :], total[24:32, :]
        for north_side in (True, False):
            if north_side:
                cos_all, sin_all = cos_even + cos_odd, sin_even + sin_odd
            else:
                cos_all, sin_all = cos_even - cos_odd, sin_even - sin_odd
            for part in range(4):
                block = slice(128 * (part // 2), 128 * (part // 2) + 128)
                cos_part, sin_part = cos_all[:, block], sin_all[:, block]
                if part % 2 == 0:
                    sent = jnp.where(left, cos_part, pltpu.roll(sin_part, 64, 1))
                else:
                    sent = jnp.where(left, pltpu.roll(cos_part, 64, 1), sin_part)
                sent = jnp.where(slot, mean, sent)
                lat = 4 + part if north_side else 3 - part
                for lon in range(LONS):
                    message[lat * LONS + lon] = sent


def inverse_kernel(received, mask, wave, phase, sal_height, turned_scratch):
    lat_index = lax.axis_index("lat")
    lon_index = lax.axis_index("lon")
    sign = jnp.where(iota((8, 128), 1) < 64, 1.0, -1.0)
    for device in range(DEVS):
        turn = (device % LONS) * lon_index % LONS
        part = received[device]
        crossed = pltpu.roll(part, 64, 1) * sign
        turned_scratch[device * ORDERS : (device + 1) * ORDERS, :] = (
            phase[0, turn] * part + phase[1, turn] * crossed
        )
    turned = turned_scratch[...].T
    high, low = halves(turned)
    cos_both = jnp.concatenate([high[:64], low[:64]], axis=0)
    sin_both = jnp.concatenate([high[64:], low[64:]], axis=0)
    both = dot_nn(cos_both, wave[0]) + dot_nn(sin_both, wave[1])
    field = both[:64] + both[64:] + dot_nn(high[:64], wave[2]) + dot_nn(high[64:], wave[3])
    sal_height[...] = reorder(row_order(lat_index), field) * mask[...].astype(f32)


def column_kernel(
    height, flux_u, flux_v, depth, mask, flux, from_south, from_north, to_west, to_east, block
):
    lane = iota((128, 128), 1)
    west = jnp.zeros((128, 128), f32)
    east = jnp.zeros((128, 128), f32)
    block[PAD_ROWS:, :] = jnp.zeros((128 - PAD_ROWS, COLS), f32)
    for slot, ref in enumerate((height, flux_u, flux_v, depth, mask, flux)):
        block[0:ROWS, :] = ref[...].astype(f32)
        block[ROWS : ROWS + WIDE, :] = from_north[slot * WIDE : (slot + 1) * WIDE, :]
        block[ROWS + WIDE : PAD_ROWS, :] = from_south[slot * WIDE : (slot + 1) * WIDE, :]
        here = (lane >= slot * WIDE) & (lane < (slot + 1) * WIDE)
        west_part = block[:, 0:128]
        east_part = pltpu.roll(block[:, COLS - 128 : COLS], (WIDE + slot * WIDE) % 128, 1)
        if slot:
            west_part = pltpu.roll(west_part, slot * WIDE, 1)
        west = jnp.where(here, west_part, west)
        east = jnp.where(here, east_part, east)
    to_west[...] = west.T[:STRIP, :]
    to_east[...] = east.T[:STRIP, :]


def substep_kernel(
    height,
    flux_u,
    flux_v,
    depth,
    mask,
    flux,
    from_south,
    from_north,
    from_west,
    from_east,
    first_part,
    bands,
    height_out,
    u_out,
    v_out,
    block,
):
    lat_index = lax.axis_index("lat")
    row = iota((8, 128), 0)
    spot = iota((8, 128), 1)
    mean = jnp.sum(jnp.where((row == 0) & (spot == 64), first_part[0], 0.0))
    lane = iota((PAD_ROWS, 128), 1)
    fill = jnp.zeros((128 - STRIP, 128), f32)
    west = jnp.concatenate([from_west[...], fill], axis=0).T[:PAD_ROWS, :]
    east = jnp.concatenate([from_east[...], fill], axis=0).T[:PAD_ROWS, :]
    padded = []
    for slot, ref in enumerate((height, flux_u, flux_v, depth, mask, flux)):
        block[slot, 0:ROWS, 0:COLS] = ref[...].astype(f32)
        block[slot, ROWS : ROWS + WIDE, 0:COLS] = from_north[slot * WIDE : (slot + 1) * WIDE, :]
        block[slot, ROWS + WIDE : PAD_ROWS, 0:COLS] = from_south[slot * WIDE : (slot + 1) * WIDE, :]
        high_side = pltpu.roll(east, 128 - slot * WIDE, 1) if slot else east
        low_side = pltpu.roll(west, 128 - WIDE - slot * WIDE, 1)
        block[slot, :, COLS:] = jnp.where(
            lane < WIDE, high_side, jnp.where(lane >= 128 - WIDE, low_side, 0.0)
        )
        padded.append(block[slot])

    def eastward(values):
        return pltpu.roll(values, PAD_COLS - 1, 1)

    def northward(values):
        return pltpu.roll(values, PAD_ROWS - 1, 0)

    height_now, u_now, v_now, depth_all, sea, flux_all = padded
    inverse_cos = jnp.concatenate([bands[lat_index, 0]] * 3, axis=1)
    north_cos = jnp.concatenate([bands[lat_index, 1]] * 3, axis=1)
    forcing = step_time * sea * (flux_all - mean)
    open_u = sea * eastward(sea)
    open_v = sea * northward(sea)
    pull_u = open_u * (0.5 * step_time) * (depth_all + eastward(depth_all)) * inverse_cos
    pull_v = open_v * (0.5 * step_time) * (depth_all + northward(depth_all))
    scale = step_time * inverse_cos
    for repeat in range(ITERS):
        north_flux = v_now * north_cos
        divergence = u_now - pltpu.roll(u_now, 1, 1) + (north_flux - pltpu.roll(north_flux, 1, 0))
        height_now = height_now - scale * divergence + forcing
        u_now = open_u * u_now - pull_u * (eastward(height_now) - height_now)
        v_now = open_v * v_now - pull_v * (northward(height_now) - height_now)
    height_out[...] = height_now[:ROWS, :COLS]
    u_out[...] = u_now[:ROWS, :COLS]
    v_out[...] = v_now[:ROWS, :COLS]


def whole(space=pltpu.VMEM):
    return pl.BlockSpec(memory_space=space)


def shaped(*shape, kind=f32):
    return jax.ShapeDtypeStruct(shape, kind)


def cost(flops, moved):
    return pl.CostEstimate(flops=flops, bytes_accessed=moved, transcendentals=0)


def params(mebibytes=40):
    return pltpu.CompilerParams(vmem_limit_bytes=mebibytes << 20)


def on_device(sea_height, trans_u, trans_v, depth, sea_mask, freshwater_flux, love_factor):
    both_axes = ("lat", "lon")
    wave = jnp.asarray(wave_tables())
    phase = jnp.asarray(phase_tables())
    north = jnp.asarray(north_tables())
    fields = (sea_height, trans_u, trans_v, depth, sea_mask, freshwater_flux)

    message, strip_north, strip_south = pl.pallas_call(
        forward_kernel,
        out_shape=(shaped(DEVS, 8, 128), shaped(STRIP, COLS), shaped(STRIP, COLS)),
        in_specs=[whole()] * 7 + [whole(pltpu.SMEM), whole()],
        out_specs=(whole(),) * 3,
        compiler_params=params(),
        cost_estimate=cost(6 * 2 * 1024 * 256 * 256, 3 << 20),
        name="forward",
    )(*fields, wave, phase, jnp.asarray(area_table()))
    received = lax.all_to_all(message, both_axes, split_axis=0, concat_axis=0, tiled=True)

    upward = [(i, i + 1) for i in range(LATS - 1)]
    downward = [(i + 1, i) for i in range(LATS - 1)]
    from_south = lax.ppermute(strip_north, "lat", upward)
    from_north = lax.ppermute(strip_south, "lat", downward)
    to_west, to_east = pl.pallas_call(
        column_kernel,
        out_shape=(shaped(STRIP, 128), shaped(STRIP, 128)),
        in_specs=[whole()] * 8,
        out_specs=(whole(),) * 2,
        scratch_shapes=[pltpu.VMEM((128, COLS), f32)],
        compiler_params=params(),
        name="columns",
    )(*fields, from_south, from_north)
    from_west = lax.ppermute(to_east, "lon", [(i, (i + 1) % LONS) for i in range(LONS)])
    from_east = lax.ppermute(to_west, "lon", [((i + 1) % LONS, i) for i in range(LONS)])

    table_shape = shaped(DEG * ORDERS, HALF, kind=bf16)
    high, low = pl.pallas_call(
        table_kernel,
        out_shape=(table_shape, table_shape),
        in_specs=[whole()] * 2,
        out_specs=(whole(),) * 2,
        compiler_params=params(),
        cost_estimate=cost(DEG * ORDERS * HALF * 16, 8 << 20),
        name="table",
    )(north, jnp.asarray(seed_table()))

    span = CHUNK * ORDERS
    reply = pl.pallas_call(
        legendre_kernel,
        grid=(CHUNKS,),
        out_shape=shaped(DEVS, 8, 128),
        in_specs=[
            whole(),
            pl.BlockSpec((span, HALF), lambda chunk: (chunk, 0)),
            pl.BlockSpec((span, HALF), lambda chunk: (chunk, 0)),
            whole(),
            whole(),
        ],
        out_specs=whole(),
        scratch_shapes=[
            pltpu.VMEM((64, HALF), bf16),
            pltpu.VMEM((CHUNKS, ORDERS, span), f32),
            pltpu.VMEM((40, HALF), f32),
        ],
        compiler_params=params(),
        cost_estimate=cost(6 * 2 * 64 * 8192 * 256, 9 << 20),
        name="legendre",
    )(received, high, low, love_factor.reshape(8, 128), north)
    answer = lax.all_to_all(reply, both_axes, split_axis=0, concat_axis=0, tiled=True)

    tile = shaped(ROWS, COLS)
    height_out, u_out, v_out = pl.pallas_call(
        substep_kernel,
        grid=(1,),
        out_shape=(tile, tile, tile),
        in_specs=[whole()] * 10 + [pl.BlockSpec((1, 8, 128), lambda step: (0, 0, 0)), whole()],
        out_specs=(whole(),) * 3,
        scratch_shapes=[pltpu.VMEM((FIELDS, PAD_ROWS, PAD_COLS), f32)],
        compiler_params=params(),
        name="substeps",
    )(
        *fields,
        from_south,
        from_north,
        from_west,
        from_east,
        answer,
        jnp.asarray(row_tables()),
    )
    sal_height = pl.pallas_call(
        inverse_kernel,
        out_shape=tile,
        in_specs=[whole()] * 3 + [whole(pltpu.SMEM)],
        out_specs=whole(),
        scratch_shapes=[pltpu.VMEM((DEG, 128), f32)],
        compiler_params=params(),
        name="inverse",
    )(answer, sea_mask, wave, phase)
    return height_out, u_out, v_out, sal_height


def solution(mesh):
    tiles = P("lat", "lon")
    return jax.shard_map(
        on_device,
        mesh=mesh,
        in_specs=(tiles,) * 6 + (P(),),
        out_specs=(tiles,) * 4,
        check_vma=False,
    )
```

```python
import math

import jax
import jax.numpy as jnp
import ml_dtypes
import numpy as np
from jax import lax
from jax.experimental import pallas as pl
from jax.experimental.pallas import tpu as pltpu
from jax.sharding import PartitionSpec as P

ITERS = 4
NLON = 4096
NLAT = 512
DEG = 1024
LATS = 8
LONS = 16
DEVS = LATS * LONS
ROWS = NLAT // LATS
COLS = NLON // LONS
HALF = NLAT // 2
ORDERS = DEG // DEVS
WIDE = 4
FIELDS = 6
PAD_ROWS = ROWS + 2 * WIDE
PAD_COLS = COLS + 128
STRIP = FIELDS * WIDE
CHUNK = 128
CHUNKS = DEG // CHUNK
TILE = 256

step_time = 0.5
sal_ratio = 3.0 * 1035.0 / 5517.0
spacing = 2.0 * math.pi / NLON

f32 = jnp.float32
bf16 = jnp.bfloat16


def split_table(values):
    high = values.astype(ml_dtypes.bfloat16)
    low = (values - high.astype(np.float64)).astype(ml_dtypes.bfloat16)
    return high, low


def wave_tables():
    order = (np.arange(DEVS)[:, None] + DEVS * np.arange(ORDERS)[None, :]).reshape(-1)
    angle = (order[:, None] * np.arange(COLS)[None, :] % NLON) * (2.0 * math.pi / NLON)
    cos_high, cos_low = split_table(np.cos(angle))
    sin_high, sin_low = split_table(np.sin(angle))
    return np.stack([cos_high, sin_high, cos_low, sin_low])


def phase_tables():
    angle = np.arange(LONS)[:, None] * np.arange(LONS)[None, :] % LONS * (2.0 * math.pi / LONS)
    both = np.concatenate([np.cos(angle), np.sin(angle)], axis=1)
    return np.broadcast_to(both[..., None], both.shape + (128,)).astype(np.float32)


def balance_table():
    order = np.arange(DEG, dtype=np.float64)
    scale = np.ones(DEG)
    squares = []
    for step in range(DEG):
        squares.append(scale * scale)
        degree = order + step + 1.0
        factor = np.sqrt((4.0 * degree * degree - 1.0) / (degree * degree - order * order))
        scale = factor / scale
    return np.stack(squares, axis=1).reshape(ORDERS, DEVS, DEG).transpose(1, 0, 2).astype(np.float32)


def latitude_of(rows):
    return (rows + 0.5 - NLAT / 2) * spacing


def row_tables():
    local = np.concatenate([np.arange(ROWS + WIDE), np.arange(-WIDE, 0)])
    latitude = latitude_of(np.arange(LATS)[:, None] * ROWS + local[None, :])
    both = np.stack([1.0 / np.cos(latitude), np.cos(latitude + spacing / 2)], axis=1)
    return np.broadcast_to(both[..., None], both.shape + (128,)).astype(np.float32)


def area_table():
    latitude = latitude_of(np.arange(NLAT)).reshape(LATS, ROWS, 1)
    return np.broadcast_to(np.cos(latitude), (LATS, ROWS, 128)).astype(np.float32)


def north_tables():
    latitude = latitude_of(np.arange(HALF, NLAT))
    weight = np.cos(latitude) * spacing * spacing / (4.0 * math.pi)
    table = np.stack([np.sin(latitude), np.log(np.cos(latitude)), weight])
    return np.broadcast_to(table[:, None, :], (3, 8, HALF)).astype(np.float32)


def seed_table():
    order = np.arange(1, DEG)
    grown = 0.5 * math.log(2.0) + 0.5 * np.cumsum(np.log((2.0 * order + 1.0) / (2.0 * order)))
    return np.concatenate([[0.0], grown]).reshape(ORDERS, DEVS).astype(np.float32)


def iota(shape, dim):
    return lax.broadcasted_iota(jnp.int32, shape, dim)


def halves(values):
    high = values.astype(bf16)
    low = (values - high.astype(f32)).astype(bf16)
    return high, low


def dot_nt(left, right):
    return lax.dot_general(left, right, (((1,), (1,)), ((), ())), preferred_element_type=f32)


def dot_nn(left, right):
    return lax.dot_general(left, right, (((1,), (0,)), ((), ())), preferred_element_type=f32)


def fetch(pairs, sems):
    copies = [pltpu.make_async_copy(a, b, sems.at[slot]) for slot, (a, b) in enumerate(pairs)]
    for copy in copies:
        copy.start()
    return copies


def row_order(lat_index):
    row = iota((ROWS, ROWS), 0)
    col = iota((ROWS, ROWS), 1)
    south = lat_index < LATS // 2
    return jnp.where(south, (row + col == ROWS - 1).astype(f32), (row == col).astype(f32))


def forward_kernel(
    height_in,
    flux_u_in,
    flux_v_in,
    depth_in,
    mask_in,
    flux_in,
    wave_in,
    phase_in,
    area_in,
    message_out,
    north_out,
    south_out,
    tiles,
    mask,
    wave,
    phase,
    area,
    message,
    strips,
    sems,
    send_sem,
    strip_sems,
):
    lat_index = lax.axis_index("lat")
    lon_index = lax.axis_index("lon")
    loads = fetch(
        (
            (mask_in, mask),
            (height_in, tiles.at[0]),
            (wave_in, wave),
            (phase_in.at[lon_index], phase),
            (flux_in, tiles.at[4]),
            (area_in.at[lat_index], area),
            (flux_u_in, tiles.at[1]),
            (flux_v_in, tiles.at[2]),
            (depth_in, tiles.at[3]),
        ),
        sems,
    )
    loads[0].wait()
    loads[1].wait()
    sea = mask[...].astype(f32)
    mass_high, mass_low = halves(sea * tiles[0])
    both = jnp.concatenate([mass_high, mass_low], axis=1)
    both = dot_nn(row_order(lat_index).astype(bf16), both).astype(bf16)
    mass_high, mass_low = both[:, :COLS], both[:, COLS:]
    zero = jnp.zeros_like(mass_high)

    def sides(part):
        return (
            jnp.concatenate([part, zero, zero, part], axis=0),
            jnp.concatenate([zero, part, -part, zero], axis=0),
        )

    high_cos, high_sin = sides(mass_high)
    low_cos, low_sin = sides(mass_low)
    loads[2].wait()
    spectrum = (
        dot_nt(wave[0], high_cos)
        + dot_nt(wave[1], high_sin)
        + dot_nt(wave[0], low_cos)
        + dot_nt(wave[1], low_sin)
        + dot_nt(wave[2], high_cos)
        + dot_nt(wave[3], high_sin)
    )
    loads[3].wait()
    for device in range(DEVS):
        turn = device % LONS
        part = spectrum[device * ORDERS : (device + 1) * ORDERS, :]
        cos_turn, sin_turn = phase[turn : turn + 1, :], phase[LONS + turn : LONS + turn + 1, :]
        message[device] = cos_turn * part[:, :128] + sin_turn * part[:, 128:]

    loads[4].wait()
    loads[5].wait()
    band = area[...]
    area_cells = sea * jnp.concatenate([band, band], axis=1)
    flux_sum = jnp.sum(area_cells * tiles[4])
    area_sum = jnp.sum(area_cells)
    row = iota((8, 128), 0)
    lane = iota((8, 128), 1)
    first = message[0]
    first = jnp.where((row == 0) & (lane >= 64), area_sum, first)
    message[0] = jnp.where((row == 0) & (lane == 64), flux_sum, first)
    send = pltpu.make_async_copy(message, message_out, send_sem)
    send.start()

    for load in loads[6:]:
        load.wait()
    for slot, values in enumerate((tiles[0], tiles[1], tiles[2], tiles[3], sea, tiles[4])):
        strips[0, slot * WIDE : (slot + 1) * WIDE, :] = values[ROWS - WIDE :, :]
        strips[1, slot * WIDE : (slot + 1) * WIDE, :] = values[:WIDE, :]
    sends = fetch(((strips.at[0], north_out), (strips.at[1], south_out)), strip_sems)
    for copy in [send] + sends:
        copy.wait()


def tiles_of():
    found = []
    for chunk in range(CHUNKS):
        kept = 8 if chunk < 4 else 4 if chunk < 6 else 2
        steps = TILE // kept
        found += [(chunk, first, steps, kept) for first in range(0, CHUNK, steps)]
    return found


TILES = tiles_of()


def gain_kernel(love_in, balance_in, gains_out, love, balance, gains, sems, out_sem):
    device = lax.axis_index("lat") * LONS + lax.axis_index("lon")
    loads = fetch(((love_in, love), (balance_in.at[device], balance)), sems)
    for load in loads:
        load.wait()
    lane = iota((8, 128), 1)
    row = iota((8, 128), 0)
    degree = (128 * row + lane).astype(f32)
    gain = sal_ratio * love[...] / (2.0 * degree + 1.0)
    turned = pltpu.roll(gain, (128 - device) % 128, 1)
    above = jnp.concatenate([turned[1:], jnp.zeros((1, 128), f32)], axis=0)
    shifted = jnp.where(lane + device < 128, turned, above)
    padded = jnp.concatenate([shifted, jnp.zeros((8, 128), f32)], axis=0)
    blocks = jnp.concatenate(
        [padded[c : c + 8] * balance[:, c * CHUNK : (c + 1) * CHUNK] for c in range(CHUNKS)], axis=0
    )
    high, low = halves(blocks)
    column = iota((ORDERS, TILE), 1)
    for slot, (chunk, first, steps, kept) in enumerate(TILES):
        same = iota((CHUNK, TILE), 1) // kept + first == iota((CHUNK, TILE), 0)
        spread = same.astype(f32).astype(bf16)
        place = slice(chunk * ORDERS, (chunk + 1) * ORDERS)
        wide = dot_nn(high, spread)[place] + dot_nn(low, spread)[place]
        wide = jnp.where(column % kept == iota((ORDERS, TILE), 0), wide, 0.0)
        even = jnp.where((column // kept) % 2 == 0, wide, 0.0)
        gains[slot, 0:8, :] = even
        gains[slot, 8:16, :] = wide - even
    copy = pltpu.make_async_copy(gains, gains_out, out_sem)
    copy.start()
    copy.wait()


def legendre_kernel(
    received,
    gains_in,
    balance_in,
    seeds_in,
    north_in,
    message_out,
    gains,
    balance,
    seeds,
    north,
    high,
    low,
    message,
    sems,
    out_sems,
):
    device = lax.axis_index("lat") * LONS + lax.axis_index("lon")
    loads = fetch(
        (
            (north_in, north),
            (seeds_in, seeds),
            (balance_in.at[device], balance),
            (gains_in, gains),
        ),
        sems,
    )
    lane = iota((8, 128), 1)
    row = iota((8, 128), 0)
    left = lane < 64

    bands = []
    for lat in range(LATS):
        band = received[lat * LONS]
        for lon in range(1, LONS):
            band = band + received[lat * LONS + lon]
        bands.append(band)
    sums = bands[0]
    for band in bands[1:]:
        sums = sums + band
    even = [bands[4 + part] + bands[3 - part] for part in range(4)]
    odd = [bands[4 + part] - bands[3 - part] for part in range(4)]

    for load in loads[:3]:
        load.wait()

    def arrange(parts):
        cos_parts = []
        sin_parts = []
        for first, second in ((parts[0], parts[1]), (parts[2], parts[3])):
            cos_parts.append(jnp.where(left, first, pltpu.roll(second, 64, 1)))
            sin_parts.append(jnp.where(left, pltpu.roll(first, 64, 1), second))
        weight = north[2]
        return [
            jnp.concatenate(cos_parts, axis=1) * weight,
            jnp.concatenate(sin_parts, axis=1) * weight,
        ]

    rows_high, rows_low = halves(jnp.concatenate(arrange(even) + arrange(odd), axis=0))
    rows_both = jnp.concatenate([rows_high, rows_low], axis=0)

    sine = north[0]
    seed_log = jnp.sum(jnp.where(lane == device, seeds[...], 0.0), axis=1, keepdims=True)
    order = (device + DEVS * row).astype(f32)[:, :1]
    state = [jnp.zeros((ORDERS, HALF), f32), jnp.exp(seed_log + order * north[1])]
    wide_row = iota((ORDERS, HALF), 0)

    def extend(slot):
        chunk, first, steps, kept = TILES[slot]
        share = ORDERS // kept
        packed = []
        for step in range(first, first + steps, share):
            block = None
            for part in range(share):
                previous, current = state
                spot = chunk * CHUNK + step + part
                if part == 0:
                    block = current
                else:
                    moved = pltpu.roll(current, part * kept, 0)
                    block = jnp.where(wide_row < part * kept, block, moved)
                turn = balance[:, spot : spot + 1] * sine
                state[0], state[1] = current, turn * current - previous
            packed.append(block)
            if len(packed) == 2:
                place = slice(slot * TILE + (step - first) // share * 8 - 8, None)
                place = slice(place.start, place.start + 16)
                high[place, :], low[place, :] = halves(jnp.concatenate(packed, axis=0))
                packed = []

    def analyse(slot):
        place = slice(slot * TILE, (slot + 1) * TILE)
        both = dot_nt(rows_both, high[place, :])
        coefs = both[:32] + both[32:] + dot_nt(rows_high, low[place, :])
        even, odd = gains[slot, 0:8, :], gains[slot, 8:16, :]
        coefs_high, coefs_low = halves(coefs * jnp.concatenate([even, even, odd, odd], axis=0))
        return jnp.concatenate([coefs_high, coefs_low], axis=0)

    def synthesise(slot, coefs):
        place = slice(slot * TILE, (slot + 1) * TILE)
        return dot_nn(coefs, high[place, :]), dot_nn(coefs[:32], low[place, :])

    count = len(TILES)
    total_high = jnp.zeros((64, HALF), f32)
    total_low = jnp.zeros((32, HALF), f32)
    coefs = {}
    for turn in range(count + 2):
        if turn < count:
            extend(turn)
        if turn == 1:
            loads[3].wait()
        if 1 <= turn <= count:
            coefs[turn - 1] = analyse(turn - 1)
        if turn >= 2:
            more_high, more_low = synthesise(turn - 2, coefs.pop(turn - 2))
            total_high = total_high + more_high
            total_low = total_low + more_low
    total = total_high[:32] + total_high[32:] + total_low

    flux_sum = jnp.sum(jnp.where((row == 0) & (lane == 64), sums, 0.0))
    area_sum = jnp.sum(jnp.where((row == 0) & (lane == 65), sums, 0.0))
    mean = jnp.full((8, 128), flux_sum, f32) / jnp.full((8, 128), area_sum, f32)
    slot = (device == 0) & (row == 0) & (lane >= 64)
    cos_even, sin_even = total[0:8, :], total[8:16, :]
    cos_odd, sin_odd = total[16:24, :], total[24:32, :]
    copies = []
    for north_side in (True, False):
        if north_side:
            cos_all, sin_all = cos_even + cos_odd, sin_even + sin_odd
        else:
            cos_all, sin_all = cos_even - cos_odd, sin_even - sin_odd
        for part in range(4):
            block = slice(128 * (part // 2), 128 * (part // 2) + 128)
            cos_part, sin_part = cos_all[:, block], sin_all[:, block]
            if part % 2 == 0:
                sent = jnp.where(left, cos_part, pltpu.roll(sin_part, 64, 1))
            else:
                sent = jnp.where(left, pltpu.roll(cos_part, 64, 1), sin_part)
            sent = jnp.where(slot, mean, sent)
            lat = 4 + part if north_side else 3 - part
            for lon in range(LONS):
                message[lat * LONS + lon] = sent
            part_place = pl.ds(lat * LONS, LONS)
            copies += fetch(((message.at[part_place], message_out.at[part_place]),), out_sems.at[pl.ds(lat, 1)])
    for copy in copies:
        copy.wait()


def inverse_kernel(
    received,
    mask_in,
    wave_in,
    phase_in,
    plain_in,
    response_in,
    sal_out,
    height_out,
    u_out,
    v_out,
    mask,
    wave,
    phase,
    plain,
    response,
    turned_scratch,
    results,
    sems,
    out_sems,
    sal_sem,
):
    lat_index = lax.axis_index("lat")
    lon_index = lax.axis_index("lon")
    loads = fetch(
        (
            (phase_in.at[lon_index], phase),
            (wave_in, wave),
            (plain_in, plain),
            (response_in, response),
            (mask_in, mask),
        ),
        sems,
    )
    loads[0].wait()
    lane = iota((8, 128), 1)
    sign = jnp.where(lane[:1] < 64, 1.0, -1.0)
    for device in range(DEVS):
        turn = device % LONS
        part = received[device]
        cos_turn, sin_turn = phase[turn : turn + 1, :], phase[LONS + turn : LONS + turn + 1, :] * sign
        turned_scratch[device * ORDERS : (device + 1) * ORDERS, :] = (
            cos_turn * part + sin_turn * pltpu.roll(part, 64, 1)
        )
    turned = turned_scratch[...].T
    high, low = halves(turned)
    cos_both = jnp.concatenate([high[:64], low[:64]], axis=0)
    sin_both = jnp.concatenate([high[64:], low[64:]], axis=0)
    loads[1].wait()
    both = dot_nn(cos_both, wave[0]) + dot_nn(sin_both, wave[1])
    field = both[:64] + both[64:] + dot_nn(high[:64], wave[2]) + dot_nn(high[64:], wave[3])
    for load in loads[2:]:
        load.wait()
    mean = jnp.sum(jnp.where((iota((8, 128), 0) == 0) & (lane == 64), received[0], 0.0))
    for slot in range(3):
        results[slot] = plain[slot] - mean * response[slot]
    sends = fetch(zip((results.at[0], results.at[1], results.at[2]), (height_out, u_out, v_out)), out_sems)
    field_high, field_low = halves(field)
    order = row_order(lat_index).astype(bf16)
    field = dot_nn(order, field_high) + dot_nn(order, field_low)
    results[3] = field * mask[...].astype(f32)
    send = pltpu.make_async_copy(results.at[3], sal_out, sal_sem)
    send.start()
    for copy in sends + [send]:
        copy.wait()


def column_kernel(
    height_in,
    flux_u_in,
    flux_v_in,
    depth_in,
    mask_in,
    flux_in,
    south_in,
    north_in,
    west_out,
    east_out,
    tiles,
    mask,
    strips,
    sides,
    block,
    sems,
    out_sems,
):
    loads = fetch(
        (
            (south_in, strips.at[0]),
            (north_in, strips.at[1]),
            (height_in, tiles.at[0]),
            (flux_u_in, tiles.at[1]),
            (flux_v_in, tiles.at[2]),
            (depth_in, tiles.at[3]),
            (mask_in, mask),
            (flux_in, tiles.at[5]),
        ),
        sems,
    )
    lane = iota((128, 128), 1)
    west = jnp.zeros((128, 128), f32)
    east = jnp.zeros((128, 128), f32)
    block[PAD_ROWS:, :] = jnp.zeros((128 - PAD_ROWS, COLS), f32)
    for load in loads:
        load.wait()
    for slot in range(FIELDS):
        block[0:ROWS, :] = mask[...].astype(f32) if slot == 4 else tiles[slot]
        block[ROWS : ROWS + WIDE, :] = strips[1, slot * WIDE : (slot + 1) * WIDE, :]
        block[ROWS + WIDE : PAD_ROWS, :] = strips[0, slot * WIDE : (slot + 1) * WIDE, :]
        here = (lane >= slot * WIDE) & (lane < (slot + 1) * WIDE)
        west_part = block[:, 0:128]
        east_part = pltpu.roll(block[:, COLS - 128 : COLS], (WIDE + slot * WIDE) % 128, 1)
        if slot:
            west_part = pltpu.roll(west_part, slot * WIDE, 1)
        west = jnp.where(here, west_part, west)
        east = jnp.where(here, east_part, east)
    sides[0] = west.T[:STRIP, :]
    sides[1] = east.T[:STRIP, :]
    for copy in fetch(((sides.at[0], west_out), (sides.at[1], east_out)), out_sems):
        copy.wait()


def substep_kernel(
    height_in,
    flux_u_in,
    flux_v_in,
    depth_in,
    mask_in,
    flux_in,
    south_in,
    north_in,
    west_in,
    east_in,
    bands_in,
    plain_out,
    response_out,
    tiles,
    mask,
    strips,
    sides,
    bands,
    block,
    plain,
    response,
    sems,
    out_sems,
):
    lat_index = lax.axis_index("lat")
    loads = fetch(
        (
            (south_in, strips.at[0]),
            (north_in, strips.at[1]),
            (west_in, sides.at[0]),
            (east_in, sides.at[1]),
            (height_in, tiles.at[0]),
            (flux_u_in, tiles.at[1]),
            (flux_v_in, tiles.at[2]),
            (depth_in, tiles.at[3]),
            (mask_in, mask),
            (flux_in, tiles.at[5]),
            (bands_in.at[lat_index], bands),
        ),
        sems,
    )
    for load in loads:
        load.wait()
    lane = iota((PAD_ROWS, 128), 1)
    fill = jnp.zeros((128 - STRIP, 128), f32)
    west = jnp.concatenate([sides[0], fill], axis=0).T[:PAD_ROWS, :]
    east = jnp.concatenate([sides[1], fill], axis=0).T[:PAD_ROWS, :]
    padded = []
    for slot in range(FIELDS):
        block[slot, 0:ROWS, 0:COLS] = mask[...].astype(f32) if slot == 4 else tiles[slot]
        block[slot, ROWS : ROWS + WIDE, 0:COLS] = strips[1, slot * WIDE : (slot + 1) * WIDE, :]
        block[slot, ROWS + WIDE : PAD_ROWS, 0:COLS] = strips[0, slot * WIDE : (slot + 1) * WIDE, :]
        high_side = pltpu.roll(east, 128 - slot * WIDE, 1) if slot else east
        low_side = pltpu.roll(west, 128 - WIDE - slot * WIDE, 1)
        block[slot, :, COLS:] = jnp.where(
            lane < WIDE, high_side, jnp.where(lane >= 128 - WIDE, low_side, 0.0)
        )
        padded.append(block[slot])

    def eastward(values):
        return pltpu.roll(values, PAD_COLS - 1, 1)

    def northward(values):
        return pltpu.roll(values, PAD_ROWS - 1, 0)

    height_now, u_now, v_now, depth_all, sea, flux_all = padded
    inverse_cos = jnp.concatenate([bands[0]] * 3, axis=1)
    north_cos = jnp.concatenate([bands[1]] * 3, axis=1)
    open_u = sea * eastward(sea)
    open_v = sea * northward(sea)
    pull_u = open_u * (0.5 * step_time) * (depth_all + eastward(depth_all)) * inverse_cos
    pull_v = open_v * (0.5 * step_time) * (depth_all + northward(depth_all))
    scale = step_time * inverse_cos

    def advance(state, forcing):
        height_now, u_now, v_now = state
        north_flux = v_now * north_cos
        divergence = u_now - pltpu.roll(u_now, 1, 1) + (north_flux - pltpu.roll(north_flux, 1, 0))
        height_now = height_now - scale * divergence + forcing
        u_now = open_u * u_now - pull_u * (eastward(height_now) - height_now)
        v_now = open_v * v_now - pull_v * (northward(height_now) - height_now)
        return height_now, u_now, v_now

    own = step_time * sea
    with_flux = (height_now, u_now, v_now)
    with_one = (jnp.zeros_like(sea),) * 3
    for repeat in range(ITERS):
        with_flux = advance(with_flux, own * flux_all)
        with_one = advance(with_one, own)
    for slot in range(3):
        plain[slot] = with_flux[slot][:ROWS, :COLS]
        response[slot] = with_one[slot][:ROWS, :COLS]
    for copy in fetch(((plain, plain_out), (response, response_out)), out_sems):
        copy.wait()


def far_call(kernel, name, operands, results, scratch, work=None, here=()):
    placed = []
    specs = []
    for slot, operand in enumerate(operands):
        if slot in here:
            space = pltpu.VMEM
        else:
            space = pltpu.HBM
            operand = pltpu.with_memory_space_constraint(operand, pltpu.HBM)
        placed.append(operand)
        specs.append(pl.BlockSpec(memory_space=space))
    return pl.pallas_call(
        kernel,
        out_shape=tuple(pltpu.HBM(shape, kind) for shape, kind in results),
        in_specs=specs,
        out_specs=(pl.BlockSpec(memory_space=pltpu.HBM),) * len(results),
        scratch_shapes=scratch,
        compiler_params=pltpu.CompilerParams(vmem_limit_bytes=32 << 20),
        cost_estimate=work,
        name=name,
    )(*placed)


def cost(flops, moved):
    return pl.CostEstimate(flops=flops, bytes_accessed=moved, transcendentals=0)


def on_device(sea_height, trans_u, trans_v, depth, sea_mask, freshwater_flux, love_factor):
    both_axes = ("lat", "lon")
    wave = jnp.asarray(wave_tables())
    phase = jnp.asarray(phase_tables())
    north = jnp.asarray(north_tables())
    fields = (sea_height, trans_u, trans_v, depth, sea_mask, freshwater_flux)
    vmem = pltpu.VMEM
    copies = pltpu.SemaphoreType.DMA
    tile = ((ROWS, COLS), f32)
    strip = ((STRIP, COLS), f32)
    side = ((STRIP, 128), f32)
    messages = ((DEVS, 8, 128), f32)
    tiles = vmem((FIELDS, ROWS, COLS), f32)
    mask_tile = vmem((ROWS, COLS), jnp.int32)

    message, strip_north, strip_south = far_call(
        forward_kernel,
        "forward",
        fields + (wave, phase, jnp.asarray(area_table())),
        (messages, strip, strip),
        [
            tiles,
            mask_tile,
            vmem((4, DEG, COLS), bf16),
            vmem((2 * LONS, 128), f32),
            vmem((ROWS, 128), f32),
            vmem(*messages),
            vmem((2, STRIP, COLS), f32),
            copies((9,)),
            copies,
            copies((2,)),
        ],
        work=cost(6 * 2 * 1024 * 256 * 256, 3 << 20),
    )
    received = lax.all_to_all(message, both_axes, split_axis=0, concat_axis=0, tiled=True)

    upward = [(i, i + 1) for i in range(LATS - 1)]
    downward = [(i + 1, i) for i in range(LATS - 1)]
    from_south = lax.ppermute(strip_north, "lat", upward)
    from_north = lax.ppermute(strip_south, "lat", downward)

    balance = jnp.asarray(balance_table())
    gain_tiles = ((len(TILES), 16, TILE), f32)
    (gains,) = far_call(
        gain_kernel,
        "gains",
        (love_factor.reshape(8, 128), balance),
        (gain_tiles,),
        [
            vmem((8, 128), f32),
            vmem((ORDERS, DEG), f32),
            vmem(*gain_tiles),
            copies((2,)),
            copies,
        ],
        work=cost(2 << 20, 1 << 20),
    )
    received, from_south, from_north = lax.optimization_barrier((received, from_south, from_north))
    table = ((len(TILES) * TILE, HALF), bf16)
    (reply,) = far_call(
        legendre_kernel,
        "legendre",
        (received, gains, balance, jnp.asarray(seed_table()), north),
        (messages,),
        [
            vmem(*gain_tiles),
            vmem((ORDERS, DEG), f32),
            vmem((ORDERS, DEVS), f32),
            vmem((3, 8, HALF), f32),
            vmem(*table),
            vmem(*table),
            vmem(*messages),
            copies((4,)),
            copies((LATS,)),
        ],
        work=cost(6 * 2 * 64 * 8192 * 256, 9 << 20),
        here=(0,),
    )
    answer = lax.all_to_all(reply, both_axes, split_axis=0, concat_axis=0, tiled=True)

    to_west, to_east = far_call(
        column_kernel,
        "columns",
        fields + (from_south, from_north),
        (side, side),
        [
            tiles,
            mask_tile,
            vmem((2, STRIP, COLS), f32),
            vmem((2, STRIP, 128), f32),
            vmem((128, COLS), f32),
            copies((8,)),
            copies((2,)),
        ],
    )
    from_west = lax.ppermute(to_east, "lon", [(i, (i + 1) % LONS) for i in range(LONS)])
    from_east = lax.ppermute(to_west, "lon", [((i + 1) % LONS, i) for i in range(LONS)])

    three = ((3, ROWS, COLS), f32)
    plain, response = far_call(
        substep_kernel,
        "substeps",
        fields + (from_south, from_north, from_west, from_east, jnp.asarray(row_tables())),
        (three, three),
        [
            tiles,
            mask_tile,
            vmem((2, STRIP, COLS), f32),
            vmem((2, STRIP, 128), f32),
            vmem((2, PAD_ROWS, 128), f32),
            vmem((FIELDS, PAD_ROWS, PAD_COLS), f32),
            vmem(*three),
            vmem(*three),
            copies((11,)),
            copies((2,)),
        ],
    )
    sal_height, height_out, u_out, v_out = far_call(
        inverse_kernel,
        "inverse",
        (answer, sea_mask, wave, phase, plain, response),
        (tile,) * 4,
        [
            mask_tile,
            vmem((4, DEG, COLS), bf16),
            vmem((2 * LONS, 128), f32),
            vmem(*three),
            vmem(*three),
            vmem((DEG, 128), f32),
            vmem((4, ROWS, COLS), f32),
            copies((5,)),
            copies((3,)),
            copies,
        ],
        here=(0,),
    )
    return height_out, u_out, v_out, sal_height


def solution(mesh):
    tiles = P("lat", "lon")
    return jax.shard_map(
        on_device,
        mesh=mesh,
        in_specs=(tiles,) * 6 + (P(),),
        out_specs=(tiles,) * 4,
        check_vma=False,
    )
```

```python
import math

import jax
import jax.numpy as jnp
import ml_dtypes
import numpy as np
from jax import lax
from jax.experimental import pallas as pl
from jax.experimental.pallas import tpu as pltpu
from jax.sharding import PartitionSpec as P

ITERS = 4
NLON = 4096
NLAT = 512
DEG = 1024
LATS = 8
LONS = 16
DEVS = LATS * LONS
ROWS = NLAT // LATS
COLS = NLON // LONS
HALF = NLAT // 2
ORDERS = DEG // DEVS
WIDE = 4
FIELDS = 6
PAD_ROWS = ROWS + 2 * WIDE
PAD_COLS = COLS + 128
STRIP = FIELDS * WIDE
CHUNK = 128
CHUNKS = DEG // CHUNK
TILE = 256

step_time = 0.5
sal_ratio = 3.0 * 1035.0 / 5517.0
spacing = 2.0 * math.pi / NLON

f32 = jnp.float32
bf16 = jnp.bfloat16


def split_table(values):
    high = values.astype(ml_dtypes.bfloat16)
    low = (values - high.astype(np.float64)).astype(ml_dtypes.bfloat16)
    return high, low


def wave_tables():
    order = (np.arange(DEVS)[:, None] + DEVS * np.arange(ORDERS)[None, :]).reshape(-1)
    angle = (order[:, None] * np.arange(COLS)[None, :] % NLON) * (2.0 * math.pi / NLON)
    cos_high, cos_low = split_table(np.cos(angle))
    sin_high, sin_low = split_table(np.sin(angle))
    return np.stack([cos_high, sin_high, cos_low, sin_low])


def phase_tables():
    angle = np.arange(LONS)[:, None] * np.arange(LONS)[None, :] % LONS * (2.0 * math.pi / LONS)
    left = np.broadcast_to(np.array([np.cos(angle), -np.sin(angle)])[..., None], (2, LONS, LONS, 64))
    right = np.broadcast_to(np.array([np.sin(angle), np.cos(angle)])[..., None], (2, LONS, LONS, 64))
    both = np.concatenate([left, right], axis=-1).transpose(1, 0, 2, 3)
    return both.reshape(LONS, 2 * LONS, 128).astype(np.float32)


def balance_table():
    order = np.arange(DEG, dtype=np.float64)
    scale = np.ones(DEG)
    squares = []
    for step in range(DEG):
        squares.append(scale * scale)
        degree = order + step + 1.0
        factor = np.sqrt((4.0 * degree * degree - 1.0) / (degree * degree - order * order))
        scale = factor / scale
    return np.stack(squares, axis=1).reshape(ORDERS, DEVS, DEG).transpose(1, 0, 2).astype(np.float32)


def latitude_of(rows):
    return (rows + 0.5 - NLAT / 2) * spacing


def row_tables():
    local = np.concatenate([np.arange(ROWS + WIDE), np.arange(-WIDE, 0)])
    latitude = latitude_of(np.arange(LATS)[:, None] * ROWS + local[None, :])
    both = np.stack([1.0 / np.cos(latitude), np.cos(latitude + spacing / 2)], axis=1)
    return np.broadcast_to(both[..., None], both.shape + (128,)).astype(np.float32)


def area_table():
    latitude = latitude_of(np.arange(NLAT)).reshape(LATS, ROWS, 1)
    return np.broadcast_to(np.cos(latitude), (LATS, ROWS, 128)).astype(np.float32)


def north_tables():
    latitude = latitude_of(np.arange(HALF, NLAT))
    weight = np.cos(latitude) * spacing * spacing / (4.0 * math.pi)
    table = np.stack([np.sin(latitude), np.log(np.cos(latitude)), weight])
    return np.broadcast_to(table[:, None, :], (3, 8, HALF)).astype(np.float32)


def seed_table():
    order = np.arange(1, DEG)
    grown = 0.5 * math.log(2.0) + 0.5 * np.cumsum(np.log((2.0 * order + 1.0) / (2.0 * order)))
    return np.concatenate([[0.0], grown]).reshape(ORDERS, DEVS).astype(np.float32)


def iota(shape, dim):
    return lax.broadcasted_iota(jnp.int32, shape, dim)


def halves(values):
    high = values.astype(bf16)
    low = (values - high.astype(f32)).astype(bf16)
    return high, low


def dot_nt(left, right):
    return lax.dot_general(left, right, (((1,), (1,)), ((), ())), preferred_element_type=f32)


def dot_nn(left, right):
    return lax.dot_general(left, right, (((1,), (0,)), ((), ())), preferred_element_type=f32)


def fetch(pairs, sems):
    copies = [pltpu.make_async_copy(a, b, sems.at[slot]) for slot, (a, b) in enumerate(pairs)]
    for copy in copies:
        copy.start()
    return copies


def row_order(lat_index):
    row = iota((ROWS, ROWS), 0)
    col = iota((ROWS, ROWS), 1)
    south = lat_index < LATS // 2
    return jnp.where(south, (row + col == ROWS - 1).astype(f32), (row == col).astype(f32))


def forward_kernel(
    height_in,
    flux_u_in,
    flux_v_in,
    depth_in,
    mask_in,
    flux_in,
    wave_in,
    phase_in,
    area_in,
    message_out,
    north_out,
    south_out,
    tiles,
    mask,
    wave,
    phase,
    area,
    message,
    strips,
    sems,
    send_sems,
    strip_sems,
):
    lat_index = lax.axis_index("lat")
    lon_index = lax.axis_index("lon")
    loads = fetch(
        (
            (mask_in, mask),
            (height_in, tiles.at[0]),
            (wave_in, wave),
            (phase_in.at[lon_index], phase),
            (flux_in, tiles.at[4]),
            (area_in.at[lat_index], area),
            (flux_u_in, tiles.at[1]),
            (flux_v_in, tiles.at[2]),
            (depth_in, tiles.at[3]),
        ),
        sems,
    )
    loads[0].wait()
    loads[1].wait()
    sea = mask[...].astype(f32)
    mass_high, mass_low = halves(sea * tiles[0])
    both = jnp.concatenate([mass_high, mass_low], axis=1)
    both = dot_nn(row_order(lat_index).astype(bf16), both).astype(bf16)
    mass_high, mass_low = both[:, :COLS], both[:, COLS:]
    twice = jnp.concatenate([mass_high, mass_high], axis=0)
    all_parts = jnp.concatenate([twice, mass_low, mass_low], axis=0)

    for load in loads[3:6]:
        load.wait()
    band = area[...]
    area_cells = sea * jnp.concatenate([band, band], axis=1)
    flux_sum = jnp.sum(area_cells * tiles[4])
    area_sum = jnp.sum(area_cells)
    row = iota((8, 128), 0)
    lane = iota((8, 128), 1)

    loads[2].wait()
    sends = []
    share = DEVS // 4
    for quarter in range(4):
        place = slice(quarter * share * ORDERS, (quarter + 1) * share * ORDERS)
        cos_parts = dot_nt(wave[0, place], all_parts)
        sin_parts = dot_nt(wave[1, place], all_parts)
        cos_sums = cos_parts[:, :128] + cos_parts[:, 128:] + dot_nt(wave[2, place], twice)
        sin_sums = sin_parts[:, :128] + sin_parts[:, 128:] + dot_nt(wave[3, place], twice)
        for spot in range(share):
            device = quarter * share + spot
            turn = device % LONS
            rows = slice(spot * ORDERS, (spot + 1) * ORDERS)
            sent = (
                phase[turn : turn + 1, :] * cos_sums[rows]
                + phase[LONS + turn : LONS + turn + 1, :] * sin_sums[rows]
            )
            if device == 0:
                sent = jnp.where((row == 0) & (lane >= 64), area_sum, sent)
                sent = jnp.where((row == 0) & (lane == 64), flux_sum, sent)
            message[device] = sent
        place = pl.ds(quarter * share, share)
        pair = (message.at[place], message_out.at[place])
        sends += fetch((pair,), send_sems.at[pl.ds(quarter, 1)])

    for load in loads[6:]:
        load.wait()
    for slot, values in enumerate((tiles[0], tiles[1], tiles[2], tiles[3], sea, tiles[4])):
        strips[0, slot * WIDE : (slot + 1) * WIDE, :] = values[ROWS - WIDE :, :]
        strips[1, slot * WIDE : (slot + 1) * WIDE, :] = values[:WIDE, :]
    sends += fetch(((strips.at[0], north_out), (strips.at[1], south_out)), strip_sems)
    for copy in sends:
        copy.wait()


def tiles_of():
    found = []
    for chunk in range(CHUNKS):
        kept = 8 if chunk < 4 else 4 if chunk < 6 else 2
        steps = TILE // kept
        found += [(chunk, first, steps, kept) for first in range(0, CHUNK, steps)]
    return found


TILES = tiles_of()


def make_gains(love, balance, device, gains):
    lane = iota((8, 128), 1)
    degree = (128 * iota((8, 128), 0) + lane).astype(f32)
    gain = sal_ratio * love[...] / (2.0 * degree + 1.0)
    turned = pltpu.roll(gain, (128 - device) % 128, 1)
    above = jnp.concatenate([turned[1:], jnp.zeros((1, 128), f32)], axis=0)
    shifted = jnp.where(lane + device < 128, turned, above)
    padded = jnp.concatenate([shifted, jnp.zeros((8, 128), f32)], axis=0)
    column = iota((ORDERS, TILE), 1)
    for kept in sorted({kept for _, _, _, kept in TILES}):
        slots = [slot for slot in range(len(TILES)) if TILES[slot][3] == kept]
        chunks = sorted({TILES[slot][0] for slot in slots})
        blocks = [padded[c : c + 8] * balance[:, c * CHUNK : (c + 1) * CHUNK] for c in chunks]
        parts = jnp.concatenate(halves(jnp.concatenate(blocks, axis=0)), axis=0)
        half = len(chunks) * ORDERS
        same = column % kept == iota((ORDERS, TILE), 0)
        even_step = (column // kept) % 2 == 0
        for begin in sorted({TILES[slot][1] for slot in slots}):
            spread = iota((CHUNK, TILE), 1) // kept + begin == iota((CHUNK, TILE), 0)
            wide = dot_nn(parts, spread.astype(f32).astype(bf16))
            wide = wide[:half] + wide[half:]
            for spot, chunk in enumerate(chunks):
                slot = [slot for slot in slots if TILES[slot][:2] == (chunk, begin)][0]
                here = jnp.where(same, wide[spot * ORDERS : (spot + 1) * ORDERS], 0.0)
                even = jnp.where(even_step, here, 0.0)
                gains[slot, 0:8, :] = even
                gains[slot, 8:16, :] = here - even


def setup_kernel(
    love_in,
    balance_in,
    seeds_in,
    north_in,
    phase_in,
    gains,
    balance,
    start,
    phase,
    love,
    seeds,
    north,
    sems,
):
    device = lax.axis_index("lat") * LONS + lax.axis_index("lon")
    loads = fetch(
        (
            (seeds_in, seeds),
            (north_in, north),
            (balance_in.at[device], balance),
            (love_in, love),
            (phase_in.at[lax.axis_index("lon")], phase),
        ),
        sems,
    )
    for load in loads:
        load.wait()
    lane = iota((8, 128), 1)
    seed_log = jnp.sum(jnp.where(lane == device, seeds[...], 0.0), axis=1, keepdims=True)
    order = (device + DEVS * iota((8, 128), 0)).astype(f32)[:, :1]
    start[...] = jnp.exp(seed_log + order * north[1])
    make_gains(love, balance, device, gains)


def legendre_kernel(
    received, gains, balance, start, north, message_out, high, low, message, out_sems
):
    device = lax.axis_index("lat") * LONS + lax.axis_index("lon")
    lane = iota((8, 128), 1)
    row = iota((8, 128), 0)
    left = lane < 64

    bands = []
    for lat in range(LATS):
        band = received[lat * LONS]
        for lon in range(1, LONS):
            band = band + received[lat * LONS + lon]
        bands.append(band)
    sums = bands[0]
    for band in bands[1:]:
        sums = sums + band
    even = [bands[4 + part] + bands[3 - part] for part in range(4)]
    odd = [bands[4 + part] - bands[3 - part] for part in range(4)]

    def arrange(parts):
        cos_parts = []
        sin_parts = []
        for first, second in ((parts[0], parts[1]), (parts[2], parts[3])):
            cos_parts.append(jnp.where(left, first, pltpu.roll(second, 64, 1)))
            sin_parts.append(jnp.where(left, pltpu.roll(first, 64, 1), second))
        weight = north[2]
        return [
            jnp.concatenate(cos_parts, axis=1) * weight,
            jnp.concatenate(sin_parts, axis=1) * weight,
        ]

    rows_high, rows_low = halves(jnp.concatenate(arrange(even) + arrange(odd), axis=0))
    rows_both = jnp.concatenate([rows_high, rows_low], axis=0)

    sine = north[0]
    state = [jnp.zeros((ORDERS, HALF), f32), start[...]]
    wide_row = iota((ORDERS, HALF), 0)

    def extend(slot):
        chunk, first, steps, kept = TILES[slot]
        share = ORDERS // kept
        packed = []
        for step in range(first, first + steps, share):
            block = None
            for part in range(share):
                previous, current = state
                spot = chunk * CHUNK + step + part
                if part == 0:
                    block = current
                else:
                    moved = pltpu.roll(current, part * kept, 0)
                    block = jnp.where(wide_row < part * kept, block, moved)
                turn = balance[:, spot : spot + 1] * sine
                state[0], state[1] = current, turn * current - previous
            packed.append(block)
            if len(packed) == 2:
                place = slice(slot * TILE + (step - first) // share * 8 - 8, None)
                place = slice(place.start, place.start + 16)
                high[place, :], low[place, :] = halves(jnp.concatenate(packed, axis=0))
                packed = []

    def analyse(slot):
        place = slice(slot * TILE, (slot + 1) * TILE)
        both = dot_nt(rows_both, high[place, :])
        coefs = both[:32] + both[32:] + dot_nt(rows_high, low[place, :])
        even, odd = gains[slot, 0:8, :], gains[slot, 8:16, :]
        coefs_high, coefs_low = halves(coefs * jnp.concatenate([even, even, odd, odd], axis=0))
        return jnp.concatenate([coefs_high, coefs_low], axis=0)

    def synthesise(slot, coefs):
        place = slice(slot * TILE, (slot + 1) * TILE)
        return dot_nn(coefs, high[place, :]), dot_nn(coefs[:32], low[place, :])

    count = len(TILES)
    total_high = jnp.zeros((64, HALF), f32)
    total_low = jnp.zeros((32, HALF), f32)
    coefs = {}
    for turn in range(count + 2):
        if turn < count:
            extend(turn)
        if 1 <= turn <= count:
            coefs[turn - 1] = analyse(turn - 1)
        if turn >= 2:
            more_high, more_low = synthesise(turn - 2, coefs.pop(turn - 2))
            total_high = total_high + more_high
            total_low = total_low + more_low
    total = total_high[:32] + total_high[32:] + total_low

    flux_sum = jnp.sum(jnp.where((row == 0) & (lane == 64), sums, 0.0))
    area_sum = jnp.sum(jnp.where((row == 0) & (lane == 65), sums, 0.0))
    mean = jnp.full((8, 128), flux_sum, f32) / jnp.full((8, 128), area_sum, f32)
    slot = (device == 0) & (row == 0) & (lane >= 64)
    cos_even, sin_even = total[0:8, :], total[8:16, :]
    cos_odd, sin_odd = total[16:24, :], total[24:32, :]
    copies = []
    for north_side in (True, False):
        if north_side:
            cos_all, sin_all = cos_even + cos_odd, sin_even + sin_odd
        else:
            cos_all, sin_all = cos_even - cos_odd, sin_even - sin_odd
        for part in range(4):
            block = slice(128 * (part // 2), 128 * (part // 2) + 128)
            cos_part, sin_part = cos_all[:, block], sin_all[:, block]
            if part % 2 == 0:
                sent = jnp.where(left, cos_part, pltpu.roll(sin_part, 64, 1))
            else:
                sent = jnp.where(left, pltpu.roll(cos_part, 64, 1), sin_part)
            sent = jnp.where(slot, mean, sent)
            lat = 4 + part if north_side else 3 - part
            for lon in range(LONS):
                message[lat * LONS + lon] = sent
            part_place = pl.ds(lat * LONS, LONS)
            copies += fetch(((message.at[part_place], message_out.at[part_place]),), out_sems.at[pl.ds(lat, 1)])
    for copy in copies:
        copy.wait()


def finish_kernel(
    received,
    phase,
    west_in,
    east_in,
    wave,
    blocks_in,
    bands_in,
    height_out,
    u_out,
    v_out,
    sal_out,
    blocks,
    bands,
    turned_scratch,
    results,
    sems,
    out_sems,
):
    lat_index = lax.axis_index("lat")
    loads = fetch(
        (
            (blocks_in, blocks.at[:, :, pl.ds(0, COLS)]),
            (bands_in.at[lat_index], bands),
        ),
        sems,
    )
    lane = iota((8, 128), 1)
    left = lane < 64
    for device in range(DEVS):
        turn = device % LONS
        part = received[device]
        first, second = phase[turn : turn + 1, :], phase[LONS + turn : LONS + turn + 1, :]
        cos_turn = jnp.where(left[:1], first, second)
        sin_turn = -jnp.where(left[:1], second, first)
        turned_scratch[device * ORDERS : (device + 1) * ORDERS, :] = (
            cos_turn * part + sin_turn * pltpu.roll(part, 64, 1)
        )
    mean = jnp.sum(jnp.where((iota((8, 128), 0) == 0) & (lane == 64), received[0], 0.0))
    turned = turned_scratch[...].T
    high, low = halves(turned)
    cos_both = jnp.concatenate([high[:64], low[:64]], axis=0)
    sin_both = jnp.concatenate([high[64:], low[64:]], axis=0)

    wide_lane = iota((PAD_ROWS, 128), 1)
    fill = jnp.zeros((128 - STRIP, 128), f32)
    west = jnp.concatenate([west_in[...], fill], axis=0).T[:PAD_ROWS, :]
    east = jnp.concatenate([east_in[...], fill], axis=0).T[:PAD_ROWS, :]
    for slot in range(FIELDS):
        high_side = pltpu.roll(east, 128 - slot * WIDE, 1) if slot else east
        low_side = pltpu.roll(west, 128 - WIDE - slot * WIDE, 1)
        blocks[slot, :, COLS:] = jnp.where(
            wide_lane < WIDE, high_side, jnp.where(wide_lane >= 128 - WIDE, low_side, 0.0)
        )
    for load in loads:
        load.wait()

    both = dot_nn(cos_both, wave[0]) + dot_nn(sin_both, wave[1])
    field = both[:64] + both[64:] + dot_nn(high[:64], wave[2]) + dot_nn(high[64:], wave[3])
    field_high, field_low = halves(field)
    order = row_order(lat_index).astype(bf16)
    field = dot_nn(order, field_high) + dot_nn(order, field_low)

    def eastward(values):
        return pltpu.roll(values, PAD_COLS - 1, 1)

    def northward(values):
        return pltpu.roll(values, PAD_ROWS - 1, 0)

    height_now, u_now, v_now, depth_all, sea, flux_all = [blocks[slot] for slot in range(FIELDS)]
    inverse_cos = jnp.concatenate([bands[0]] * 3, axis=1)
    north_cos = jnp.concatenate([bands[1]] * 3, axis=1)
    open_u = sea * eastward(sea)
    open_v = sea * northward(sea)
    pull_u = open_u * (0.5 * step_time) * (depth_all + eastward(depth_all)) * inverse_cos
    pull_v = open_v * (0.5 * step_time) * (depth_all + northward(depth_all))
    scale = step_time * inverse_cos
    forcing = step_time * sea * (flux_all - mean)
    for repeat in range(ITERS):
        north_flux = v_now * north_cos
        divergence = u_now - pltpu.roll(u_now, 1, 1) + (north_flux - pltpu.roll(north_flux, 1, 0))
        height_now = height_now - scale * divergence + forcing
        u_now = open_u * u_now - pull_u * (eastward(height_now) - height_now)
        v_now = open_v * v_now - pull_v * (northward(height_now) - height_now)
    for slot, values in enumerate((height_now, u_now, v_now)):
        results[slot] = values[:ROWS, :COLS]
    results[3] = field * sea[:ROWS, :COLS]
    outs = (height_out, u_out, v_out, sal_out)
    for copy in fetch([(results.at[slot], out) for slot, out in enumerate(outs)], out_sems):
        copy.wait()


def column_kernel(
    height_in,
    flux_u_in,
    flux_v_in,
    depth_in,
    mask_in,
    flux_in,
    south_in,
    north_in,
    west_out,
    east_out,
    blocks_out,
    mask,
    strips,
    sides,
    blocks,
    sems,
    out_sems,
):
    own = pl.ds(0, ROWS)
    loads = fetch(
        (
            (south_in, strips.at[0]),
            (north_in, strips.at[1]),
            (height_in, blocks.at[0, own]),
            (flux_u_in, blocks.at[1, own]),
            (flux_v_in, blocks.at[2, own]),
            (depth_in, blocks.at[3, own]),
            (mask_in, mask),
            (flux_in, blocks.at[5, own]),
        ),
        sems,
    )
    lane = iota((PAD_ROWS, 128), 1)
    west = jnp.zeros((PAD_ROWS, 128), f32)
    east = jnp.zeros((PAD_ROWS, 128), f32)
    for load in loads:
        load.wait()
    blocks[4, 0:ROWS, :] = mask[...].astype(f32)
    for slot in range(FIELDS):
        blocks[slot, ROWS : ROWS + WIDE, :] = strips[1, slot * WIDE : (slot + 1) * WIDE, :]
        blocks[slot, ROWS + WIDE : PAD_ROWS, :] = strips[0, slot * WIDE : (slot + 1) * WIDE, :]
        here = (lane >= slot * WIDE) & (lane < (slot + 1) * WIDE)
        west_part = blocks[slot, :, 0:128]
        east_part = pltpu.roll(blocks[slot, :, COLS - 128 : COLS], (WIDE + slot * WIDE) % 128, 1)
        if slot:
            west_part = pltpu.roll(west_part, slot * WIDE, 1)
        west = jnp.where(here, west_part, west)
        east = jnp.where(here, east_part, east)
    fill = jnp.zeros((128 - PAD_ROWS, 128), f32)
    sides[0] = jnp.concatenate([west, fill], axis=0).T[:STRIP, :]
    sides[1] = jnp.concatenate([east, fill], axis=0).T[:STRIP, :]
    pairs = ((sides.at[0], west_out), (sides.at[1], east_out), (blocks, blocks_out))
    for copy in fetch(pairs, out_sems):
        copy.wait()


def far_call(kernel, name, operands, results, scratch, work=None, here=(), near=(), near_out=False):
    placed = []
    specs = []
    out_space = pltpu.VMEM if near_out else pltpu.HBM
    for slot, operand in enumerate(operands):
        if slot in here:
            space = pltpu.VMEM
        elif slot in near:
            space = pltpu.VMEM
            operand = pltpu.with_memory_space_constraint(operand, pltpu.VMEM)
        else:
            space = pltpu.HBM
            operand = pltpu.with_memory_space_constraint(operand, pltpu.HBM)
        placed.append(operand)
        specs.append(pl.BlockSpec(memory_space=space))
    return pl.pallas_call(
        kernel,
        out_shape=tuple(out_space(shape, kind) for shape, kind in results),
        in_specs=specs,
        out_specs=(pl.BlockSpec(memory_space=out_space),) * len(results),
        scratch_shapes=scratch,
        compiler_params=pltpu.CompilerParams(vmem_limit_bytes=32 << 20),
        cost_estimate=work,
        name=name,
    )(*placed)


def cost(flops, moved):
    return pl.CostEstimate(flops=flops, bytes_accessed=moved, transcendentals=0)


def on_device(sea_height, trans_u, trans_v, depth, sea_mask, freshwater_flux, love_factor):
    both_axes = ("lat", "lon")
    wave = jnp.asarray(wave_tables())
    phase = jnp.asarray(phase_tables())
    north = jnp.asarray(north_tables())
    fields = (sea_height, trans_u, trans_v, depth, sea_mask, freshwater_flux)
    vmem = pltpu.VMEM
    copies = pltpu.SemaphoreType.DMA
    tile = ((ROWS, COLS), f32)
    strip = ((STRIP, COLS), f32)
    side = ((STRIP, 128), f32)
    messages = ((DEVS, 8, 128), f32)
    tiles = vmem((FIELDS, ROWS, COLS), f32)
    mask_tile = vmem((ROWS, COLS), jnp.int32)

    message, strip_north, strip_south = far_call(
        forward_kernel,
        "forward",
        fields + (wave, phase, jnp.asarray(area_table())),
        (messages, strip, strip),
        [
            tiles,
            mask_tile,
            vmem((4, DEG, COLS), bf16),
            vmem((2 * LONS, 128), f32),
            vmem((ROWS, 128), f32),
            vmem(*messages),
            vmem((2, STRIP, COLS), f32),
            copies((9,)),
            copies((4,)),
            copies((2,)),
        ],
        work=cost(6 * 2 * 1024 * 256 * 256, 3 << 20),
    )
    received = lax.all_to_all(message, both_axes, split_axis=0, concat_axis=0, tiled=True)

    upward = [(i, i + 1) for i in range(LATS - 1)]
    downward = [(i + 1, i) for i in range(LATS - 1)]
    from_south = lax.ppermute(strip_north, "lat", upward)
    from_north = lax.ppermute(strip_south, "lat", downward)

    gain_tiles = ((len(TILES), 16, TILE), f32)
    squares = ((ORDERS, DEG), f32)
    first_rows = ((ORDERS, HALF), f32)
    turns = ((2 * LONS, 128), f32)
    gains, balance, start, phase_here = far_call(
        setup_kernel,
        "setup",
        (
            love_factor.reshape(8, 128),
            jnp.asarray(balance_table()),
            jnp.asarray(seed_table()),
            north,
            phase,
        ),
        (gain_tiles, squares, first_rows, turns),
        [
            vmem((8, 128), f32),
            vmem((ORDERS, DEVS), f32),
            vmem((3, 8, HALF), f32),
            copies((5,)),
        ],
        work=cost(2 << 20, 1 << 20),
        near_out=True,
    )
    received, from_south, from_north = lax.optimization_barrier((received, from_south, from_north))
    table = ((len(TILES) * TILE, HALF), bf16)
    (reply,) = far_call(
        legendre_kernel,
        "legendre",
        (received, gains, balance, start, north),
        (messages,),
        [vmem(*table), vmem(*table), vmem(*messages), copies((LATS,))],
        work=cost(6 * 2 * 64 * 8192 * 256, 9 << 20),
        here=(0, 4),
        near=(1, 2, 3),
    )
    answer = lax.all_to_all(reply, both_axes, split_axis=0, concat_axis=0, tiled=True)

    padded = ((FIELDS, PAD_ROWS, COLS), f32)
    to_west, to_east, blocks = far_call(
        column_kernel,
        "columns",
        fields + (from_south, from_north),
        (side, side, padded),
        [
            mask_tile,
            vmem((2, STRIP, COLS), f32),
            vmem((2, STRIP, 128), f32),
            vmem(*padded),
            copies((8,)),
            copies((3,)),
        ],
    )
    from_west = lax.ppermute(to_east, "lon", [(i, (i + 1) % LONS) for i in range(LONS)])
    from_east = lax.ppermute(to_west, "lon", [((i + 1) % LONS, i) for i in range(LONS)])

    return far_call(
        finish_kernel,
        "finish",
        (answer, phase_here, from_west, from_east, wave, blocks, jnp.asarray(row_tables())),
        (tile,) * 4,
        [
            vmem((FIELDS, PAD_ROWS, PAD_COLS), f32),
            vmem((2, PAD_ROWS, 128), f32),
            vmem((DEG, 128), f32),
            vmem((4, ROWS, COLS), f32),
            copies((2,)),
            copies((4,)),
        ],
        here=(0, 2, 3, 4),
        near=(1,),
    )


def solution(mesh):
    tiles = P("lat", "lon")
    return jax.shard_map(
        on_device,
        mesh=mesh,
        in_specs=(tiles,) * 6 + (P(),),
        out_specs=(tiles,) * 4,
        check_vma=False,
    )
```

```python
import math

import jax
import jax.numpy as jnp
import ml_dtypes
import numpy as np
from jax import lax
from jax.experimental import pallas as pl
from jax.experimental.pallas import tpu as pltpu
from jax.sharding import PartitionSpec as P

ITERS = 4
NLON = 4096
NLAT = 512
DEG = 1024
LATS = 8
LONS = 16
DEVS = LATS * LONS
ROWS = NLAT // LATS
COLS = NLON // LONS
HALF = NLAT // 2
ORDERS = DEG // DEVS
WIDE = 4
FIELDS = 6
PAD_ROWS = ROWS + 2 * WIDE
PAD_COLS = COLS + 128
STRIP = FIELDS * WIDE
CHUNK = 128
CHUNKS = DEG // CHUNK
TILE = 256
QUARTERS = 4
QUARTER = DEG // QUARTERS

step_time = 0.5
sal_ratio = 3.0 * 1035.0 / 5517.0
spacing = 2.0 * math.pi / NLON

f32 = jnp.float32
bf16 = jnp.bfloat16


def turn_tables():
    column = np.arange(NLON).reshape(LONS, 1, COLS)
    angle = column * np.arange(DEVS)[None, :, None] % NLON * (2.0 * math.pi / NLON)
    return np.stack([np.cos(angle), np.sin(angle)], axis=1).astype(np.float32)


def step_tables():
    angle = np.arange(ORDERS)[:, None] * DEVS * np.arange(COLS)[None, :] % NLON
    angle = angle * (2.0 * math.pi / NLON)
    return np.stack([np.cos(angle), np.sin(angle)]).astype(np.float32)


def balance_table():
    order = np.arange(DEG, dtype=np.float64)
    scale = np.ones(DEG)
    squares = []
    for step in range(DEG):
        squares.append(scale * scale)
        degree = order + step + 1.0
        factor = np.sqrt((4.0 * degree * degree - 1.0) / (degree * degree - order * order))
        scale = factor / scale
    return np.stack(squares, axis=1).reshape(ORDERS, DEVS, DEG).transpose(1, 0, 2).astype(np.float32)


def latitude_of(rows):
    return (rows + 0.5 - NLAT / 2) * spacing


def row_tables():
    local = np.concatenate([np.arange(ROWS + WIDE), np.arange(-WIDE, 0)])
    latitude = latitude_of(np.arange(LATS)[:, None] * ROWS + local[None, :])
    both = np.stack([1.0 / np.cos(latitude), np.cos(latitude + spacing / 2)], axis=1)
    return np.broadcast_to(both[..., None], both.shape + (128,)).astype(np.float32)


def area_table():
    latitude = latitude_of(np.arange(NLAT)).reshape(LATS, ROWS, 1)
    return np.broadcast_to(np.cos(latitude), (LATS, ROWS, 128)).astype(np.float32)


def north_tables():
    latitude = latitude_of(np.arange(HALF, NLAT))
    weight = np.cos(latitude) * spacing * spacing / (4.0 * math.pi)
    table = np.stack([np.sin(latitude), np.log(np.cos(latitude)), weight])
    return np.broadcast_to(table[:, None, :], (3, 8, HALF)).astype(np.float32)


def seed_table():
    order = np.arange(1, DEG)
    grown = 0.5 * math.log(2.0) + 0.5 * np.cumsum(np.log((2.0 * order + 1.0) / (2.0 * order)))
    return np.concatenate([[0.0], grown]).reshape(ORDERS, DEVS).astype(np.float32)


def iota(shape, dim):
    return lax.broadcasted_iota(jnp.int32, shape, dim)


def halves(values):
    high = values.astype(bf16)
    low = (values - high.astype(f32)).astype(bf16)
    return high, low


def dot_nt(left, right):
    return lax.dot_general(left, right, (((1,), (1,)), ((), ())), preferred_element_type=f32)


def dot_nn(left, right):
    return lax.dot_general(left, right, (((1,), (0,)), ((), ())), preferred_element_type=f32)


def fetch(pairs, sems):
    copies = [pltpu.make_async_copy(a, b, sems.at[slot]) for slot, (a, b) in enumerate(pairs)]
    for copy in copies:
        copy.start()
    return copies


def row_order(lat_index):
    row = iota((ROWS, ROWS), 0)
    col = iota((ROWS, ROWS), 1)
    south = lat_index < LATS // 2
    return jnp.where(south, (row + col == ROWS - 1).astype(f32), (row == col).astype(f32))


def forward_kernel(
    height_in,
    flux_u_in,
    flux_v_in,
    depth_in,
    mask_in,
    flux_in,
    turn_in,
    step_in,
    area_in,
    message_out,
    north_out,
    south_out,
    wave,
    tiles,
    mask,
    turn,
    step,
    area,
    message,
    strips,
    sems,
    send_sems,
    strip_sems,
):
    lat_index = lax.axis_index("lat")
    loads = fetch(
        (
            (mask_in, mask),
            (height_in, tiles.at[0]),
            (turn_in.at[lax.axis_index("lon")], turn),
            (step_in, step),
            (flux_in, tiles.at[4]),
            (area_in.at[lat_index], area),
            (flux_u_in, tiles.at[1]),
            (flux_v_in, tiles.at[2]),
            (depth_in, tiles.at[3]),
        ),
        sems,
    )
    for load in loads[:6]:
        load.wait()
    sea = mask[...].astype(f32)
    mass_high, mass_low = halves(sea * tiles[0])
    both = jnp.concatenate([mass_high, mass_low], axis=1)
    both = dot_nn(row_order(lat_index).astype(bf16), both).astype(bf16)
    mass_high, mass_low = both[:, :COLS], both[:, COLS:]
    zero = jnp.zeros_like(mass_high)
    for_cos = jnp.concatenate([mass_high, zero, mass_low, zero], axis=0)
    for_sin = jnp.concatenate([zero, mass_high, zero, mass_low], axis=0)

    band = area[...]
    area_cells = sea * jnp.concatenate([band, band], axis=1)
    flux_sum = jnp.sum(area_cells * tiles[4])
    area_sum = jnp.sum(area_cells)
    row = iota((8, 128), 0)
    lane = iota((8, 128), 1)

    step_cos, step_sin = step[0], step[1]
    share = DEVS // QUARTERS
    sends = []
    for quarter in range(QUARTERS):
        for pair in range(share // 2):
            cos_rows = []
            sin_rows = []
            for device in (quarter * share + 2 * pair, quarter * share + 2 * pair + 1):
                turn_cos, turn_sin = turn[0, device : device + 1, :], turn[1, device : device + 1, :]
                cos_rows.append(turn_cos * step_cos - turn_sin * step_sin)
                sin_rows.append(turn_sin * step_cos + turn_cos * step_sin)
            rows = slice(2 * ORDERS * pair, 2 * ORDERS * (pair + 1))
            for slot, parts in enumerate((cos_rows, sin_rows)):
                high, low = halves(jnp.concatenate(parts, axis=0))
                wave[quarter, slot, rows, :] = high
                wave[quarter, 2 + slot, rows, :] = low
        sums = dot_nt(wave[quarter, 0], for_cos) + dot_nt(wave[quarter, 1], for_sin)
        sums = sums[:, :128] + sums[:, 128:]
        sums = sums + dot_nt(wave[quarter, 2], for_cos[:128]) + dot_nt(wave[quarter, 3], for_sin[:128])
        for spot in range(share):
            sent = sums[spot * ORDERS : (spot + 1) * ORDERS]
            if quarter == 0 and spot == 0:
                sent = jnp.where((row == 0) & (lane >= 64), area_sum, sent)
                sent = jnp.where((row == 0) & (lane == 64), flux_sum, sent)
            message[quarter * share + spot] = sent
        place = pl.ds(quarter * share, share)
        pair = (message.at[place], message_out.at[place])
        sends += fetch((pair,), send_sems.at[pl.ds(quarter, 1)])
    for load in loads[6:]:
        load.wait()
    for slot, values in enumerate((tiles[0], tiles[1], tiles[2], tiles[3], sea, tiles[4])):
        strips[0, slot * WIDE : (slot + 1) * WIDE, :] = values[ROWS - WIDE :, :]
        strips[1, slot * WIDE : (slot + 1) * WIDE, :] = values[:WIDE, :]
    sends += fetch(((strips.at[0], north_out), (strips.at[1], south_out)), strip_sems)
    for copy in sends:
        copy.wait()


def pairs_of():
    found = []
    for first, last, kept in ((0, 512, 8), (512, 768, 4), (768, 1024, 2)):
        steps = 2 * TILE // kept
        found += [(start, steps, kept) for start in range(first, last, steps)]
    return found


PAIRS = pairs_of()


def make_gains(love, balance, device, gains):
    lane = iota((8, 128), 1)
    degree = (128 * iota((8, 128), 0) + lane).astype(f32)
    gain = sal_ratio * love[...] / (2.0 * degree + 1.0)
    turned = pltpu.roll(gain, (128 - device) % 128, 1)
    above = jnp.concatenate([turned[1:], jnp.zeros((1, 128), f32)], axis=0)
    shifted = jnp.where(lane + device < 128, turned, above)
    padded = jnp.concatenate([shifted, jnp.zeros((8, 128), f32)], axis=0)
    for pair, (first, steps, kept) in enumerate(PAIRS):
        chunks = range(first // CHUNK, -(-(first + steps) // CHUNK))
        width = CHUNK * len(chunks)
        blocks = [padded[c : c + 8] * balance[:, c * CHUNK : (c + 1) * CHUNK] for c in chunks]
        parts = jnp.concatenate(halves(jnp.concatenate(blocks, axis=1)), axis=0)
        same = iota((ORDERS, TILE), 1) % kept == iota((ORDERS, TILE), 0)
        for parity in range(2):
            step = first % CHUNK + 2 * (iota((width, TILE), 1) // kept) + parity
            spread = (step == iota((width, TILE), 0)).astype(f32).astype(bf16)
            wide = dot_nn(parts, spread)
            gains[2 * pair + parity] = jnp.where(same, wide[:ORDERS] + wide[ORDERS:], 0.0)


def setup_kernel(
    love_in,
    balance_in,
    seeds_in,
    north_in,
    gains,
    balance,
    start,
    love,
    seeds,
    north,
    sems,
):
    device = lax.axis_index("lat") * LONS + lax.axis_index("lon")
    loads = fetch(
        (
            (seeds_in, seeds),
            (north_in, north),
            (balance_in.at[device], balance),
            (love_in, love),
        ),
        sems,
    )
    for load in loads:
        load.wait()
    lane = iota((8, 128), 1)
    seed_log = jnp.sum(jnp.where(lane == device, seeds[...], 0.0), axis=1, keepdims=True)
    order = (device + DEVS * iota((8, 128), 0)).astype(f32)[:, :1]
    start[...] = jnp.exp(seed_log + order * north[1])
    make_gains(love, balance, device, gains)


def legendre_kernel(
    received, gains, balance, start, north, message_out, high, low, message, out_sems
):
    device = lax.axis_index("lat") * LONS + lax.axis_index("lon")
    lane = iota((8, 128), 1)
    row = iota((8, 128), 0)
    left = lane < 64

    bands = []
    for lat in range(LATS):
        band = received[lat * LONS]
        for lon in range(1, LONS):
            band = band + received[lat * LONS + lon]
        bands.append(band)
    sums = bands[0]
    for band in bands[1:]:
        sums = sums + band
    even = [bands[4 + part] + bands[3 - part] for part in range(4)]
    odd = [bands[4 + part] - bands[3 - part] for part in range(4)]

    def arrange(parts):
        cos_parts = []
        sin_parts = []
        for first, second in ((parts[0], parts[1]), (parts[2], parts[3])):
            cos_parts.append(jnp.where(left, first, pltpu.roll(second, 64, 1)))
            sin_parts.append(jnp.where(left, pltpu.roll(first, 64, 1), second))
        weight = north[2]
        return [
            jnp.concatenate(cos_parts, axis=1) * weight,
            jnp.concatenate(sin_parts, axis=1) * weight,
        ]

    lefts = []
    for parts in (even, odd):
        rows_high, rows_low = halves(jnp.concatenate(arrange(parts), axis=0))
        lefts.append(jnp.concatenate([rows_high, rows_low], axis=0))

    sine = north[0]
    state = [jnp.zeros((ORDERS, HALF), f32), start[...]]
    wide_row = iota((ORDERS, HALF), 0)

    def extend(pair):
        first, steps, kept = PAIRS[pair]
        share = ORDERS // kept
        block, packed, place = [None, None], [[], []], [2 * pair * TILE, (2 * pair + 1) * TILE]
        for step in range(steps):
            parity, part = step % 2, step // 2 % share
            previous, current = state
            if part == 0:
                block[parity] = current
            else:
                moved = pltpu.roll(current, part * kept, 0)
                block[parity] = jnp.where(wide_row < part * kept, block[parity], moved)
            turn = balance[:, first + step : first + step + 1] * sine
            state[0], state[1] = current, turn * current - previous
            if part == share - 1:
                packed[parity].append(block[parity])
            if len(packed[parity]) == 2:
                rows = slice(place[parity], place[parity] + 16)
                high[rows, :], low[rows, :] = halves(jnp.concatenate(packed[parity], axis=0))
                packed[parity] = []
                place[parity] += 16

    def analyse(tile):
        place = slice(tile * TILE, (tile + 1) * TILE)
        left_rows = lefts[tile % 2]
        both = dot_nt(left_rows, high[place, :])
        found = both[:16] + both[16:] + dot_nt(left_rows[:16], low[place, :])
        gain = gains[tile]
        return jnp.concatenate(halves(found * jnp.concatenate([gain, gain], axis=0)), axis=0)

    def synthesise(tile, coefs):
        place = slice(tile * TILE, (tile + 1) * TILE)
        return dot_nn(coefs, high[place, :]), dot_nn(coefs[:16], low[place, :])

    count = len(PAIRS)
    total_high = [jnp.zeros((32, HALF), f32)] * 2
    total_low = [jnp.zeros((16, HALF), f32)] * 2
    coefs = {}
    for turn in range(count + 2):
        if turn < count:
            extend(turn)
        for parity in range(2):
            if 1 <= turn <= count:
                tile = 2 * (turn - 1) + parity
                coefs[tile] = analyse(tile)
        for parity in range(2):
            if turn >= 2:
                tile = 2 * (turn - 2) + parity
                more_high, more_low = synthesise(tile, coefs.pop(tile))
                total_high[parity] = total_high[parity] + more_high
                total_low[parity] = total_low[parity] + more_low
    total_even, total_odd = [
        total_high[parity][:16] + total_high[parity][16:] + total_low[parity] for parity in range(2)
    ]

    flux_sum = jnp.sum(jnp.where((row == 0) & (lane == 64), sums, 0.0))
    area_sum = jnp.sum(jnp.where((row == 0) & (lane == 65), sums, 0.0))
    mean = jnp.full((8, 128), flux_sum, f32) / jnp.full((8, 128), area_sum, f32)
    slot = (device == 0) & (row == 0) & (lane >= 64)
    cos_even, sin_even = total_even[0:8, :], total_even[8:16, :]
    cos_odd, sin_odd = total_odd[0:8, :], total_odd[8:16, :]
    copies = []
    for north_side in (True, False):
        if north_side:
            cos_all, sin_all = cos_even + cos_odd, sin_even + sin_odd
        else:
            cos_all, sin_all = cos_even - cos_odd, sin_even - sin_odd
        for part in range(4):
            block = slice(128 * (part // 2), 128 * (part // 2) + 128)
            cos_part, sin_part = cos_all[:, block], sin_all[:, block]
            if part % 2 == 0:
                sent = jnp.where(left, cos_part, pltpu.roll(sin_part, 64, 1))
            else:
                sent = jnp.where(left, pltpu.roll(cos_part, 64, 1), sin_part)
            sent = jnp.where(slot, mean, sent)
            lat = 4 + part if north_side else 3 - part
            for lon in range(LONS):
                message[lat * LONS + lon] = sent
            part_place = pl.ds(lat * LONS, LONS)
            copies += fetch(((message.at[part_place], message_out.at[part_place]),), out_sems.at[pl.ds(lat, 1)])
    for copy in copies:
        copy.wait()


def finish_kernel(
    received,
    west_in,
    east_in,
    wave,
    tiles,
    bands,
    height_out,
    u_out,
    v_out,
    sal_out,
    blocks,
    results,
    out_sems,
):
    lat_index = lax.axis_index("lat")
    lane = iota((8, 128), 1)
    mean = jnp.sum(jnp.where((iota((8, 128), 0) == 0) & (lane == 64), received[0], 0.0))
    turned = received[...].reshape(DEG, 128).T
    high, low = halves(turned)
    cos_both = jnp.concatenate([high[:64], low[:64]], axis=0)
    sin_both = jnp.concatenate([high[64:], low[64:]], axis=0)

    wide_lane = iota((PAD_ROWS, 128), 1)
    fill = jnp.zeros((128 - STRIP, 128), f32)
    west = jnp.concatenate([west_in[...], fill], axis=0).T[:PAD_ROWS, :]
    east = jnp.concatenate([east_in[...], fill], axis=0).T[:PAD_ROWS, :]
    for slot in range(FIELDS):
        high_side = pltpu.roll(east, 128 - slot * WIDE, 1) if slot else east
        low_side = pltpu.roll(west, 128 - WIDE - slot * WIDE, 1)
        blocks[slot, :, :COLS] = tiles[slot]
        blocks[slot, :, COLS:] = jnp.where(
            wide_lane < WIDE, high_side, jnp.where(wide_lane >= 128 - WIDE, low_side, 0.0)
        )
    both = jnp.zeros((2 * ROWS, COLS), f32)
    field = jnp.zeros((ROWS, COLS), f32)
    for part in range(QUARTERS):
        place = slice(part * QUARTER, (part + 1) * QUARTER)
        both += dot_nn(cos_both[:, place], wave[part, 0]) + dot_nn(sin_both[:, place], wave[part, 1])
        field += dot_nn(high[:64, place], wave[part, 2]) + dot_nn(high[64:, place], wave[part, 3])
    field = field + both[:64] + both[64:]
    field_high, field_low = halves(field)
    order = row_order(lat_index).astype(bf16)
    field = dot_nn(order, field_high) + dot_nn(order, field_low)

    def eastward(values):
        return pltpu.roll(values, PAD_COLS - 1, 1)

    def northward(values):
        return pltpu.roll(values, PAD_ROWS - 1, 0)

    height_now, u_now, v_now, depth_all, sea, flux_all = [blocks[slot] for slot in range(FIELDS)]
    inverse_cos = jnp.concatenate([bands[0]] * 3, axis=1)
    north_cos = jnp.concatenate([bands[1]] * 3, axis=1)
    open_u = sea * eastward(sea)
    open_v = sea * northward(sea)
    pull_u = open_u * (0.5 * step_time) * (depth_all + eastward(depth_all)) * inverse_cos
    pull_v = open_v * (0.5 * step_time) * (depth_all + northward(depth_all))
    scale = step_time * inverse_cos
    forcing = step_time * sea * (flux_all - mean)
    for repeat in range(ITERS):
        north_flux = v_now * north_cos
        divergence = u_now - pltpu.roll(u_now, 1, 1) + (north_flux - pltpu.roll(north_flux, 1, 0))
        height_now = height_now - scale * divergence + forcing
        u_now = open_u * u_now - pull_u * (eastward(height_now) - height_now)
        v_now = open_v * v_now - pull_v * (northward(height_now) - height_now)
    for slot, values in enumerate((height_now, u_now, v_now)):
        results[slot] = values[:ROWS, :COLS]
    results[3] = field * sea[:ROWS, :COLS]
    outs = (height_out, u_out, v_out, sal_out)
    for copy in fetch([(results.at[slot], out) for slot, out in enumerate(outs)], out_sems):
        copy.wait()


def column_kernel(
    height_in,
    flux_u_in,
    flux_v_in,
    depth_in,
    mask_in,
    flux_in,
    south_in,
    north_in,
    bands_in,
    west_out,
    east_out,
    blocks,
    bands,
    mask,
    strips,
    sides,
    sems,
    out_sems,
):
    own = pl.ds(0, ROWS)
    loads = fetch(
        (
            (south_in, strips.at[0]),
            (north_in, strips.at[1]),
            (height_in, blocks.at[0, own]),
            (flux_u_in, blocks.at[1, own]),
            (flux_v_in, blocks.at[2, own]),
            (depth_in, blocks.at[3, own]),
            (mask_in, mask),
            (flux_in, blocks.at[5, own]),
            (bands_in.at[lax.axis_index("lat")], bands),
        ),
        sems,
    )
    lane = iota((PAD_ROWS, 128), 1)
    west = jnp.zeros((PAD_ROWS, 128), f32)
    east = jnp.zeros((PAD_ROWS, 128), f32)
    for load in loads:
        load.wait()
    blocks[4, 0:ROWS, :] = mask[...].astype(f32)
    for slot in range(FIELDS):
        blocks[slot, ROWS : ROWS + WIDE, :] = strips[1, slot * WIDE : (slot + 1) * WIDE, :]
        blocks[slot, ROWS + WIDE : PAD_ROWS, :] = strips[0, slot * WIDE : (slot + 1) * WIDE, :]
        here = (lane >= slot * WIDE) & (lane < (slot + 1) * WIDE)
        west_part = blocks[slot, :, 0:128]
        east_part = pltpu.roll(blocks[slot, :, COLS - 128 : COLS], (WIDE + slot * WIDE) % 128, 1)
        if slot:
            west_part = pltpu.roll(west_part, slot * WIDE, 1)
        west = jnp.where(here, west_part, west)
        east = jnp.where(here, east_part, east)
    fill = jnp.zeros((128 - PAD_ROWS, 128), f32)
    sides[0] = jnp.concatenate([west, fill], axis=0).T[:STRIP, :]
    sides[1] = jnp.concatenate([east, fill], axis=0).T[:STRIP, :]
    pairs = ((sides.at[0], west_out), (sides.at[1], east_out))
    for copy in fetch(pairs, out_sems):
        copy.wait()


def far_call(kernel, name, operands, results, scratch, work=None, here=(), near=(), near_out=()):
    placed = []
    specs = []
    out_spaces = [pltpu.VMEM if slot in near_out else pltpu.HBM for slot in range(len(results))]
    for slot, operand in enumerate(operands):
        if slot in here:
            space = pltpu.VMEM
        elif slot in near:
            space = pltpu.VMEM
            operand = pltpu.with_memory_space_constraint(operand, pltpu.VMEM)
        else:
            space = pltpu.HBM
            operand = pltpu.with_memory_space_constraint(operand, pltpu.HBM)
        placed.append(operand)
        specs.append(pl.BlockSpec(memory_space=space))
    return pl.pallas_call(
        kernel,
        out_shape=tuple(space(*result) for space, result in zip(out_spaces, results)),
        in_specs=specs,
        out_specs=tuple(pl.BlockSpec(memory_space=space) for space in out_spaces),
        scratch_shapes=scratch,
        compiler_params=pltpu.CompilerParams(vmem_limit_bytes=32 << 20),
        cost_estimate=work,
        name=name,
    )(*placed)


def cost(flops, moved):
    return pl.CostEstimate(flops=flops, bytes_accessed=moved, transcendentals=0)


def on_device(sea_height, trans_u, trans_v, depth, sea_mask, freshwater_flux, love_factor):
    both_axes = ("lat", "lon")
    north = jnp.asarray(north_tables())
    fields = (sea_height, trans_u, trans_v, depth, sea_mask, freshwater_flux)
    vmem = pltpu.VMEM
    copies = pltpu.SemaphoreType.DMA
    tile = ((ROWS, COLS), f32)
    strip = ((STRIP, COLS), f32)
    side = ((STRIP, 128), f32)
    messages = ((DEVS, 8, 128), f32)
    tiles = vmem((FIELDS, ROWS, COLS), f32)
    mask_tile = vmem((ROWS, COLS), jnp.int32)

    message, strip_north, strip_south, wave = far_call(
        forward_kernel,
        "forward",
        fields + (jnp.asarray(turn_tables()), jnp.asarray(step_tables()), jnp.asarray(area_table())),
        (messages, strip, strip, ((QUARTERS, 4, QUARTER, COLS), bf16)),
        [
            tiles,
            mask_tile,
            vmem((2, DEVS, COLS), f32),
            vmem((2, ORDERS, COLS), f32),
            vmem((ROWS, 128), f32),
            vmem(*messages),
            vmem((2, STRIP, COLS), f32),
            copies((9,)),
            copies((QUARTERS,)),
            copies((2,)),
        ],
        work=cost(6 * 2 * 1024 * 256 * 256, 3 << 20),
        near_out=(3,),
    )
    received = lax.all_to_all(message, both_axes, split_axis=0, concat_axis=0, tiled=True)

    upward = [(i, i + 1) for i in range(LATS - 1)]
    downward = [(i + 1, i) for i in range(LATS - 1)]
    from_south = lax.ppermute(strip_north, "lat", upward)
    from_north = lax.ppermute(strip_south, "lat", downward)

    gain_tiles = ((2 * len(PAIRS), ORDERS, TILE), f32)
    squares = ((ORDERS, DEG), f32)
    first_rows = ((ORDERS, HALF), f32)
    gains, balance, start = far_call(
        setup_kernel,
        "setup",
        (
            love_factor.reshape(8, 128),
            jnp.asarray(balance_table()),
            jnp.asarray(seed_table()),
            north,
        ),
        (gain_tiles, squares, first_rows),
        [
            vmem((8, 128), f32),
            vmem((ORDERS, DEVS), f32),
            vmem((3, 8, HALF), f32),
            copies((4,)),
        ],
        work=cost(2 << 20, 1 << 20),
        near_out=(0, 1, 2),
    )
    received, from_south, from_north = lax.optimization_barrier((received, from_south, from_north))
    table = ((2 * len(PAIRS) * TILE, HALF), bf16)
    (reply,) = far_call(
        legendre_kernel,
        "legendre",
        (received, gains, balance, start, north),
        (messages,),
        [vmem(*table), vmem(*table), vmem(*messages), copies((LATS,))],
        work=cost(6 * 2 * 64 * 8192 * 256, 9 << 20),
        here=(0, 4),
        near=(1, 2, 3),
    )
    answer = lax.all_to_all(reply, both_axes, split_axis=0, concat_axis=0, tiled=True)

    padded = ((FIELDS, PAD_ROWS, COLS), f32)
    to_west, to_east, blocks, bands = far_call(
        column_kernel,
        "columns",
        fields + (from_south, from_north, jnp.asarray(row_tables())),
        (side, side, padded, ((2, PAD_ROWS, 128), f32)),
        [
            mask_tile,
            vmem((2, STRIP, COLS), f32),
            vmem((2, STRIP, 128), f32),
            copies((9,)),
            copies((2,)),
        ],
        near_out=(2, 3),
    )
    from_west = lax.ppermute(to_east, "lon", [(i, (i + 1) % LONS) for i in range(LONS)])
    from_east = lax.ppermute(to_west, "lon", [((i + 1) % LONS, i) for i in range(LONS)])

    return far_call(
        finish_kernel,
        "finish",
        (answer, from_west, from_east, wave, blocks, bands),
        (tile,) * 4,
        [
            vmem((FIELDS, PAD_ROWS, PAD_COLS), f32),
            vmem((4, ROWS, COLS), f32),
            copies((4,)),
        ],
        here=(0, 1, 2),
        near=(3, 4, 5),
    )


def solution(mesh):
    tiles = P("lat", "lon")
    return jax.shard_map(
        on_device,
        mesh=mesh,
        in_specs=(tiles,) * 6 + (P(),),
        out_specs=(tiles,) * 4,
        check_vma=False,
    )
```

```python
import math

import jax
import jax.numpy as jnp
import ml_dtypes
import numpy as np
from jax import lax
from jax.experimental import pallas as pl
from jax.experimental.pallas import tpu as pltpu
from jax.sharding import PartitionSpec as P

ITERS = 4
NLON = 4096
NLAT = 512
DEG = 1024
LATS = 8
LONS = 16
DEVS = LATS * LONS
ROWS = NLAT // LATS
COLS = NLON // LONS
HALF = NLAT // 2
ORDERS = DEG // DEVS
WIDE = 4
FIELDS = 6
PAD_ROWS = ROWS + 2 * WIDE
PAD_COLS = COLS + 128
STRIP = FIELDS * WIDE
CHUNK = 128
CHUNKS = DEG // CHUNK
TILE = 256
QUARTERS = 4
QUARTER = DEG // QUARTERS

step_time = 0.5
sal_ratio = 3.0 * 1035.0 / 5517.0
spacing = 2.0 * math.pi / NLON

f32 = jnp.float32
bf16 = jnp.bfloat16


def turn_tables():
    column = np.arange(NLON).reshape(LONS, 1, COLS)
    angle = column * np.arange(DEVS)[None, :, None] % NLON * (2.0 * math.pi / NLON)
    return np.stack([np.cos(angle), np.sin(angle)], axis=1).astype(np.float32)


def step_tables():
    angle = np.arange(ORDERS)[:, None] * DEVS * np.arange(COLS)[None, :] % NLON
    angle = angle * (2.0 * math.pi / NLON)
    return np.stack([np.cos(angle), np.sin(angle)]).astype(np.float32)


def balance_table():
    order = np.arange(DEG, dtype=np.float64)
    scale = np.ones(DEG)
    squares = []
    for step in range(DEG):
        squares.append(scale * scale)
        degree = order + step + 1.0
        factor = np.sqrt((4.0 * degree * degree - 1.0) / (degree * degree - order * order))
        scale = factor / scale
    return np.stack(squares, axis=1).reshape(ORDERS, DEVS, DEG).transpose(1, 0, 2).astype(np.float32)


def latitude_of(rows):
    return (rows + 0.5 - NLAT / 2) * spacing


def row_tables():
    local = np.concatenate([np.arange(ROWS + WIDE), np.arange(-WIDE, 0)])
    latitude = latitude_of(np.arange(LATS)[:, None] * ROWS + local[None, :])
    both = np.stack([1.0 / np.cos(latitude), np.cos(latitude + spacing / 2)], axis=1)
    return np.broadcast_to(both[..., None], both.shape + (128,)).astype(np.float32)


def area_table():
    latitude = latitude_of(np.arange(NLAT)).reshape(LATS, ROWS, 1)
    return np.broadcast_to(np.cos(latitude), (LATS, ROWS, 128)).astype(np.float32)


def north_tables():
    latitude = latitude_of(np.arange(HALF, NLAT))
    weight = np.cos(latitude) * spacing * spacing / (4.0 * math.pi)
    table = np.stack([np.sin(latitude), np.log(np.cos(latitude)), weight])
    return np.broadcast_to(table[:, None, :], (3, 8, HALF)).astype(np.float32)


def seed_table():
    order = np.arange(1, DEG)
    grown = 0.5 * math.log(2.0) + 0.5 * np.cumsum(np.log((2.0 * order + 1.0) / (2.0 * order)))
    return np.concatenate([[0.0], grown]).reshape(ORDERS, DEVS).astype(np.float32)


def position(lat, lon):
    return (lat % 2 * (LATS // 2) + lat // 2) * LONS + (lon + 4) % LONS


def exchange(messages):
    mesh_order = [(position(lat, lon), lat * LONS + lon) for lat in range(LATS) for lon in range(LONS)]
    group = [place for _, place in sorted(mesh_order)]
    return lax.all_to_all(
        messages,
        ("lat", "lon"),
        split_axis=0,
        concat_axis=0,
        tiled=True,
        axis_index_groups=[group],
    )


def iota(shape, dim):
    return lax.broadcasted_iota(jnp.int32, shape, dim)


def halves(values):
    high = values.astype(bf16)
    low = (values - high.astype(f32)).astype(bf16)
    return high, low


def dot_nt(left, right):
    return lax.dot_general(left, right, (((1,), (1,)), ((), ())), preferred_element_type=f32)


def dot_nn(left, right):
    return lax.dot_general(left, right, (((1,), (0,)), ((), ())), preferred_element_type=f32)


def fetch(pairs, sems):
    copies = [pltpu.make_async_copy(a, b, sems.at[slot]) for slot, (a, b) in enumerate(pairs)]
    for copy in copies:
        copy.start()
    return copies


def row_order(lat_index):
    row = iota((ROWS, ROWS), 0)
    col = iota((ROWS, ROWS), 1)
    south = lat_index < LATS // 2
    return jnp.where(south, (row + col == ROWS - 1).astype(f32), (row == col).astype(f32))


def forward_kernel(
    height_in,
    flux_u_in,
    flux_v_in,
    depth_in,
    mask_in,
    flux_in,
    turn_in,
    step_in,
    area_in,
    message_out,
    north_out,
    south_out,
    wave,
    tiles,
    mask,
    turn,
    step,
    area,
    message,
    strips,
    sems,
    send_sems,
    strip_sems,
):
    lat_index = lax.axis_index("lat")
    loads = fetch(
        (
            (mask_in, mask),
            (height_in, tiles.at[0]),
            (turn_in.at[lax.axis_index("lon")], turn),
            (step_in, step),
            (flux_in, tiles.at[4]),
            (area_in.at[lat_index], area),
            (flux_u_in, tiles.at[1]),
            (flux_v_in, tiles.at[2]),
            (depth_in, tiles.at[3]),
        ),
        sems,
    )
    for load in loads[:6]:
        load.wait()
    sea = mask[...].astype(f32)
    mass_high, mass_low = halves(sea * tiles[0])
    both = jnp.concatenate([mass_high, mass_low], axis=1)
    both = dot_nn(row_order(lat_index).astype(bf16), both).astype(bf16)
    mass_high, mass_low = both[:, :COLS], both[:, COLS:]
    zero = jnp.zeros_like(mass_high)
    for_cos = jnp.concatenate([mass_high, zero, mass_low, zero], axis=0)
    for_sin = jnp.concatenate([zero, mass_high, zero, mass_low], axis=0)

    band = area[...]
    area_cells = sea * jnp.concatenate([band, band], axis=1)
    flux_sum = jnp.sum(area_cells * tiles[4])
    area_sum = jnp.sum(area_cells)
    row = iota((8, 128), 0)
    lane = iota((8, 128), 1)

    step_cos, step_sin = step[0], step[1]
    share = DEVS // QUARTERS
    sends = []
    for quarter in range(QUARTERS):
        for pair in range(share // 2):
            cos_rows = []
            sin_rows = []
            for device in (quarter * share + 2 * pair, quarter * share + 2 * pair + 1):
                turn_cos, turn_sin = turn[0, device : device + 1, :], turn[1, device : device + 1, :]
                cos_rows.append(turn_cos * step_cos - turn_sin * step_sin)
                sin_rows.append(turn_sin * step_cos + turn_cos * step_sin)
            rows = slice(2 * ORDERS * pair, 2 * ORDERS * (pair + 1))
            for slot, parts in enumerate((cos_rows, sin_rows)):
                high, low = halves(jnp.concatenate(parts, axis=0))
                wave[quarter, slot, rows, :] = high
                wave[quarter, 2 + slot, rows, :] = low
        sums = dot_nt(wave[quarter, 0], for_cos) + dot_nt(wave[quarter, 1], for_sin)
        sums = sums[:, :128] + sums[:, 128:]
        sums = sums + dot_nt(wave[quarter, 2], for_cos[:128]) + dot_nt(wave[quarter, 3], for_sin[:128])
        for spot in range(share):
            sent = sums[spot * ORDERS : (spot + 1) * ORDERS]
            if quarter == 0 and spot == 0:
                sent = jnp.where((row == 0) & (lane >= 64), area_sum, sent)
                sent = jnp.where((row == 0) & (lane == 64), flux_sum, sent)
            message[quarter * share + spot] = sent
        place = pl.ds(quarter * share, share)
        pair = (message.at[place], message_out.at[place])
        sends += fetch((pair,), send_sems.at[pl.ds(quarter, 1)])
    for load in loads[6:]:
        load.wait()
    for slot, values in enumerate((tiles[0], tiles[1], tiles[2], tiles[3], sea, tiles[4])):
        strips[0, slot * WIDE : (slot + 1) * WIDE, :] = values[ROWS - WIDE :, :]
        strips[1, slot * WIDE : (slot + 1) * WIDE, :] = values[:WIDE, :]
    sends += fetch(((strips.at[0], north_out), (strips.at[1], south_out)), strip_sems)
    for copy in sends:
        copy.wait()


def pairs_of():
    found = []
    for first, last, kept in ((0, 512, 8), (512, 768, 4), (768, 1024, 2)):
        steps = 2 * TILE // kept
        found += [(start, steps, kept) for start in range(first, last, steps)]
    return found


PAIRS = pairs_of()


def make_gains(love, balance, device, gains):
    lane = iota((8, 128), 1)
    degree = (128 * iota((8, 128), 0) + lane).astype(f32)
    gain = sal_ratio * love[...] / (2.0 * degree + 1.0)
    turned = pltpu.roll(gain, (128 - device) % 128, 1)
    above = jnp.concatenate([turned[1:], jnp.zeros((1, 128), f32)], axis=0)
    shifted = jnp.where(lane + device < 128, turned, above)
    padded = jnp.concatenate([shifted, jnp.zeros((8, 128), f32)], axis=0)
    for pair, (first, steps, kept) in enumerate(PAIRS):
        chunks = range(first // CHUNK, -(-(first + steps) // CHUNK))
        width = CHUNK * len(chunks)
        blocks = [padded[c : c + 8] * balance[:, c * CHUNK : (c + 1) * CHUNK] for c in chunks]
        parts = jnp.concatenate(halves(jnp.concatenate(blocks, axis=1)), axis=0)
        same = iota((ORDERS, TILE), 1) % kept == iota((ORDERS, TILE), 0)
        for parity in range(2):
            step = first % CHUNK + 2 * (iota((width, TILE), 1) // kept) + parity
            spread = (step == iota((width, TILE), 0)).astype(f32).astype(bf16)
            wide = dot_nn(parts, spread)
            gains[2 * pair + parity] = jnp.where(same, wide[:ORDERS] + wide[ORDERS:], 0.0)


def setup_kernel(
    height_in,
    flux_u_in,
    flux_v_in,
    depth_in,
    mask_in,
    flux_in,
    bands_in,
    love_in,
    balance_in,
    seeds_in,
    north_in,
    gains,
    balance,
    start,
    own,
    bands,
    mask,
    love,
    seeds,
    north,
    sems,
):
    device = position(lax.axis_index("lat"), lax.axis_index("lon"))
    loads = fetch(
        (
            (seeds_in, seeds),
            (north_in, north),
            (balance_in.at[device], balance),
            (love_in, love),
            (height_in, own.at[0]),
            (flux_u_in, own.at[1]),
            (flux_v_in, own.at[2]),
            (depth_in, own.at[3]),
            (mask_in, mask),
            (flux_in, own.at[5]),
            (bands_in.at[lax.axis_index("lat")], bands),
        ),
        sems,
    )
    for load in loads:
        load.wait()
    own[4] = mask[...].astype(f32)
    lane = iota((8, 128), 1)
    seed_log = jnp.sum(jnp.where(lane == device, seeds[...], 0.0), axis=1, keepdims=True)
    order = (device + DEVS * iota((8, 128), 0)).astype(f32)[:, :1]
    start[...] = jnp.exp(seed_log + order * north[1])
    make_gains(love, balance, device, gains)


def legendre_kernel(
    received, gains, balance, start, north, message_out, high, low, message, out_sems
):
    device = position(lax.axis_index("lat"), lax.axis_index("lon"))
    lane = iota((8, 128), 1)
    row = iota((8, 128), 0)
    left = lane < 64

    bands = []
    for lat in range(LATS):
        band = received[position(lat, 0)]
        for lon in range(1, LONS):
            band = band + received[position(lat, lon)]
        bands.append(band)
    sums = bands[0]
    for band in bands[1:]:
        sums = sums + band
    even = [bands[4 + part] + bands[3 - part] for part in range(4)]
    odd = [bands[4 + part] - bands[3 - part] for part in range(4)]

    def arrange(parts):
        cos_parts = []
        sin_parts = []
        for first, second in ((parts[0], parts[1]), (parts[2], parts[3])):
            cos_parts.append(jnp.where(left, first, pltpu.roll(second, 64, 1)))
            sin_parts.append(jnp.where(left, pltpu.roll(first, 64, 1), second))
        weight = north[2]
        return [
            jnp.concatenate(cos_parts, axis=1) * weight,
            jnp.concatenate(sin_parts, axis=1) * weight,
        ]

    lefts = []
    for parts in (even, odd):
        rows_high, rows_low = halves(jnp.concatenate(arrange(parts), axis=0))
        lefts.append(jnp.concatenate([rows_high, rows_low], axis=0))

    sine = north[0]
    state = [jnp.zeros((ORDERS, HALF), f32), start[...]]
    wide_row = iota((ORDERS, HALF), 0)

    def extend(pair):
        first, steps, kept = PAIRS[pair]
        share = ORDERS // kept
        block, packed, place = [None, None], [[], []], [2 * pair * TILE, (2 * pair + 1) * TILE]
        for step in range(steps):
            parity, part = step % 2, step // 2 % share
            previous, current = state
            if part == 0:
                block[parity] = current
            else:
                moved = pltpu.roll(current, part * kept, 0)
                block[parity] = jnp.where(wide_row < part * kept, block[parity], moved)
            turn = balance[:, first + step : first + step + 1] * sine
            state[0], state[1] = current, turn * current - previous
            if part == share - 1:
                packed[parity].append(block[parity])
            if len(packed[parity]) == 2:
                rows = slice(place[parity], place[parity] + 16)
                high[rows, :], low[rows, :] = halves(jnp.concatenate(packed[parity], axis=0))
                packed[parity] = []
                place[parity] += 16

    def analyse(tile):
        place = slice(tile * TILE, (tile + 1) * TILE)
        left_rows = lefts[tile % 2]
        both = dot_nt(left_rows, high[place, :])
        found = both[:16] + both[16:] + dot_nt(left_rows[:16], low[place, :])
        gain = gains[tile]
        return jnp.concatenate(halves(found * jnp.concatenate([gain, gain], axis=0)), axis=0)

    def synthesise(tile, coefs):
        place = slice(tile * TILE, (tile + 1) * TILE)
        return dot_nn(coefs, high[place, :]), dot_nn(coefs[:16], low[place, :])

    count = len(PAIRS)
    total_high = [jnp.zeros((32, HALF), f32)] * 2
    total_low = [jnp.zeros((16, HALF), f32)] * 2
    coefs = {}
    for turn in range(count + 2):
        if turn < count:
            extend(turn)
        for parity in range(2):
            if 1 <= turn <= count:
                tile = 2 * (turn - 1) + parity
                coefs[tile] = analyse(tile)
        for parity in range(2):
            if turn >= 2:
                tile = 2 * (turn - 2) + parity
                more_high, more_low = synthesise(tile, coefs.pop(tile))
                total_high[parity] = total_high[parity] + more_high
                total_low[parity] = total_low[parity] + more_low
    total_even, total_odd = [
        total_high[parity][:16] + total_high[parity][16:] + total_low[parity] for parity in range(2)
    ]

    flux_sum = jnp.sum(jnp.where((row == 0) & (lane == 64), sums, 0.0))
    area_sum = jnp.sum(jnp.where((row == 0) & (lane == 65), sums, 0.0))
    mean = jnp.full((8, 128), flux_sum, f32) / jnp.full((8, 128), area_sum, f32)
    slot = (device == 0) & (row == 0) & (lane >= 64)
    cos_even, sin_even = total_even[0:8, :], total_even[8:16, :]
    cos_odd, sin_odd = total_odd[0:8, :], total_odd[8:16, :]
    copies = []
    for north_side in (True, False):
        if north_side:
            cos_all, sin_all = cos_even + cos_odd, sin_even + sin_odd
        else:
            cos_all, sin_all = cos_even - cos_odd, sin_even - sin_odd
        for part in range(4):
            block = slice(128 * (part // 2), 128 * (part // 2) + 128)
            cos_part, sin_part = cos_all[:, block], sin_all[:, block]
            if part % 2 == 0:
                sent = jnp.where(left, cos_part, pltpu.roll(sin_part, 64, 1))
            else:
                sent = jnp.where(left, pltpu.roll(cos_part, 64, 1), sin_part)
            sent = jnp.where(slot, mean, sent)
            lat = 4 + part if north_side else 3 - part
            for lon in range(LONS):
                message[position(lat, lon)] = sent
            part_place = pl.ds(position(lat, 0) // LONS * LONS, LONS)
            copies += fetch(((message.at[part_place], message_out.at[part_place]),), out_sems.at[pl.ds(lat, 1)])
    for copy in copies:
        copy.wait()


def finish_kernel(
    received,
    west_in,
    east_in,
    wave,
    own,
    edges,
    bands,
    height_out,
    u_out,
    v_out,
    sal_out,
    blocks,
    results,
    out_sems,
):
    lat_index = lax.axis_index("lat")
    lane = iota((8, 128), 1)
    mean = jnp.sum(jnp.where((iota((8, 128), 0) == 0) & (lane == 64), received[0], 0.0))
    turned = received[...].reshape(DEG, 128).T
    high, low = halves(turned)
    cos_both = jnp.concatenate([high[:64], low[:64]], axis=0)
    sin_both = jnp.concatenate([high[64:], low[64:]], axis=0)

    wide_lane = iota((PAD_ROWS, 128), 1)
    fill = jnp.zeros((128 - STRIP, 128), f32)
    west = jnp.concatenate([west_in[...], fill], axis=0).T[:PAD_ROWS, :]
    east = jnp.concatenate([east_in[...], fill], axis=0).T[:PAD_ROWS, :]
    for slot in range(FIELDS):
        high_side = pltpu.roll(east, 128 - slot * WIDE, 1) if slot else east
        low_side = pltpu.roll(west, 128 - WIDE - slot * WIDE, 1)
        blocks[slot, :ROWS, :COLS] = own[slot]
        blocks[slot, ROWS:, :COLS] = edges[slot]
        blocks[slot, :, COLS:] = jnp.where(
            wide_lane < WIDE, high_side, jnp.where(wide_lane >= 128 - WIDE, low_side, 0.0)
        )
    both = jnp.zeros((2 * ROWS, COLS), f32)
    field = jnp.zeros((ROWS, COLS), f32)
    for part in range(QUARTERS):
        place = slice(part * QUARTER, (part + 1) * QUARTER)
        both += dot_nn(cos_both[:, place], wave[part, 0]) + dot_nn(sin_both[:, place], wave[part, 1])
        field += dot_nn(high[:64, place], wave[part, 2]) + dot_nn(high[64:, place], wave[part, 3])
    field = field + both[:64] + both[64:]
    field_high, field_low = halves(field)
    order = row_order(lat_index).astype(bf16)
    field = dot_nn(order, field_high) + dot_nn(order, field_low)

    def eastward(values):
        return pltpu.roll(values, PAD_COLS - 1, 1)

    def northward(values):
        return pltpu.roll(values, PAD_ROWS - 1, 0)

    height_now, u_now, v_now, depth_all, sea, flux_all = [blocks[slot] for slot in range(FIELDS)]
    inverse_cos = jnp.concatenate([bands[0]] * 3, axis=1)
    north_cos = jnp.concatenate([bands[1]] * 3, axis=1)
    open_u = sea * eastward(sea)
    open_v = sea * northward(sea)
    pull_u = open_u * (0.5 * step_time) * (depth_all + eastward(depth_all)) * inverse_cos
    pull_v = open_v * (0.5 * step_time) * (depth_all + northward(depth_all))
    scale = step_time * inverse_cos
    forcing = step_time * sea * (flux_all - mean)
    for repeat in range(ITERS):
        north_flux = v_now * north_cos
        divergence = u_now - pltpu.roll(u_now, 1, 1) + (north_flux - pltpu.roll(north_flux, 1, 0))
        height_now = height_now - scale * divergence + forcing
        u_now = open_u * u_now - pull_u * (eastward(height_now) - height_now)
        v_now = open_v * v_now - pull_v * (northward(height_now) - height_now)
    for slot, values in enumerate((height_now, u_now, v_now)):
        results[slot] = values[:ROWS, :COLS]
    results[3] = field * sea[:ROWS, :COLS]
    outs = (height_out, u_out, v_out, sal_out)
    for copy in fetch([(results.at[slot], out) for slot, out in enumerate(outs)], out_sems):
        copy.wait()


def column_kernel(from_south, from_north, own, west_out, east_out, edges, sides, out_sems):
    lane = iota((PAD_ROWS, 128), 1)
    west = jnp.zeros((PAD_ROWS, 128), f32)
    east = jnp.zeros((PAD_ROWS, 128), f32)
    for slot in range(FIELDS):
        rows = slice(slot * WIDE, (slot + 1) * WIDE)
        edges[slot, 0:WIDE, :] = from_north[rows, :]
        edges[slot, WIDE : 2 * WIDE, :] = from_south[rows, :]
        here = (lane >= slot * WIDE) & (lane < (slot + 1) * WIDE)
        west_part = jnp.concatenate([own[slot, :, 0:128], edges[slot, :, 0:128]], axis=0)
        east_part = jnp.concatenate([own[slot, :, COLS - 128 :], edges[slot, :, COLS - 128 :]], axis=0)
        east_part = pltpu.roll(east_part, (WIDE + slot * WIDE) % 128, 1)
        if slot:
            west_part = pltpu.roll(west_part, slot * WIDE, 1)
        west = jnp.where(here, west_part, west)
        east = jnp.where(here, east_part, east)
    fill = jnp.zeros((128 - PAD_ROWS, 128), f32)
    sides[0] = jnp.concatenate([west, fill], axis=0).T[:STRIP, :]
    sides[1] = jnp.concatenate([east, fill], axis=0).T[:STRIP, :]
    for copy in fetch(((sides.at[0], west_out), (sides.at[1], east_out)), out_sems):
        copy.wait()


def far_call(kernel, name, operands, results, scratch, work=None, here=(), near=(), near_out=()):
    placed = []
    specs = []
    out_spaces = [pltpu.VMEM if slot in near_out else pltpu.HBM for slot in range(len(results))]
    for slot, operand in enumerate(operands):
        if slot in here:
            space = pltpu.VMEM
        elif slot in near:
            space = pltpu.VMEM
            operand = pltpu.with_memory_space_constraint(operand, pltpu.VMEM)
        else:
            space = pltpu.HBM
            operand = pltpu.with_memory_space_constraint(operand, pltpu.HBM)
        placed.append(operand)
        specs.append(pl.BlockSpec(memory_space=space))
    return pl.pallas_call(
        kernel,
        out_shape=tuple(space(*result) for space, result in zip(out_spaces, results)),
        in_specs=specs,
        out_specs=tuple(pl.BlockSpec(memory_space=space) for space in out_spaces),
        scratch_shapes=scratch,
        compiler_params=pltpu.CompilerParams(vmem_limit_bytes=32 << 20),
        cost_estimate=work,
        name=name,
    )(*placed)


def cost(flops, moved):
    return pl.CostEstimate(flops=flops, bytes_accessed=moved, transcendentals=0)


def on_device(sea_height, trans_u, trans_v, depth, sea_mask, freshwater_flux, love_factor):
    north = jnp.asarray(north_tables())
    fields = (sea_height, trans_u, trans_v, depth, sea_mask, freshwater_flux)
    vmem = pltpu.VMEM
    copies = pltpu.SemaphoreType.DMA
    tile = ((ROWS, COLS), f32)
    strip = ((STRIP, COLS), f32)
    side = ((STRIP, 128), f32)
    messages = ((DEVS, 8, 128), f32)
    tiles = vmem((FIELDS, ROWS, COLS), f32)
    mask_tile = vmem((ROWS, COLS), jnp.int32)

    message, strip_north, strip_south, wave = far_call(
        forward_kernel,
        "forward",
        fields + (jnp.asarray(turn_tables()), jnp.asarray(step_tables()), jnp.asarray(area_table())),
        (messages, strip, strip, ((QUARTERS, 4, QUARTER, COLS), bf16)),
        [
            tiles,
            mask_tile,
            vmem((2, DEVS, COLS), f32),
            vmem((2, ORDERS, COLS), f32),
            vmem((ROWS, 128), f32),
            vmem(*messages),
            vmem((2, STRIP, COLS), f32),
            copies((9,)),
            copies((QUARTERS,)),
            copies((2,)),
        ],
        work=cost(6 * 2 * 1024 * 256 * 256, 3 << 20),
        near_out=(3,),
    )
    received = exchange(message)

    upward = [(i, i + 1) for i in range(LATS - 1)]
    downward = [(i + 1, i) for i in range(LATS - 1)]
    from_south = lax.ppermute(strip_north, "lat", upward)
    from_north = lax.ppermute(strip_south, "lat", downward)

    gain_tiles = ((2 * len(PAIRS), ORDERS, TILE), f32)
    squares = ((ORDERS, DEG), f32)
    first_rows = ((ORDERS, HALF), f32)
    own_fields = ((FIELDS, ROWS, COLS), f32)
    gains, balance, start, own, bands = far_call(
        setup_kernel,
        "setup",
        fields
        + (
            jnp.asarray(row_tables()),
            love_factor.reshape(8, 128),
            jnp.asarray(balance_table()),
            jnp.asarray(seed_table()),
            north,
        ),
        (gain_tiles, squares, first_rows, own_fields, ((2, PAD_ROWS, 128), f32)),
        [
            mask_tile,
            vmem((8, 128), f32),
            vmem((ORDERS, DEVS), f32),
            vmem((3, 8, HALF), f32),
            copies((11,)),
        ],
        work=cost(2 << 20, 1 << 20),
        near_out=(0, 1, 2, 3, 4),
    )
    received, from_south, from_north = lax.optimization_barrier((received, from_south, from_north))
    table = ((2 * len(PAIRS) * TILE, HALF), bf16)
    (reply,) = far_call(
        legendre_kernel,
        "legendre",
        (received, gains, balance, start, north),
        (messages,),
        [vmem(*table), vmem(*table), vmem(*messages), copies((LATS,))],
        work=cost(6 * 2 * 64 * 8192 * 256, 9 << 20),
        here=(0, 4),
        near=(1, 2, 3),
    )
    answer = exchange(reply)

    to_west, to_east, edges = far_call(
        column_kernel,
        "columns",
        (from_south, from_north, own),
        (side, side, ((FIELDS, 2 * WIDE, COLS), f32)),
        [vmem((2, STRIP, 128), f32), copies((2,))],
        here=(0, 1),
        near=(2,),
        near_out=(2,),
    )
    from_west = lax.ppermute(to_east, "lon", [(i, (i + 1) % LONS) for i in range(LONS)])
    from_east = lax.ppermute(to_west, "lon", [((i + 1) % LONS, i) for i in range(LONS)])

    return far_call(
        finish_kernel,
        "finish",
        (answer, from_west, from_east, wave, own, edges, bands),
        (tile,) * 4,
        [
            vmem((FIELDS, PAD_ROWS, PAD_COLS), f32),
            vmem((4, ROWS, COLS), f32),
            copies((4,)),
        ],
        here=(0, 1, 2),
        near=(3, 4, 5, 6),
    )


def solution(mesh):
    tiles = P("lat", "lon")
    return jax.shard_map(
        on_device,
        mesh=mesh,
        in_specs=(tiles,) * 6 + (P(),),
        out_specs=(tiles,) * 4,
        check_vma=False,
    )
```

```python
import math

import jax
import jax.numpy as jnp
import ml_dtypes
import numpy as np
from jax import lax
from jax.experimental import pallas as pl
from jax.experimental.pallas import tpu as pltpu
from jax.sharding import PartitionSpec as P

ITERS = 4
NLON = 4096
NLAT = 512
DEG = 1024
LATS = 8
LONS = 16
DEVS = LATS * LONS
ROWS = NLAT // LATS
COLS = NLON // LONS
HALF = NLAT // 2
ORDERS = DEG // DEVS
WIDE = 4
FIELDS = 6
PAD_ROWS = ROWS + 2 * WIDE
PAD_COLS = COLS + 128
STRIP = FIELDS * WIDE
CHUNK = 128
CHUNKS = DEG // CHUNK
TILE = 256
QUARTERS = 4
QUARTER = DEG // QUARTERS

step_time = 0.5
sal_ratio = 3.0 * 1035.0 / 5517.0
spacing = 2.0 * math.pi / NLON

f32 = jnp.float32
bf16 = jnp.bfloat16


def turn_tables():
    column = np.arange(NLON).reshape(LONS, 1, COLS)
    angle = column * np.arange(DEVS)[None, :, None] % NLON * (2.0 * math.pi / NLON)
    return np.stack([np.cos(angle), np.sin(angle)], axis=1).astype(np.float32)


def step_tables():
    angle = np.arange(ORDERS)[:, None] * DEVS * np.arange(COLS)[None, :] % NLON
    angle = angle * (2.0 * math.pi / NLON)
    return np.stack([np.cos(angle), np.sin(angle)]).astype(np.float32)


def balance_table():
    order = np.arange(DEG, dtype=np.float64)
    scale = np.ones(DEG)
    squares = []
    for step in range(DEG):
        squares.append(scale * scale)
        degree = order + step + 1.0
        factor = np.sqrt((4.0 * degree * degree - 1.0) / (degree * degree - order * order))
        scale = factor / scale
    return np.stack(squares, axis=1).reshape(ORDERS, DEVS, DEG).transpose(1, 0, 2).astype(np.float32)


def latitude_of(rows):
    return (rows + 0.5 - NLAT / 2) * spacing


def row_tables():
    local = np.concatenate([np.arange(ROWS + WIDE), np.arange(-WIDE, 0)])
    latitude = latitude_of(np.arange(LATS)[:, None] * ROWS + local[None, :])
    both = np.stack([1.0 / np.cos(latitude), np.cos(latitude + spacing / 2)], axis=1)
    return np.broadcast_to(both[..., None], both.shape + (128,)).astype(np.float32)


def area_table():
    latitude = latitude_of(np.arange(NLAT)).reshape(LATS, ROWS, 1)
    return np.broadcast_to(np.cos(latitude), (LATS, ROWS, 128)).astype(np.float32)


def north_tables():
    latitude = latitude_of(np.arange(HALF, NLAT))
    weight = np.cos(latitude) * spacing * spacing / (4.0 * math.pi)
    table = np.stack([np.sin(latitude), np.log(np.cos(latitude)), weight])
    return np.broadcast_to(table[:, None, :], (3, 8, HALF)).astype(np.float32)


def seed_table():
    order = np.arange(1, DEG)
    grown = 0.5 * math.log(2.0) + 0.5 * np.cumsum(np.log((2.0 * order + 1.0) / (2.0 * order)))
    return np.concatenate([[0.0], grown]).reshape(ORDERS, DEVS).astype(np.float32)


def position(lat, lon):
    return (lat % 2 * (LATS // 2) + lat // 2) * LONS + (lon + 4) % LONS


def exchange(messages):
    mesh_order = [(position(lat, lon), lat * LONS + lon) for lat in range(LATS) for lon in range(LONS)]
    group = [place for _, place in sorted(mesh_order)]
    return lax.all_to_all(
        messages,
        ("lat", "lon"),
        split_axis=0,
        concat_axis=0,
        tiled=True,
        axis_index_groups=[group],
    )


def iota(shape, dim):
    return lax.broadcasted_iota(jnp.int32, shape, dim)


def halves(values):
    high = values.astype(bf16)
    low = (values - high.astype(f32)).astype(bf16)
    return high, low


def dot_nt(left, right):
    return lax.dot_general(left, right, (((1,), (1,)), ((), ())), preferred_element_type=f32)


def dot_nn(left, right):
    return lax.dot_general(left, right, (((1,), (0,)), ((), ())), preferred_element_type=f32)


def fetch(pairs, sems):
    copies = [pltpu.make_async_copy(a, b, sems.at[slot]) for slot, (a, b) in enumerate(pairs)]
    for copy in copies:
        copy.start()
    return copies


def row_order(lat_index):
    row = iota((ROWS, ROWS), 0)
    col = iota((ROWS, ROWS), 1)
    south = lat_index < LATS // 2
    return jnp.where(south, (row + col == ROWS - 1).astype(f32), (row == col).astype(f32))


def forward_kernel(
    height_in,
    flux_u_in,
    flux_v_in,
    depth_in,
    mask_in,
    flux_in,
    turn_in,
    step_in,
    area_in,
    message_out,
    near_out,
    far_out,
    wave,
    tiles,
    mask,
    turn,
    step,
    area,
    message,
    strips,
    sems,
    send_sems,
    strip_sems,
):
    lat_index = lax.axis_index("lat")
    loads = fetch(
        (
            (mask_in, mask),
            (height_in, tiles.at[0]),
            (turn_in.at[lax.axis_index("lon")], turn),
            (step_in, step),
            (flux_in, tiles.at[4]),
            (area_in.at[lat_index], area),
            (flux_u_in, tiles.at[1]),
            (flux_v_in, tiles.at[2]),
            (depth_in, tiles.at[3]),
        ),
        sems,
    )
    for load in loads[:6]:
        load.wait()
    sea = mask[...].astype(f32)
    mass_high, mass_low = halves(sea * tiles[0])
    both = jnp.concatenate([mass_high, mass_low], axis=1)
    both = dot_nn(row_order(lat_index).astype(bf16), both).astype(bf16)
    mass_high, mass_low = both[:, :COLS], both[:, COLS:]
    zero = jnp.zeros_like(mass_high)
    for_cos = jnp.concatenate([mass_high, zero, mass_low, zero], axis=0)
    for_sin = jnp.concatenate([zero, mass_high, zero, mass_low], axis=0)

    band = area[...]
    area_cells = sea * jnp.concatenate([band, band], axis=1)
    flux_sum = jnp.sum(area_cells * tiles[4])
    area_sum = jnp.sum(area_cells)
    row = iota((8, 128), 0)
    lane = iota((8, 128), 1)

    step_cos, step_sin = step[0], step[1]
    share = DEVS // QUARTERS
    sends = []
    for quarter in range(QUARTERS):
        for pair in range(share // 2):
            cos_rows = []
            sin_rows = []
            for device in (quarter * share + 2 * pair, quarter * share + 2 * pair + 1):
                turn_cos, turn_sin = turn[0, device : device + 1, :], turn[1, device : device + 1, :]
                cos_rows.append(turn_cos * step_cos - turn_sin * step_sin)
                sin_rows.append(turn_sin * step_cos + turn_cos * step_sin)
            rows = slice(2 * ORDERS * pair, 2 * ORDERS * (pair + 1))
            for slot, parts in enumerate((cos_rows, sin_rows)):
                high, low = halves(jnp.concatenate(parts, axis=0))
                wave[quarter, slot, rows, :] = high
                wave[quarter, 2 + slot, rows, :] = low
        sums = dot_nt(wave[quarter, 0], for_cos) + dot_nt(wave[quarter, 1], for_sin)
        sums = sums[:, :128] + sums[:, 128:]
        sums = sums + dot_nt(wave[quarter, 2], for_cos[:128]) + dot_nt(wave[quarter, 3], for_sin[:128])
        for spot in range(share):
            sent = sums[spot * ORDERS : (spot + 1) * ORDERS]
            if quarter == 0 and spot == 0:
                sent = jnp.where((row == 0) & (lane >= 64), area_sum, sent)
                sent = jnp.where((row == 0) & (lane == 64), flux_sum, sent)
            message[quarter * share + spot] = sent
        place = pl.ds(quarter * share, share)
        pair = (message.at[place], message_out.at[place])
        sends += fetch((pair,), send_sems.at[pl.ds(quarter, 1)])
    for load in loads[6:]:
        load.wait()
    for slot, values in enumerate((tiles[0], tiles[1], tiles[2], tiles[3], sea, tiles[4])):
        strips[0, slot * WIDE : (slot + 1) * WIDE, :] = values[ROWS - WIDE :, :]
        strips[1, slot * WIDE : (slot + 1) * WIDE, :] = values[:WIDE, :]
    odd = lat_index % 2
    sends += fetch(((strips.at[odd], near_out), (strips.at[1 - odd], far_out)), strip_sems)
    for copy in sends:
        copy.wait()


def pairs_of():
    found = []
    for first, last, kept in ((0, 512, 8), (512, 768, 4), (768, 1024, 2)):
        steps = 2 * TILE // kept
        found += [(start, steps, kept) for start in range(first, last, steps)]
    return found


PAIRS = pairs_of()


def make_gains(love, balance, device, gains):
    lane = iota((8, 128), 1)
    degree = (128 * iota((8, 128), 0) + lane).astype(f32)
    gain = sal_ratio * love[...] / (2.0 * degree + 1.0)
    turned = pltpu.roll(gain, (128 - device) % 128, 1)
    above = jnp.concatenate([turned[1:], jnp.zeros((1, 128), f32)], axis=0)
    shifted = jnp.where(lane + device < 128, turned, above)
    padded = jnp.concatenate([shifted, jnp.zeros((8, 128), f32)], axis=0)
    for pair, (first, steps, kept) in enumerate(PAIRS):
        chunks = range(first // CHUNK, -(-(first + steps) // CHUNK))
        width = CHUNK * len(chunks)
        blocks = [padded[c : c + 8] * balance[:, c * CHUNK : (c + 1) * CHUNK] for c in chunks]
        parts = jnp.concatenate(halves(jnp.concatenate(blocks, axis=1)), axis=0)
        same = iota((ORDERS, TILE), 1) % kept == iota((ORDERS, TILE), 0)
        for parity in range(2):
            step = first % CHUNK + 2 * (iota((width, TILE), 1) // kept) + parity
            spread = (step == iota((width, TILE), 0)).astype(f32).astype(bf16)
            wide = dot_nn(parts, spread)
            gains[2 * pair + parity] = jnp.where(same, wide[:ORDERS] + wide[ORDERS:], 0.0)


def setup_kernel(
    height_in,
    flux_u_in,
    flux_v_in,
    depth_in,
    mask_in,
    flux_in,
    bands_in,
    love_in,
    balance_in,
    seeds_in,
    north_in,
    gains,
    balance,
    start,
    own,
    bands,
    mask,
    love,
    seeds,
    north,
    sems,
):
    device = position(lax.axis_index("lat"), lax.axis_index("lon"))
    loads = fetch(
        (
            (seeds_in, seeds),
            (north_in, north),
            (balance_in.at[device], balance),
            (love_in, love),
            (height_in, own.at[0]),
            (flux_u_in, own.at[1]),
            (flux_v_in, own.at[2]),
            (depth_in, own.at[3]),
            (mask_in, mask),
            (flux_in, own.at[5]),
            (bands_in.at[lax.axis_index("lat")], bands),
        ),
        sems,
    )
    for load in loads:
        load.wait()
    own[4] = mask[...].astype(f32)
    lane = iota((8, 128), 1)
    seed_log = jnp.sum(jnp.where(lane == device, seeds[...], 0.0), axis=1, keepdims=True)
    order = (device + DEVS * iota((8, 128), 0)).astype(f32)[:, :1]
    start[...] = jnp.exp(seed_log + order * north[1])
    make_gains(love, balance, device, gains)


def legendre_kernel(
    received, gains, balance, start, north, message_out, high, low, message, out_sems
):
    device = position(lax.axis_index("lat"), lax.axis_index("lon"))
    lane = iota((8, 128), 1)
    row = iota((8, 128), 0)
    left = lane < 64

    bands = []
    for lat in range(LATS):
        band = received[position(lat, 0)]
        for lon in range(1, LONS):
            band = band + received[position(lat, lon)]
        bands.append(band)
    sums = bands[0]
    for band in bands[1:]:
        sums = sums + band
    even = [bands[4 + part] + bands[3 - part] for part in range(4)]
    odd = [bands[4 + part] - bands[3 - part] for part in range(4)]

    def arrange(parts):
        cos_parts = []
        sin_parts = []
        for first, second in ((parts[0], parts[1]), (parts[2], parts[3])):
            cos_parts.append(jnp.where(left, first, pltpu.roll(second, 64, 1)))
            sin_parts.append(jnp.where(left, pltpu.roll(first, 64, 1), second))
        weight = north[2]
        return [
            jnp.concatenate(cos_parts, axis=1) * weight,
            jnp.concatenate(sin_parts, axis=1) * weight,
        ]

    lefts = []
    for parts in (even, odd):
        rows_high, rows_low = halves(jnp.concatenate(arrange(parts), axis=0))
        lefts.append(jnp.concatenate([rows_high, rows_low], axis=0))

    sine = north[0]
    state = [jnp.zeros((ORDERS, HALF), f32), start[...]]
    wide_row = iota((ORDERS, HALF), 0)

    def extend(pair):
        first, steps, kept = PAIRS[pair]
        share = ORDERS // kept
        block, packed, place = [None, None], [[], []], [2 * pair * TILE, (2 * pair + 1) * TILE]
        for step in range(steps):
            parity, part = step % 2, step // 2 % share
            previous, current = state
            if part == 0:
                block[parity] = current
            else:
                moved = pltpu.roll(current, part * kept, 0)
                block[parity] = jnp.where(wide_row < part * kept, block[parity], moved)
            turn = balance[:, first + step : first + step + 1] * sine
            state[0], state[1] = current, turn * current - previous
            if part == share - 1:
                packed[parity].append(block[parity])
            if len(packed[parity]) == 2:
                rows = slice(place[parity], place[parity] + 16)
                high[rows, :], low[rows, :] = halves(jnp.concatenate(packed[parity], axis=0))
                packed[parity] = []
                place[parity] += 16

    def analyse(tile):
        place = slice(tile * TILE, (tile + 1) * TILE)
        left_rows = lefts[tile % 2]
        both = dot_nt(left_rows, high[place, :])
        found = both[:16] + both[16:] + dot_nt(left_rows[:16], low[place, :])
        gain = gains[tile]
        return jnp.concatenate(halves(found * jnp.concatenate([gain, gain], axis=0)), axis=0)

    def synthesise(tile, coefs):
        place = slice(tile * TILE, (tile + 1) * TILE)
        return dot_nn(coefs, high[place, :]), dot_nn(coefs[:16], low[place, :])

    count = len(PAIRS)
    total_high = [jnp.zeros((32, HALF), f32)] * 2
    total_low = [jnp.zeros((16, HALF), f32)] * 2
    coefs = {}
    for turn in range(count + 2):
        if turn < count:
            extend(turn)
        for parity in range(2):
            if 1 <= turn <= count:
                tile = 2 * (turn - 1) + parity
                coefs[tile] = analyse(tile)
        for parity in range(2):
            if turn >= 2:
                tile = 2 * (turn - 2) + parity
                more_high, more_low = synthesise(tile, coefs.pop(tile))
                total_high[parity] = total_high[parity] + more_high
                total_low[parity] = total_low[parity] + more_low
    total_even, total_odd = [
        total_high[parity][:16] + total_high[parity][16:] + total_low[parity] for parity in range(2)
    ]

    flux_sum = jnp.sum(jnp.where((row == 0) & (lane == 64), sums, 0.0))
    area_sum = jnp.sum(jnp.where((row == 0) & (lane == 65), sums, 0.0))
    mean = jnp.full((8, 128), flux_sum, f32) / jnp.full((8, 128), area_sum, f32)
    slot = (device == 0) & (row == 0) & (lane >= 64)
    cos_even, sin_even = total_even[0:8, :], total_even[8:16, :]
    cos_odd, sin_odd = total_odd[0:8, :], total_odd[8:16, :]
    copies = []
    for north_side in (True, False):
        if north_side:
            cos_all, sin_all = cos_even + cos_odd, sin_even + sin_odd
        else:
            cos_all, sin_all = cos_even - cos_odd, sin_even - sin_odd
        for part in range(4):
            block = slice(128 * (part // 2), 128 * (part // 2) + 128)
            cos_part, sin_part = cos_all[:, block], sin_all[:, block]
            if part % 2 == 0:
                sent = jnp.where(left, cos_part, pltpu.roll(sin_part, 64, 1))
            else:
                sent = jnp.where(left, pltpu.roll(cos_part, 64, 1), sin_part)
            sent = jnp.where(slot, mean, sent)
            lat = 4 + part if north_side else 3 - part
            for lon in range(LONS):
                message[position(lat, lon)] = sent
            part_place = pl.ds(position(lat, 0) // LONS * LONS, LONS)
            copies += fetch(((message.at[part_place], message_out.at[part_place]),), out_sems.at[pl.ds(lat, 1)])
    for copy in copies:
        copy.wait()


def finish_kernel(
    received,
    from_near,
    from_far,
    wave,
    own,
    edges,
    bands,
    height_out,
    u_out,
    v_out,
    sal_out,
    blocks,
    results,
    out_sems,
):
    lat_index = lax.axis_index("lat")
    lane = iota((8, 128), 1)
    first_row = iota((8, 128), 0) == 0
    mean = jnp.sum(jnp.where(first_row & (lane == 64), received[0], 0.0))
    first = jnp.where(first_row & (lane >= 64), 0.0, received[0])
    others = received[1:].reshape(DEG - ORDERS, 128)
    turned = jnp.concatenate([first, others], axis=0).T
    high, low = halves(turned)
    cos_both = jnp.concatenate([high[:64], low[:64]], axis=0)
    sin_both = jnp.concatenate([high[64:], low[64:]], axis=0)

    wide_lane = iota((PAD_ROWS, 128), 1)
    fill = jnp.zeros((128 - STRIP, 128), f32)
    odd_lon = lax.axis_index("lon") % 2 == 1
    west_in = jnp.where(odd_lon, from_near[...], from_far[...])
    east_in = jnp.where(odd_lon, from_far[...], from_near[...])
    west = jnp.concatenate([west_in, fill], axis=0).T[:PAD_ROWS, :]
    east = jnp.concatenate([east_in, fill], axis=0).T[:PAD_ROWS, :]
    for slot in range(FIELDS):
        high_side = pltpu.roll(east, 128 - slot * WIDE, 1) if slot else east
        low_side = pltpu.roll(west, 128 - WIDE - slot * WIDE, 1)
        blocks[slot, :ROWS, :COLS] = own[slot]
        blocks[slot, ROWS:, :COLS] = edges[slot]
        blocks[slot, :, COLS:] = jnp.where(
            wide_lane < WIDE, high_side, jnp.where(wide_lane >= 128 - WIDE, low_side, 0.0)
        )
    both = jnp.zeros((2 * ROWS, COLS), f32)
    field = jnp.zeros((ROWS, COLS), f32)
    for part in range(QUARTERS):
        place = slice(part * QUARTER, (part + 1) * QUARTER)
        both += dot_nn(cos_both[:, place], wave[part, 0]) + dot_nn(sin_both[:, place], wave[part, 1])
        field += dot_nn(high[:64, place], wave[part, 2]) + dot_nn(high[64:, place], wave[part, 3])
    field = field + both[:64] + both[64:]
    field_high, field_low = halves(field)
    order = row_order(lat_index).astype(bf16)
    field = dot_nn(order, field_high) + dot_nn(order, field_low)

    def eastward(values):
        return pltpu.roll(values, PAD_COLS - 1, 1)

    def northward(values):
        return pltpu.roll(values, PAD_ROWS - 1, 0)

    height_now, u_now, v_now, depth_all, sea, flux_all = [blocks[slot] for slot in range(FIELDS)]
    inverse_cos = jnp.concatenate([bands[0]] * 3, axis=1)
    north_cos = jnp.concatenate([bands[1]] * 3, axis=1)
    open_u = sea * eastward(sea)
    open_v = sea * northward(sea)
    pull_u = open_u * (0.5 * step_time) * (depth_all + eastward(depth_all)) * inverse_cos
    pull_v = open_v * (0.5 * step_time) * (depth_all + northward(depth_all))
    scale = step_time * inverse_cos
    forcing = step_time * sea * (flux_all - mean)
    for repeat in range(ITERS):
        north_flux = v_now * north_cos
        divergence = u_now - pltpu.roll(u_now, 1, 1) + (north_flux - pltpu.roll(north_flux, 1, 0))
        height_now = height_now - scale * divergence + forcing
        u_now = open_u * u_now - pull_u * (eastward(height_now) - height_now)
        v_now = open_v * v_now - pull_v * (northward(height_now) - height_now)
    for slot, values in enumerate((height_now, u_now, v_now)):
        results[slot] = values[:ROWS, :COLS]
    results[3] = field * sea[:ROWS, :COLS]
    outs = (height_out, u_out, v_out, sal_out)
    for copy in fetch([(results.at[slot], out) for slot, out in enumerate(outs)], out_sems):
        copy.wait()


def column_kernel(from_near, from_far, own, near_out, far_out, edges, sides, out_sems):
    odd_lat = lax.axis_index("lat") % 2 == 1
    odd = lax.axis_index("lon") % 2
    lane = iota((PAD_ROWS, 128), 1)
    west = jnp.zeros((PAD_ROWS, 128), f32)
    east = jnp.zeros((PAD_ROWS, 128), f32)
    for slot in range(FIELDS):
        rows = slice(slot * WIDE, (slot + 1) * WIDE)
        one, other = from_near[rows, :], from_far[rows, :]
        edges[slot, 0:WIDE, :] = jnp.where(odd_lat, other, one)
        edges[slot, WIDE : 2 * WIDE, :] = jnp.where(odd_lat, one, other)
        here = (lane >= slot * WIDE) & (lane < (slot + 1) * WIDE)
        west_part = jnp.concatenate([own[slot, :, 0:128], edges[slot, :, 0:128]], axis=0)
        east_part = jnp.concatenate([own[slot, :, COLS - 128 :], edges[slot, :, COLS - 128 :]], axis=0)
        east_part = pltpu.roll(east_part, (WIDE + slot * WIDE) % 128, 1)
        if slot:
            west_part = pltpu.roll(west_part, slot * WIDE, 1)
        west = jnp.where(here, west_part, west)
        east = jnp.where(here, east_part, east)
    fill = jnp.zeros((128 - PAD_ROWS, 128), f32)
    sides[1] = jnp.concatenate([west, fill], axis=0).T[:STRIP, :]
    sides[0] = jnp.concatenate([east, fill], axis=0).T[:STRIP, :]
    for copy in fetch(((sides.at[odd], near_out), (sides.at[1 - odd], far_out)), out_sems):
        copy.wait()


def far_call(kernel, name, operands, results, scratch, work=None, here=(), near=(), near_out=()):
    placed = []
    specs = []
    out_spaces = [pltpu.VMEM if slot in near_out else pltpu.HBM for slot in range(len(results))]
    for slot, operand in enumerate(operands):
        if slot in here:
            space = pltpu.VMEM
        elif slot in near:
            space = pltpu.VMEM
            operand = pltpu.with_memory_space_constraint(operand, pltpu.VMEM)
        else:
            space = pltpu.HBM
            operand = pltpu.with_memory_space_constraint(operand, pltpu.HBM)
        placed.append(operand)
        specs.append(pl.BlockSpec(memory_space=space))
    return pl.pallas_call(
        kernel,
        out_shape=tuple(space(*result) for space, result in zip(out_spaces, results)),
        in_specs=specs,
        out_specs=tuple(pl.BlockSpec(memory_space=space) for space in out_spaces),
        scratch_shapes=scratch,
        compiler_params=pltpu.CompilerParams(vmem_limit_bytes=32 << 20),
        cost_estimate=work,
        name=name,
    )(*placed)


def cost(flops, moved):
    return pl.CostEstimate(flops=flops, bytes_accessed=moved, transcendentals=0)


def on_device(sea_height, trans_u, trans_v, depth, sea_mask, freshwater_flux, love_factor):
    north = jnp.asarray(north_tables())
    fields = (sea_height, trans_u, trans_v, depth, sea_mask, freshwater_flux)
    vmem = pltpu.VMEM
    copies = pltpu.SemaphoreType.DMA
    tile = ((ROWS, COLS), f32)
    strip = ((STRIP, COLS), f32)
    side = ((STRIP, 128), f32)
    messages = ((DEVS, 8, 128), f32)
    tiles = vmem((FIELDS, ROWS, COLS), f32)
    mask_tile = vmem((ROWS, COLS), jnp.int32)

    message, strip_near, strip_far, wave = far_call(
        forward_kernel,
        "forward",
        fields + (jnp.asarray(turn_tables()), jnp.asarray(step_tables()), jnp.asarray(area_table())),
        (messages, strip, strip, ((QUARTERS, 4, QUARTER, COLS), bf16)),
        [
            tiles,
            mask_tile,
            vmem((2, DEVS, COLS), f32),
            vmem((2, ORDERS, COLS), f32),
            vmem((ROWS, 128), f32),
            vmem(*messages),
            vmem((2, STRIP, COLS), f32),
            copies((9,)),
            copies((QUARTERS,)),
            copies((2,)),
        ],
        work=cost(6 * 2 * 1024 * 256 * 256, 3 << 20),
        near_out=(3,),
    )
    received = exchange(message)

    near_pairs = [(i, i ^ 1) for i in range(LATS)]
    far_pairs = [(i, ((i + 1) ^ 1) - 1) for i in range(1, LATS - 1)]
    from_near = lax.ppermute(strip_near, "lat", near_pairs)
    from_far = lax.ppermute(strip_far, "lat", far_pairs)

    gain_tiles = ((2 * len(PAIRS), ORDERS, TILE), f32)
    squares = ((ORDERS, DEG), f32)
    first_rows = ((ORDERS, HALF), f32)
    own_fields = ((FIELDS, ROWS, COLS), f32)
    gains, balance, start, own, bands = far_call(
        setup_kernel,
        "setup",
        fields
        + (
            jnp.asarray(row_tables()),
            love_factor.reshape(8, 128),
            jnp.asarray(balance_table()),
            jnp.asarray(seed_table()),
            north,
        ),
        (gain_tiles, squares, first_rows, own_fields, ((2, PAD_ROWS, 128), f32)),
        [
            mask_tile,
            vmem((8, 128), f32),
            vmem((ORDERS, DEVS), f32),
            vmem((3, 8, HALF), f32),
            copies((11,)),
        ],
        work=cost(2 << 20, 1 << 20),
        near_out=(0, 1, 2, 3, 4),
    )
    received, from_near, from_far = lax.optimization_barrier((received, from_near, from_far))
    table = ((2 * len(PAIRS) * TILE, HALF), bf16)
    (reply,) = far_call(
        legendre_kernel,
        "legendre",
        (received, gains, balance, start, north),
        (messages,),
        [vmem(*table), vmem(*table), vmem(*messages), copies((LATS,))],
        work=cost(6 * 2 * 64 * 8192 * 256, 9 << 20),
        here=(0, 4),
        near=(1, 2, 3),
    )
    answer = exchange(reply)

    to_near, to_far, edges = far_call(
        column_kernel,
        "columns",
        (from_near, from_far, own),
        (side, side, ((FIELDS, 2 * WIDE, COLS), f32)),
        [vmem((2, STRIP, 128), f32), copies((2,))],
        here=(0, 1),
        near=(2,),
        near_out=(2,),
    )
    near_lons = [(i, i ^ 1) for i in range(LONS)]
    far_lons = [(i, (((i + 1) ^ 1) - 1) % LONS) for i in range(LONS)]
    side_near = lax.ppermute(to_near, "lon", near_lons)
    side_far = lax.ppermute(to_far, "lon", far_lons)

    return far_call(
        finish_kernel,
        "finish",
        (answer, side_near, side_far, wave, own, edges, bands),
        (tile,) * 4,
        [
            vmem((FIELDS, PAD_ROWS, PAD_COLS), f32),
            vmem((4, ROWS, COLS), f32),
            copies((4,)),
        ],
        here=(0, 1, 2),
        near=(3, 4, 5, 6),
    )


def solution(mesh):
    tiles = P("lat", "lon")
    return jax.shard_map(
        on_device,
        mesh=mesh,
        in_specs=(tiles,) * 6 + (P(),),
        out_specs=(tiles,) * 4,
        check_vma=False,
    )
```

```python
import math

import jax
import jax.numpy as jnp
import ml_dtypes
import numpy as np
from jax import lax
from jax.experimental import pallas as pl
from jax.experimental.pallas import tpu as pltpu
from jax.sharding import PartitionSpec as P

ITERS = 4
NLON = 4096
NLAT = 512
DEG = 1024
LATS = 8
LONS = 16
DEVS = LATS * LONS
ROWS = NLAT // LATS
COLS = NLON // LONS
HALF = NLAT // 2
ORDERS = DEG // DEVS
WIDE = 4
FIELDS = 6
PAD_ROWS = ROWS + 2 * WIDE
PAD_COLS = COLS + 128
STRIP = FIELDS * WIDE
CHUNK = 128
CHUNKS = DEG // CHUNK
TILE = 256
QUARTERS = 4
QUARTER = DEG // QUARTERS

step_time = 0.5
sal_ratio = 3.0 * 1035.0 / 5517.0
spacing = 2.0 * math.pi / NLON

f32 = jnp.float32
bf16 = jnp.bfloat16


def turn_tables():
    column = np.arange(NLON).reshape(LONS, 1, COLS)
    angle = column * np.arange(DEVS)[None, :, None] % NLON * (2.0 * math.pi / NLON)
    return np.stack([np.cos(angle), np.sin(angle)], axis=1).astype(np.float32)


def step_tables():
    angle = np.arange(ORDERS)[:, None] * DEVS * np.arange(COLS)[None, :] % NLON
    angle = angle * (2.0 * math.pi / NLON)
    return np.stack([np.cos(angle), np.sin(angle)]).astype(np.float32)


def balance_table():
    order = np.arange(DEG, dtype=np.float64)
    scale = np.ones(DEG)
    squares = []
    for step in range(DEG):
        squares.append(scale * scale)
        degree = order + step + 1.0
        factor = np.sqrt((4.0 * degree * degree - 1.0) / (degree * degree - order * order))
        scale = factor / scale
    return np.stack(squares, axis=1).reshape(ORDERS, DEVS, DEG).transpose(1, 0, 2).astype(np.float32)


def latitude_of(rows):
    return (rows + 0.5 - NLAT / 2) * spacing


def row_tables():
    local = np.concatenate([np.arange(ROWS + WIDE), np.arange(-WIDE, 0)])
    latitude = latitude_of(np.arange(LATS)[:, None] * ROWS + local[None, :])
    both = np.stack([1.0 / np.cos(latitude), np.cos(latitude + spacing / 2)], axis=1)
    return np.broadcast_to(both[..., None], both.shape + (128,)).astype(np.float32)


def area_table():
    latitude = latitude_of(np.arange(NLAT)).reshape(LATS, ROWS, 1)
    return np.broadcast_to(np.cos(latitude), (LATS, ROWS, 128)).astype(np.float32)


def north_tables():
    latitude = latitude_of(np.arange(HALF, NLAT))
    weight = np.cos(latitude) * spacing * spacing / (4.0 * math.pi)
    table = np.stack([np.sin(latitude), np.log(np.cos(latitude)), weight])
    return np.broadcast_to(table[:, None, :], (3, 8, HALF)).astype(np.float32)


def seed_table():
    order = np.arange(1, DEG)
    grown = 0.5 * math.log(2.0) + 0.5 * np.cumsum(np.log((2.0 * order + 1.0) / (2.0 * order)))
    return np.concatenate([[0.0], grown]).reshape(ORDERS, DEVS).astype(np.float32)


def position(lat, lon):
    return (lat % 2 * (LATS // 2) + lat // 2) * LONS + (lon + 4) % LONS


def exchange(messages):
    mesh_order = [(position(lat, lon), lat * LONS + lon) for lat in range(LATS) for lon in range(LONS)]
    group = [place for _, place in sorted(mesh_order)]
    return lax.all_to_all(
        messages,
        ("lat", "lon"),
        split_axis=0,
        concat_axis=0,
        tiled=True,
        axis_index_groups=[group],
    )


def iota(shape, dim):
    return lax.broadcasted_iota(jnp.int32, shape, dim)


def halves(values):
    high = values.astype(bf16)
    low = (values - high.astype(f32)).astype(bf16)
    return high, low


def dot_nt(left, right):
    return lax.dot_general(left, right, (((1,), (1,)), ((), ())), preferred_element_type=f32)


def dot_nn(left, right):
    return lax.dot_general(left, right, (((1,), (0,)), ((), ())), preferred_element_type=f32)


def fetch(pairs, sems):
    copies = [pltpu.make_async_copy(a, b, sems.at[slot]) for slot, (a, b) in enumerate(pairs)]
    for copy in copies:
        copy.start()
    return copies


def row_order(lat_index):
    row = iota((ROWS, ROWS), 0)
    col = iota((ROWS, ROWS), 1)
    south = lat_index < LATS // 2
    return jnp.where(south, (row + col == ROWS - 1).astype(f32), (row == col).astype(f32))


def forward_kernel(
    height_in,
    flux_u_in,
    flux_v_in,
    depth_in,
    mask_in,
    flux_in,
    turn_in,
    step_in,
    area_in,
    message_out,
    near_out,
    far_out,
    wave,
    tiles,
    mask,
    turn,
    step,
    area,
    message,
    strips,
    sems,
    send_sems,
    strip_sems,
):
    lat_index = lax.axis_index("lat")
    loads = fetch(
        (
            (mask_in, mask),
            (height_in, tiles.at[0]),
            (turn_in.at[lax.axis_index("lon")], turn),
            (step_in, step),
            (flux_in, tiles.at[4]),
            (area_in.at[lat_index], area),
            (flux_u_in, tiles.at[1]),
            (flux_v_in, tiles.at[2]),
            (depth_in, tiles.at[3]),
        ),
        sems,
    )
    for load in loads[:6]:
        load.wait()
    sea = mask[...].astype(f32)
    mass_high, mass_low = halves(sea * tiles[0])
    both = jnp.concatenate([mass_high, mass_low], axis=1)
    both = dot_nn(row_order(lat_index).astype(bf16), both).astype(bf16)
    mass_high, mass_low = both[:, :COLS], both[:, COLS:]
    zero = jnp.zeros_like(mass_high)
    for_cos = jnp.concatenate([mass_high, zero, mass_low, zero], axis=0)
    for_sin = jnp.concatenate([zero, mass_high, zero, mass_low], axis=0)

    band = area[...]
    area_cells = sea * jnp.concatenate([band, band], axis=1)
    flux_sum = jnp.sum(area_cells * tiles[4])
    area_sum = jnp.sum(area_cells)
    row = iota((8, 128), 0)
    lane = iota((8, 128), 1)

    step_cos, step_sin = step[0], step[1]
    share = DEVS // QUARTERS
    sends = []
    for quarter in range(QUARTERS):
        for pair in range(share // 2):
            cos_rows = []
            sin_rows = []
            for device in (quarter * share + 2 * pair, quarter * share + 2 * pair + 1):
                turn_cos, turn_sin = turn[0, device : device + 1, :], turn[1, device : device + 1, :]
                cos_rows.append(turn_cos * step_cos - turn_sin * step_sin)
                sin_rows.append(turn_sin * step_cos + turn_cos * step_sin)
            rows = slice(2 * ORDERS * pair, 2 * ORDERS * (pair + 1))
            for slot, parts in enumerate((cos_rows, sin_rows)):
                high, low = halves(jnp.concatenate(parts, axis=0))
                wave[quarter, slot, rows, :] = high
                wave[quarter, 2 + slot, rows, :] = low
        sums = dot_nt(wave[quarter, 0], for_cos) + dot_nt(wave[quarter, 1], for_sin)
        sums = sums[:, :128] + sums[:, 128:]
        sums = sums + dot_nt(wave[quarter, 2], for_cos[:128]) + dot_nt(wave[quarter, 3], for_sin[:128])
        for spot in range(share):
            sent = sums[spot * ORDERS : (spot + 1) * ORDERS]
            if quarter == 0 and spot == 0:
                sent = jnp.where((row == 0) & (lane >= 64), area_sum, sent)
                sent = jnp.where((row == 0) & (lane == 64), flux_sum, sent)
            message[quarter * share + spot] = sent
        place = pl.ds(quarter * share, share)
        pair = (message.at[place], message_out.at[place])
        sends += fetch((pair,), send_sems.at[pl.ds(quarter, 1)])
    for load in loads[6:]:
        load.wait()
    for slot, values in enumerate((tiles[0], tiles[1], tiles[2], tiles[3], sea, tiles[4])):
        strips[0, slot * WIDE : (slot + 1) * WIDE, :] = values[ROWS - WIDE :, :]
        strips[1, slot * WIDE : (slot + 1) * WIDE, :] = values[:WIDE, :]
    odd = lat_index % 2
    sends += fetch(((strips.at[odd], near_out), (strips.at[1 - odd], far_out)), strip_sems)
    for copy in sends:
        copy.wait()


def pairs_of():
    found = []
    for first, last, kept in ((0, 512, 8), (512, 768, 4), (768, 1024, 2)):
        steps = 2 * TILE // kept
        found += [(start, steps, kept) for start in range(first, last, steps)]
    return found


PAIRS = pairs_of()


def make_gains(love, balance, device, gains):
    lane = iota((8, 128), 1)
    degree = (128 * iota((8, 128), 0) + lane).astype(f32)
    gain = sal_ratio * love[...] / (2.0 * degree + 1.0)
    turned = pltpu.roll(gain, (128 - device) % 128, 1)
    above = jnp.concatenate([turned[1:], jnp.zeros((1, 128), f32)], axis=0)
    shifted = jnp.where(lane + device < 128, turned, above)
    padded = jnp.concatenate([shifted, jnp.zeros((8, 128), f32)], axis=0)
    for pair, (first, steps, kept) in enumerate(PAIRS):
        chunks = range(first // CHUNK, -(-(first + steps) // CHUNK))
        width = CHUNK * len(chunks)
        blocks = [padded[c : c + 8] * balance[:, c * CHUNK : (c + 1) * CHUNK] for c in chunks]
        parts = jnp.concatenate(halves(jnp.concatenate(blocks, axis=1)), axis=0)
        same = iota((ORDERS, TILE), 1) % kept == iota((ORDERS, TILE), 0)
        for parity in range(2):
            step = first % CHUNK + 2 * (iota((width, TILE), 1) // kept) + parity
            spread = (step == iota((width, TILE), 0)).astype(f32).astype(bf16)
            wide = dot_nn(parts, spread)
            gains[2 * pair + parity] = jnp.where(same, wide[:ORDERS] + wide[ORDERS:], 0.0)


def setup_kernel(
    height_in,
    flux_u_in,
    flux_v_in,
    depth_in,
    mask_in,
    flux_in,
    bands_in,
    love_in,
    balance_in,
    seeds_in,
    north_in,
    gains,
    balance,
    start,
    own,
    bands,
    mask,
    love,
    seeds,
    north,
    sems,
):
    device = position(lax.axis_index("lat"), lax.axis_index("lon"))
    loads = fetch(
        (
            (seeds_in, seeds),
            (north_in, north),
            (balance_in.at[device], balance),
            (love_in, love),
            (height_in, own.at[0]),
            (flux_u_in, own.at[1]),
            (flux_v_in, own.at[2]),
            (depth_in, own.at[3]),
            (mask_in, mask),
            (flux_in, own.at[5]),
            (bands_in.at[lax.axis_index("lat")], bands),
        ),
        sems,
    )
    for load in loads:
        load.wait()
    own[4] = mask[...].astype(f32)
    lane = iota((8, 128), 1)
    seed_log = jnp.sum(jnp.where(lane == device, seeds[...], 0.0), axis=1, keepdims=True)
    order = (device + DEVS * iota((8, 128), 0)).astype(f32)[:, :1]
    start[...] = jnp.exp(seed_log + order * north[1])
    make_gains(love, balance, device, gains)


def legendre_kernel(
    received, gains, balance, start, north, message_out, high, low, message, out_sems
):
    device = position(lax.axis_index("lat"), lax.axis_index("lon"))
    lane = iota((8, 128), 1)
    row = iota((8, 128), 0)
    left = lane < 64

    bands = []
    for lat in range(LATS):
        band = received[position(lat, 0)]
        for lon in range(1, LONS):
            band = band + received[position(lat, lon)]
        bands.append(band)
    sums = bands[0]
    for band in bands[1:]:
        sums = sums + band
    even = [bands[4 + part] + bands[3 - part] for part in range(4)]
    odd = [bands[4 + part] - bands[3 - part] for part in range(4)]

    def arrange(parts):
        cos_parts = []
        sin_parts = []
        for first, second in ((parts[0], parts[1]), (parts[2], parts[3])):
            cos_parts.append(jnp.where(left, first, pltpu.roll(second, 64, 1)))
            sin_parts.append(jnp.where(left, pltpu.roll(first, 64, 1), second))
        weight = north[2]
        return [
            jnp.concatenate(cos_parts, axis=1) * weight,
            jnp.concatenate(sin_parts, axis=1) * weight,
        ]

    lefts = []
    for parts in (even, odd):
        rows_high, rows_low = halves(jnp.concatenate(arrange(parts), axis=0))
        lefts.append(jnp.concatenate([rows_high, rows_low], axis=0))

    sine = north[0]
    state = [jnp.zeros((ORDERS, HALF), f32), start[...]]
    wide_row = iota((ORDERS, HALF), 0)

    def extend(pair):
        first, steps, kept = PAIRS[pair]
        share = ORDERS // kept
        block, packed, place = [None, None], [[], []], [2 * pair * TILE, (2 * pair + 1) * TILE]
        for step in range(steps):
            parity, part = step % 2, step // 2 % share
            previous, current = state
            if part == 0:
                block[parity] = current
            else:
                moved = pltpu.roll(current, part * kept, 0)
                block[parity] = jnp.where(wide_row < part * kept, block[parity], moved)
            turn = balance[:, first + step : first + step + 1] * sine
            state[0], state[1] = current, turn * current - previous
            if part == share - 1:
                packed[parity].append(block[parity])
            if len(packed[parity]) == 2:
                rows = slice(place[parity], place[parity] + 16)
                high[rows, :], low[rows, :] = halves(jnp.concatenate(packed[parity], axis=0))
                packed[parity] = []
                place[parity] += 16

    def analyse(tile):
        place = slice(tile * TILE, (tile + 1) * TILE)
        left_rows = lefts[tile % 2]
        both = dot_nt(left_rows, high[place, :])
        found = both[:16] + both[16:] + dot_nt(left_rows[:16], low[place, :])
        gain = gains[tile]
        return jnp.concatenate(halves(found * jnp.concatenate([gain, gain], axis=0)), axis=0)

    def synthesise(tile, coefs):
        place = slice(tile * TILE, (tile + 1) * TILE)
        return dot_nn(coefs, high[place, :]), dot_nn(coefs[:16], low[place, :])

    count = len(PAIRS)
    total_high = [jnp.zeros((32, HALF), f32)] * 2
    total_low = [jnp.zeros((16, HALF), f32)] * 2
    coefs = {}
    for turn in range(count + 2):
        if turn < count:
            extend(turn)
        for parity in range(2):
            if 1 <= turn <= count:
                tile = 2 * (turn - 1) + parity
                coefs[tile] = analyse(tile)
        for parity in range(2):
            if turn >= 2:
                tile = 2 * (turn - 2) + parity
                more_high, more_low = synthesise(tile, coefs.pop(tile))
                total_high[parity] = total_high[parity] + more_high
                total_low[parity] = total_low[parity] + more_low
    total_even, total_odd = [
        total_high[parity][:16] + total_high[parity][16:] + total_low[parity] for parity in range(2)
    ]

    flux_sum = jnp.sum(jnp.where((row == 0) & (lane == 64), sums, 0.0))
    area_sum = jnp.sum(jnp.where((row == 0) & (lane == 65), sums, 0.0))
    mean = jnp.full((8, 128), flux_sum, f32) / jnp.full((8, 128), area_sum, f32)
    slot = (device == 0) & (row == 0) & (lane >= 64)
    cos_even, sin_even = total_even[0:8, :], total_even[8:16, :]
    cos_odd, sin_odd = total_odd[0:8, :], total_odd[8:16, :]
    copies = []
    for north_side in (True, False):
        if north_side:
            cos_all, sin_all = cos_even + cos_odd, sin_even + sin_odd
        else:
            cos_all, sin_all = cos_even - cos_odd, sin_even - sin_odd
        for part in range(4):
            block = slice(128 * (part // 2), 128 * (part // 2) + 128)
            cos_part, sin_part = cos_all[:, block], sin_all[:, block]
            if part % 2 == 0:
                sent = jnp.where(left, cos_part, pltpu.roll(sin_part, 64, 1))
            else:
                sent = jnp.where(left, pltpu.roll(cos_part, 64, 1), sin_part)
            sent = jnp.where(slot, mean, sent)
            lat = 4 + part if north_side else 3 - part
            for lon in range(LONS):
                message[position(lat, lon)] = sent
            part_place = pl.ds(position(lat, 0) // LONS * LONS, LONS)
            copies += fetch(((message.at[part_place], message_out.at[part_place]),), out_sems.at[pl.ds(lat, 1)])
    for copy in copies:
        copy.wait()


def finish_kernel(
    received,
    from_near,
    from_far,
    wave,
    own,
    edges,
    bands,
    height_out,
    u_out,
    v_out,
    sal_out,
    blocks,
    results,
    out_sems,
):
    lat_index = lax.axis_index("lat")
    lane = iota((8, 128), 1)
    first_row = iota((8, 128), 0) == 0
    mean = jnp.sum(jnp.where(first_row & (lane == 64), received[0], 0.0))
    first = jnp.where(first_row & (lane >= 64), 0.0, received[0])
    others = received[1:].reshape(DEG - ORDERS, 128)
    turned = jnp.concatenate([first, others], axis=0).T
    high, low = halves(turned)
    cos_both = jnp.concatenate([high[:64], low[:64]], axis=0)
    sin_both = jnp.concatenate([high[64:], low[64:]], axis=0)

    wide_lane = iota((PAD_ROWS, 128), 1)
    fill = jnp.zeros((128 - STRIP, 128), f32)
    odd_lon = lax.axis_index("lon") % 2 == 1
    west_in = jnp.where(odd_lon, from_near[...], from_far[...])
    east_in = jnp.where(odd_lon, from_far[...], from_near[...])
    west = jnp.concatenate([west_in, fill], axis=0).T[:PAD_ROWS, :]
    east = jnp.concatenate([east_in, fill], axis=0).T[:PAD_ROWS, :]
    for slot in range(FIELDS):
        high_side = pltpu.roll(east, 128 - slot * WIDE, 1) if slot else east
        low_side = pltpu.roll(west, 128 - WIDE - slot * WIDE, 1)
        blocks[slot, :ROWS, :COLS] = own[slot]
        blocks[slot, ROWS:, :COLS] = edges[slot]
        blocks[slot, :, COLS:] = jnp.where(
            wide_lane < WIDE, high_side, jnp.where(wide_lane >= 128 - WIDE, low_side, 0.0)
        )
    both = jnp.zeros((2 * ROWS, COLS), f32)
    field = jnp.zeros((ROWS, COLS), f32)
    for part in range(QUARTERS):
        place = slice(part * QUARTER, (part + 1) * QUARTER)
        both += dot_nn(cos_both[:, place], wave[part, 0]) + dot_nn(sin_both[:, place], wave[part, 1])
        field += dot_nn(high[:64, place], wave[part, 2]) + dot_nn(high[64:, place], wave[part, 3])
    field = field + both[:64] + both[64:]
    field_high, field_low = halves(field)
    order = row_order(lat_index).astype(bf16)
    field = dot_nn(order, field_high) + dot_nn(order, field_low)

    def eastward(values):
        return pltpu.roll(values, PAD_COLS - 1, 1)

    def northward(values):
        return pltpu.roll(values, PAD_ROWS - 1, 0)

    height_now, u_now, v_now, depth_all, sea, flux_all = [blocks[slot] for slot in range(FIELDS)]
    inverse_cos = jnp.concatenate([bands[0]] * 3, axis=1)
    north_cos = jnp.concatenate([bands[1]] * 3, axis=1)
    open_u = sea * eastward(sea)
    open_v = sea * northward(sea)
    pull_u = open_u * (0.5 * step_time) * (depth_all + eastward(depth_all)) * inverse_cos
    pull_v = open_v * (0.5 * step_time) * (depth_all + northward(depth_all))
    scale = step_time * inverse_cos
    forcing = step_time * sea * (flux_all - mean)
    for repeat in range(ITERS):
        north_flux = v_now * north_cos
        divergence = u_now - pltpu.roll(u_now, 1, 1) + (north_flux - pltpu.roll(north_flux, 1, 0))
        height_now = height_now - scale * divergence + forcing
        u_now = open_u * u_now - pull_u * (eastward(height_now) - height_now)
        v_now = open_v * v_now - pull_v * (northward(height_now) - height_now)
    for slot, values in enumerate((height_now, u_now, v_now)):
        results[slot] = values[:ROWS, :COLS]
    results[3] = field * sea[:ROWS, :COLS]
    outs = (height_out, u_out, v_out, sal_out)
    for copy in fetch([(results.at[slot], out) for slot, out in enumerate(outs)], out_sems):
        copy.wait()


def column_kernel(from_near, from_far, own, near_out, far_out, edges, sides, out_sems):
    odd_lat = lax.axis_index("lat") % 2 == 1
    odd = lax.axis_index("lon") % 2
    lane = iota((PAD_ROWS, 128), 1)
    west = jnp.zeros((PAD_ROWS, 128), f32)
    east = jnp.zeros((PAD_ROWS, 128), f32)
    for slot in range(FIELDS):
        rows = slice(slot * WIDE, (slot + 1) * WIDE)
        one, other = from_near[rows, :], from_far[rows, :]
        edges[slot, 0:WIDE, :] = jnp.where(odd_lat, other, one)
        edges[slot, WIDE : 2 * WIDE, :] = jnp.where(odd_lat, one, other)
        here = (lane >= slot * WIDE) & (lane < (slot + 1) * WIDE)
        west_part = jnp.concatenate([own[slot, :, 0:128], edges[slot, :, 0:128]], axis=0)
        east_part = jnp.concatenate([own[slot, :, COLS - 128 :], edges[slot, :, COLS - 128 :]], axis=0)
        east_part = pltpu.roll(east_part, (WIDE + slot * WIDE) % 128, 1)
        if slot:
            west_part = pltpu.roll(west_part, slot * WIDE, 1)
        west = jnp.where(here, west_part, west)
        east = jnp.where(here, east_part, east)
    fill = jnp.zeros((128 - PAD_ROWS, 128), f32)
    sides[1] = jnp.concatenate([west, fill], axis=0).T[:STRIP, :]
    sides[0] = jnp.concatenate([east, fill], axis=0).T[:STRIP, :]
    for copy in fetch(((sides.at[odd], near_out), (sides.at[1 - odd], far_out)), out_sems):
        copy.wait()


def far_call(kernel, name, operands, results, scratch, work=None, here=(), near=(), near_out=()):
    placed = []
    specs = []
    out_spaces = [pltpu.VMEM if slot in near_out else pltpu.HBM for slot in range(len(results))]
    for slot, operand in enumerate(operands):
        if slot in here:
            space = pltpu.VMEM
        elif slot in near:
            space = pltpu.VMEM
            operand = pltpu.with_memory_space_constraint(operand, pltpu.VMEM)
        else:
            space = pltpu.HBM
            operand = pltpu.with_memory_space_constraint(operand, pltpu.HBM)
        placed.append(operand)
        specs.append(pl.BlockSpec(memory_space=space))
    return pl.pallas_call(
        kernel,
        out_shape=tuple(space(*result) for space, result in zip(out_spaces, results)),
        in_specs=specs,
        out_specs=tuple(pl.BlockSpec(memory_space=space) for space in out_spaces),
        scratch_shapes=scratch,
        compiler_params=pltpu.CompilerParams(vmem_limit_bytes=32 << 20),
        cost_estimate=work,
        name=name,
    )(*placed)


def cost(flops, moved):
    return pl.CostEstimate(flops=flops, bytes_accessed=moved, transcendentals=0)


def on_device(sea_height, trans_u, trans_v, depth, sea_mask, freshwater_flux, love_factor):
    north = jnp.asarray(north_tables())
    fields = (sea_height, trans_u, trans_v, depth, sea_mask, freshwater_flux)
    vmem = pltpu.VMEM
    copies = pltpu.SemaphoreType.DMA
    tile = ((ROWS, COLS), f32)
    strip = ((STRIP, COLS), f32)
    side = ((STRIP, 128), f32)
    messages = ((DEVS, 8, 128), f32)
    tiles = vmem((FIELDS, ROWS, COLS), f32)
    mask_tile = vmem((ROWS, COLS), jnp.int32)

    message, strip_near, strip_far, wave = far_call(
        forward_kernel,
        "forward",
        fields + (jnp.asarray(turn_tables()), jnp.asarray(step_tables()), jnp.asarray(area_table())),
        (messages, strip, strip, ((QUARTERS, 4, QUARTER, COLS), bf16)),
        [
            tiles,
            mask_tile,
            vmem((2, DEVS, COLS), f32),
            vmem((2, ORDERS, COLS), f32),
            vmem((ROWS, 128), f32),
            vmem(*messages),
            vmem((2, STRIP, COLS), f32),
            copies((9,)),
            copies((QUARTERS,)),
            copies((2,)),
        ],
        work=cost(6 * 2 * 1024 * 256 * 256, 3 << 20),
        near_out=(3,),
    )
    received = exchange(message)

    near_pairs = [(i, i ^ 1) for i in range(LATS)]
    far_pairs = [(i, ((i + 1) ^ 1) - 1) for i in range(1, LATS - 1)]
    from_near = lax.ppermute(strip_near, "lat", near_pairs)
    from_far = lax.ppermute(strip_far, "lat", far_pairs)

    gain_tiles = ((2 * len(PAIRS), ORDERS, TILE), f32)
    squares = ((ORDERS, DEG), f32)
    first_rows = ((ORDERS, HALF), f32)
    own_fields = ((FIELDS, ROWS, COLS), f32)
    gains, balance, start, own, bands = far_call(
        setup_kernel,
        "setup",
        fields
        + (
            jnp.asarray(row_tables()),
            love_factor.reshape(8, 128),
            jnp.asarray(balance_table()),
            jnp.asarray(seed_table()),
            north,
        ),
        (gain_tiles, squares, first_rows, own_fields, ((2, PAD_ROWS, 128), f32)),
        [
            mask_tile,
            vmem((8, 128), f32),
            vmem((ORDERS, DEVS), f32),
            vmem((3, 8, HALF), f32),
            copies((11,)),
        ],
        work=cost(2 << 20, 1 << 20),
        near_out=(0, 1, 2, 3, 4),
    )
    to_near, to_far, edges = far_call(
        column_kernel,
        "columns",
        (from_near, from_far, own),
        (side, side, ((FIELDS, 2 * WIDE, COLS), f32)),
        [vmem((2, STRIP, 128), f32), copies((2,))],
        here=(0, 1),
        near=(2,),
        near_out=(2,),
    )
    received, to_near, to_far = lax.optimization_barrier((received, to_near, to_far))
    table = ((2 * len(PAIRS) * TILE, HALF), bf16)
    (reply,) = far_call(
        legendre_kernel,
        "legendre",
        (received, gains, balance, start, north),
        (messages,),
        [vmem(*table), vmem(*table), vmem(*messages), copies((LATS,))],
        work=cost(6 * 2 * 64 * 8192 * 256, 9 << 20),
        here=(0, 4),
        near=(1, 2, 3),
    )
    answer = exchange(reply)

    near_lons = [(i, i ^ 1) for i in range(LONS)]
    far_lons = [(i, (((i + 1) ^ 1) - 1) % LONS) for i in range(LONS)]
    side_near = lax.ppermute(to_near, "lon", near_lons)
    side_far = lax.ppermute(to_far, "lon", far_lons)

    return far_call(
        finish_kernel,
        "finish",
        (answer, side_near, side_far, wave, own, edges, bands),
        (tile,) * 4,
        [
            vmem((FIELDS, PAD_ROWS, PAD_COLS), f32),
            vmem((4, ROWS, COLS), f32),
            copies((4,)),
        ],
        here=(0, 1, 2),
        near=(3, 4, 5, 6),
    )


def solution(mesh):
    tiles = P("lat", "lon")
    return jax.shard_map(
        on_device,
        mesh=mesh,
        in_specs=(tiles,) * 6 + (P(),),
        out_specs=(tiles,) * 4,
        check_vma=False,
    )
```

```python
import math

import jax
import jax.numpy as jnp
import ml_dtypes
import numpy as np
from jax import lax
from jax.experimental import pallas as pl
from jax.experimental.pallas import tpu as pltpu
from jax.sharding import PartitionSpec as P

ITERS = 4
NLON = 4096
NLAT = 512
DEG = 1024
LATS = 8
LONS = 16
DEVS = LATS * LONS
ROWS = NLAT // LATS
COLS = NLON // LONS
HALF = NLAT // 2
ORDERS = DEG // DEVS
WIDE = 4
FIELDS = 6
PAD_ROWS = ROWS + 2 * WIDE
PAD_COLS = COLS + 128
STRIP = FIELDS * WIDE
CHUNK = 128
CHUNKS = DEG // CHUNK
TILE = 256
QUARTERS = 4
QUARTER = DEG // QUARTERS

step_time = 0.5
sal_ratio = 3.0 * 1035.0 / 5517.0
spacing = 2.0 * math.pi / NLON

f32 = jnp.float32
bf16 = jnp.bfloat16


def turn_tables():
    column = np.arange(NLON).reshape(LONS, 1, COLS)
    angle = column * np.arange(DEVS)[None, :, None] % NLON * (2.0 * math.pi / NLON)
    return np.stack([np.cos(angle), np.sin(angle)], axis=1).astype(np.float32)


def step_tables():
    angle = np.arange(ORDERS)[:, None] * DEVS * np.arange(COLS)[None, :] % NLON
    angle = angle * (2.0 * math.pi / NLON)
    return np.stack([np.cos(angle), np.sin(angle)]).astype(np.float32)


def balance_table():
    order = np.arange(DEG, dtype=np.float64)
    scale = np.ones(DEG)
    squares = []
    for step in range(DEG):
        squares.append(scale * scale)
        degree = order + step + 1.0
        factor = np.sqrt((4.0 * degree * degree - 1.0) / (degree * degree - order * order))
        scale = factor / scale
    return np.stack(squares, axis=1).reshape(ORDERS, DEVS, DEG).transpose(1, 0, 2).astype(np.float32)


def latitude_of(rows):
    return (rows + 0.5 - NLAT / 2) * spacing


def row_tables():
    local = np.concatenate([np.arange(ROWS + WIDE), np.arange(-WIDE, 0)])
    latitude = latitude_of(np.arange(LATS)[:, None] * ROWS + local[None, :])
    both = np.stack([1.0 / np.cos(latitude), np.cos(latitude + spacing / 2)], axis=1)
    return np.broadcast_to(both[..., None], both.shape + (128,)).astype(np.float32)


def area_table():
    latitude = latitude_of(np.arange(NLAT)).reshape(LATS, ROWS, 1)
    return np.broadcast_to(np.cos(latitude), (LATS, ROWS, 128)).astype(np.float32)


def north_tables():
    latitude = latitude_of(np.arange(HALF, NLAT))
    weight = np.cos(latitude) * spacing * spacing / (4.0 * math.pi)
    table = np.stack([np.sin(latitude), np.log(np.cos(latitude)), weight])
    return np.broadcast_to(table[:, None, :], (3, 8, HALF)).astype(np.float32)


def seed_table():
    order = np.arange(1, DEG)
    grown = 0.5 * math.log(2.0) + 0.5 * np.cumsum(np.log((2.0 * order + 1.0) / (2.0 * order)))
    return np.concatenate([[0.0], grown]).reshape(ORDERS, DEVS).astype(np.float32)


def position(lat, lon):
    return (lat % 2 * (LATS // 2) + lat // 2) * LONS + (lon + 4) % LONS


def exchange(messages):
    mesh_order = [(position(lat, lon), lat * LONS + lon) for lat in range(LATS) for lon in range(LONS)]
    group = [place for _, place in sorted(mesh_order)]
    return lax.all_to_all(
        messages,
        ("lat", "lon"),
        split_axis=0,
        concat_axis=0,
        tiled=True,
        axis_index_groups=[group],
    )


def iota(shape, dim):
    return lax.broadcasted_iota(jnp.int32, shape, dim)


def halves(values):
    high = values.astype(bf16)
    low = (values - high.astype(f32)).astype(bf16)
    return high, low


def dot_nt(left, right):
    return lax.dot_general(left, right, (((1,), (1,)), ((), ())), preferred_element_type=f32)


def dot_nn(left, right):
    return lax.dot_general(left, right, (((1,), (0,)), ((), ())), preferred_element_type=f32)


def fetch(pairs, sems):
    copies = [pltpu.make_async_copy(a, b, sems.at[slot]) for slot, (a, b) in enumerate(pairs)]
    for copy in copies:
        copy.start()
    return copies


def row_order(lat_index):
    row = iota((ROWS, ROWS), 0)
    col = iota((ROWS, ROWS), 1)
    south = lat_index < LATS // 2
    return jnp.where(south, (row + col == ROWS - 1).astype(f32), (row == col).astype(f32))


def forward_kernel(
    height_in,
    flux_u_in,
    flux_v_in,
    depth_in,
    mask_in,
    flux_in,
    turn_in,
    step_in,
    area_in,
    message_out,
    near_out,
    far_out,
    wave,
    tiles,
    mask,
    turn,
    step,
    area,
    message,
    strips,
    sems,
    send_sems,
    strip_sems,
):
    lat_index = lax.axis_index("lat")
    loads = fetch(
        (
            (mask_in, mask),
            (height_in, tiles.at[0]),
            (turn_in.at[lax.axis_index("lon")], turn),
            (step_in, step),
            (flux_in, tiles.at[4]),
            (area_in.at[lat_index], area),
            (flux_u_in, tiles.at[1]),
            (flux_v_in, tiles.at[2]),
            (depth_in, tiles.at[3]),
        ),
        sems,
    )
    for load in loads[:6]:
        load.wait()
    sea = mask[...].astype(f32)
    mass_high, mass_low = halves(sea * tiles[0])
    both = jnp.concatenate([mass_high, mass_low], axis=1)
    both = dot_nn(row_order(lat_index).astype(bf16), both).astype(bf16)
    mass_high, mass_low = both[:, :COLS], both[:, COLS:]
    zero = jnp.zeros_like(mass_high)
    for_cos = jnp.concatenate([mass_high, zero, mass_low, zero], axis=0)
    for_sin = jnp.concatenate([zero, mass_high, zero, mass_low], axis=0)

    band = area[...]
    area_cells = sea * jnp.concatenate([band, band], axis=1)
    flux_sum = jnp.sum(area_cells * tiles[4])
    area_sum = jnp.sum(area_cells)
    row = iota((8, 128), 0)
    lane = iota((8, 128), 1)

    step_cos, step_sin = step[0], step[1]
    share = DEVS // QUARTERS
    sends = []
    for quarter in range(QUARTERS):
        for pair in range(share // 2):
            cos_rows = []
            sin_rows = []
            for device in (quarter * share + 2 * pair, quarter * share + 2 * pair + 1):
                turn_cos, turn_sin = turn[0, device : device + 1, :], turn[1, device : device + 1, :]
                cos_rows.append(turn_cos * step_cos - turn_sin * step_sin)
                sin_rows.append(turn_sin * step_cos + turn_cos * step_sin)
            rows = slice(2 * ORDERS * pair, 2 * ORDERS * (pair + 1))
            for slot, parts in enumerate((cos_rows, sin_rows)):
                high, low = halves(jnp.concatenate(parts, axis=0))
                wave[quarter, slot, rows, :] = high
                wave[quarter, 2 + slot, rows, :] = low
        sums = dot_nt(wave[quarter, 0], for_cos) + dot_nt(wave[quarter, 1], for_sin)
        sums = sums[:, :128] + sums[:, 128:]
        sums = sums + dot_nt(wave[quarter, 2], for_cos[:128]) + dot_nt(wave[quarter, 3], for_sin[:128])
        for spot in range(share):
            sent = sums[spot * ORDERS : (spot + 1) * ORDERS]
            if quarter == 0 and spot == 0:
                sent = jnp.where((row == 0) & (lane >= 64), area_sum, sent)
                sent = jnp.where((row == 0) & (lane == 64), flux_sum, sent)
            message[quarter * share + spot] = sent
        place = pl.ds(quarter * share, share)
        pair = (message.at[place], message_out.at[place])
        sends += fetch((pair,), send_sems.at[pl.ds(quarter, 1)])
    for load in loads[6:]:
        load.wait()
    for slot, values in enumerate((tiles[0], tiles[1], tiles[2], tiles[3], sea, tiles[4])):
        strips[0, slot * WIDE : (slot + 1) * WIDE, :] = values[ROWS - WIDE :, :]
        strips[1, slot * WIDE : (slot + 1) * WIDE, :] = values[:WIDE, :]
    odd = lat_index % 2
    sends += fetch(((strips.at[odd], near_out), (strips.at[1 - odd], far_out)), strip_sems)
    for copy in sends:
        copy.wait()


def pairs_of():
    found = []
    for first, last, kept in ((0, 512, 8), (512, 768, 4), (768, 1024, 2)):
        steps = 2 * TILE // kept
        found += [(start, steps, kept) for start in range(first, last, steps)]
    return found


PAIRS = pairs_of()


def make_gains(love, balance, device, gains):
    lane = iota((8, 128), 1)
    degree = (128 * iota((8, 128), 0) + lane).astype(f32)
    gain = sal_ratio * love[...] / (2.0 * degree + 1.0)
    turned = pltpu.roll(gain, (128 - device) % 128, 1)
    above = jnp.concatenate([turned[1:], jnp.zeros((1, 128), f32)], axis=0)
    shifted = jnp.where(lane + device < 128, turned, above)
    padded = jnp.concatenate([shifted, jnp.zeros((8, 128), f32)], axis=0)
    for pair, (first, steps, kept) in enumerate(PAIRS):
        chunks = range(first // CHUNK, -(-(first + steps) // CHUNK))
        width = CHUNK * len(chunks)
        blocks = [padded[c : c + 8] * balance[:, c * CHUNK : (c + 1) * CHUNK] for c in chunks]
        parts = jnp.concatenate(halves(jnp.concatenate(blocks, axis=1)), axis=0)
        same = iota((ORDERS, TILE), 1) % kept == iota((ORDERS, TILE), 0)
        for parity in range(2):
            step = first % CHUNK + 2 * (iota((width, TILE), 1) // kept) + parity
            spread = (step == iota((width, TILE), 0)).astype(f32).astype(bf16)
            wide = dot_nn(parts, spread)
            gains[2 * pair + parity] = jnp.where(same, wide[:ORDERS] + wide[ORDERS:], 0.0)


def setup_kernel(
    height_in,
    flux_u_in,
    flux_v_in,
    depth_in,
    mask_in,
    flux_in,
    bands_in,
    love_in,
    balance_in,
    seeds_in,
    north_in,
    gains,
    balance,
    start,
    own,
    bands,
    mask,
    love,
    seeds,
    north,
    sems,
):
    device = position(lax.axis_index("lat"), lax.axis_index("lon"))
    loads = fetch(
        (
            (seeds_in, seeds),
            (north_in, north),
            (balance_in.at[device], balance),
            (love_in, love),
            (height_in, own.at[0]),
            (flux_u_in, own.at[1]),
            (flux_v_in, own.at[2]),
            (depth_in, own.at[3]),
            (mask_in, mask),
            (flux_in, own.at[5]),
            (bands_in.at[lax.axis_index("lat")], bands),
        ),
        sems,
    )
    for load in loads:
        load.wait()
    own[4] = mask[...].astype(f32)
    lane = iota((8, 128), 1)
    seed_log = jnp.sum(jnp.where(lane == device, seeds[...], 0.0), axis=1, keepdims=True)
    order = (device + DEVS * iota((8, 128), 0)).astype(f32)[:, :1]
    start[...] = jnp.exp(seed_log + order * north[1])
    make_gains(love, balance, device, gains)


def legendre_kernel(
    received, gains, balance, start, north, message_out, high, low, message, out_sems
):
    device = position(lax.axis_index("lat"), lax.axis_index("lon"))
    lane = iota((8, 128), 1)
    row = iota((8, 128), 0)
    left = lane < 64

    bands = []
    for lat in range(LATS):
        band = received[position(lat, 0)]
        for lon in range(1, LONS):
            band = band + received[position(lat, lon)]
        bands.append(band)
    sums = bands[0]
    for band in bands[1:]:
        sums = sums + band
    even = [bands[4 + part] + bands[3 - part] for part in range(4)]
    odd = [bands[4 + part] - bands[3 - part] for part in range(4)]

    def arrange(parts):
        cos_parts = []
        sin_parts = []
        for first, second in ((parts[0], parts[1]), (parts[2], parts[3])):
            cos_parts.append(jnp.where(left, first, pltpu.roll(second, 64, 1)))
            sin_parts.append(jnp.where(left, pltpu.roll(first, 64, 1), second))
        weight = north[2]
        return [
            jnp.concatenate(cos_parts, axis=1) * weight,
            jnp.concatenate(sin_parts, axis=1) * weight,
        ]

    lefts = []
    for parts in (even, odd):
        rows_high, rows_low = halves(jnp.concatenate(arrange(parts), axis=0))
        lefts.append(jnp.concatenate([rows_high, rows_low], axis=0))

    sine = north[0]
    state = [jnp.zeros((ORDERS, HALF), f32), start[...]]
    wide_row = iota((ORDERS, HALF), 0)

    def extend(pair):
        first, steps, kept = PAIRS[pair]
        share = ORDERS // kept
        block, packed, place = [None, None], [[], []], [2 * pair * TILE, (2 * pair + 1) * TILE]
        for step in range(steps):
            parity, part = step % 2, step // 2 % share
            previous, current = state
            if part == 0:
                block[parity] = current
            else:
                moved = pltpu.roll(current, part * kept, 0)
                block[parity] = jnp.where(wide_row < part * kept, block[parity], moved)
            turn = balance[:, first + step : first + step + 1] * sine
            state[0], state[1] = current, turn * current - previous
            if part == share - 1:
                packed[parity].append(block[parity])
            if len(packed[parity]) == 2:
                rows = slice(place[parity], place[parity] + 16)
                high[rows, :], low[rows, :] = halves(jnp.concatenate(packed[parity], axis=0))
                packed[parity] = []
                place[parity] += 16

    def analyse(tile):
        place = slice(tile * TILE, (tile + 1) * TILE)
        left_rows = lefts[tile % 2]
        both = dot_nt(left_rows, high[place, :])
        found = both[:16] + both[16:] + dot_nt(left_rows[:16], low[place, :])
        gain = gains[tile]
        return jnp.concatenate(halves(found * jnp.concatenate([gain, gain], axis=0)), axis=0)

    def synthesise(tile, coefs):
        place = slice(tile * TILE, (tile + 1) * TILE)
        return dot_nn(coefs, high[place, :]), dot_nn(coefs[:16], low[place, :])

    count = len(PAIRS)
    total_high = [jnp.zeros((32, HALF), f32)] * 2
    total_low = [jnp.zeros((16, HALF), f32)] * 2
    coefs = {}
    for turn in range(count + 2):
        if turn < count:
            extend(turn)
        for parity in range(2):
            if 1 <= turn <= count:
                tile = 2 * (turn - 1) + parity
                coefs[tile] = analyse(tile)
        for parity in range(2):
            if turn >= 2:
                tile = 2 * (turn - 2) + parity
                more_high, more_low = synthesise(tile, coefs.pop(tile))
                total_high[parity] = total_high[parity] + more_high
                total_low[parity] = total_low[parity] + more_low
    total_even, total_odd = [
        total_high[parity][:16] + total_high[parity][16:] + total_low[parity] for parity in range(2)
    ]

    flux_sum = jnp.sum(jnp.where((row == 0) & (lane == 64), sums, 0.0))
    area_sum = jnp.sum(jnp.where((row == 0) & (lane == 65), sums, 0.0))
    mean = jnp.full((8, 128), flux_sum, f32) / jnp.full((8, 128), area_sum, f32)
    slot = (device == 0) & (row == 0) & (lane >= 64)
    cos_even, sin_even = total_even[0:8, :], total_even[8:16, :]
    cos_odd, sin_odd = total_odd[0:8, :], total_odd[8:16, :]
    copies = []
    for north_side in (True, False):
        if north_side:
            cos_all, sin_all = cos_even + cos_odd, sin_even + sin_odd
        else:
            cos_all, sin_all = cos_even - cos_odd, sin_even - sin_odd
        for part in range(4):
            block = slice(128 * (part // 2), 128 * (part // 2) + 128)
            cos_part, sin_part = cos_all[:, block], sin_all[:, block]
            if part % 2 == 0:
                sent = jnp.where(left, cos_part, pltpu.roll(sin_part, 64, 1))
            else:
                sent = jnp.where(left, pltpu.roll(cos_part, 64, 1), sin_part)
            sent = jnp.where(slot, mean, sent)
            lat = 4 + part if north_side else 3 - part
            for lon in range(LONS):
                message[position(lat, lon)] = sent
            part_place = pl.ds(position(lat, 0) // LONS * LONS, LONS)
            copies += fetch(((message.at[part_place], message_out.at[part_place]),), out_sems.at[pl.ds(lat, 1)])
    for copy in copies:
        copy.wait()


def finish_kernel(
    received,
    from_near,
    from_far,
    wave,
    own,
    edges,
    bands,
    height_out,
    u_out,
    v_out,
    sal_out,
    blocks,
    results,
    out_sems,
):
    lat_index = lax.axis_index("lat")
    lane = iota((8, 128), 1)
    first_row = iota((8, 128), 0) == 0
    mean = jnp.sum(jnp.where(first_row & (lane == 64), received[0], 0.0))
    first = jnp.where(first_row & (lane >= 64), 0.0, received[0])
    others = received[1:].reshape(DEG - ORDERS, 128)
    turned = jnp.concatenate([first, others], axis=0).T
    high, low = halves(turned)
    cos_both = jnp.concatenate([high[:64], low[:64]], axis=0)
    sin_both = jnp.concatenate([high[64:], low[64:]], axis=0)

    wide_lane = iota((PAD_ROWS, 128), 1)
    fill = jnp.zeros((128 - STRIP, 128), f32)
    odd_lon = lax.axis_index("lon") % 2 == 1
    west_in = jnp.where(odd_lon, from_near[...], from_far[...])
    east_in = jnp.where(odd_lon, from_far[...], from_near[...])
    west = jnp.concatenate([west_in, fill], axis=0).T[:PAD_ROWS, :]
    east = jnp.concatenate([east_in, fill], axis=0).T[:PAD_ROWS, :]
    for slot in range(FIELDS):
        high_side = pltpu.roll(east, 128 - slot * WIDE, 1) if slot else east
        low_side = pltpu.roll(west, 128 - WIDE - slot * WIDE, 1)
        blocks[slot, :ROWS, :COLS] = own[slot]
        blocks[slot, ROWS:, :COLS] = edges[slot]
        blocks[slot, :, COLS:] = jnp.where(
            wide_lane < WIDE, high_side, jnp.where(wide_lane >= 128 - WIDE, low_side, 0.0)
        )
    both = jnp.zeros((2 * ROWS, COLS), f32)
    field = jnp.zeros((ROWS, COLS), f32)
    for part in range(QUARTERS):
        place = slice(part * QUARTER, (part + 1) * QUARTER)
        both += dot_nn(cos_both[:, place], wave[part, 0]) + dot_nn(sin_both[:, place], wave[part, 1])
        field += dot_nn(high[:64, place], wave[part, 2]) + dot_nn(high[64:, place], wave[part, 3])
    field = field + both[:64] + both[64:]

    def eastward(values):
        return pltpu.roll(values, PAD_COLS - 1, 1)

    def northward(values):
        return pltpu.roll(values, PAD_ROWS - 1, 0)

    height_now, u_now, v_now, depth_all, sea, flux_all = [blocks[slot] for slot in range(FIELDS)]
    inverse_cos = jnp.concatenate([bands[0]] * 3, axis=1)
    north_cos = jnp.concatenate([bands[1]] * 3, axis=1)
    open_u = sea * eastward(sea)
    open_v = sea * northward(sea)
    pull_u = open_u * (0.5 * step_time) * (depth_all + eastward(depth_all)) * inverse_cos
    pull_v = open_v * (0.5 * step_time) * (depth_all + northward(depth_all))
    scale = step_time * inverse_cos
    forcing = step_time * sea * (flux_all - mean)
    for repeat in range(ITERS):
        north_flux = v_now * north_cos
        divergence = u_now - pltpu.roll(u_now, 1, 1) + (north_flux - pltpu.roll(north_flux, 1, 0))
        height_now = height_now - scale * divergence + forcing
        u_now = open_u * u_now - pull_u * (eastward(height_now) - height_now)
        v_now = open_v * v_now - pull_v * (northward(height_now) - height_now)
    for slot, values in enumerate((height_now, u_now, v_now)):
        results[slot] = values[:ROWS, :COLS]
    pairs = zip((results.at[0], results.at[1], results.at[2]), (height_out, u_out, v_out))
    sends = fetch(pairs, out_sems)
    field_high, field_low = halves(field)
    order = row_order(lat_index).astype(bf16)
    field = dot_nn(order, field_high) + dot_nn(order, field_low)
    results[3] = field * sea[:ROWS, :COLS]
    sends += fetch(((results.at[3], sal_out),), out_sems.at[pl.ds(3, 1)])
    for copy in sends:
        copy.wait()


def column_kernel(from_near, from_far, own, near_out, far_out, edges, sides, out_sems):
    odd_lat = lax.axis_index("lat") % 2 == 1
    odd = lax.axis_index("lon") % 2
    lane = iota((PAD_ROWS, 128), 1)
    west = jnp.zeros((PAD_ROWS, 128), f32)
    east = jnp.zeros((PAD_ROWS, 128), f32)
    for slot in range(FIELDS):
        rows = slice(slot * WIDE, (slot + 1) * WIDE)
        one, other = from_near[rows, :], from_far[rows, :]
        edges[slot, 0:WIDE, :] = jnp.where(odd_lat, other, one)
        edges[slot, WIDE : 2 * WIDE, :] = jnp.where(odd_lat, one, other)
        here = (lane >= slot * WIDE) & (lane < (slot + 1) * WIDE)
        west_part = jnp.concatenate([own[slot, :, 0:128], edges[slot, :, 0:128]], axis=0)
        east_part = jnp.concatenate([own[slot, :, COLS - 128 :], edges[slot, :, COLS - 128 :]], axis=0)
        east_part = pltpu.roll(east_part, (WIDE + slot * WIDE) % 128, 1)
        if slot:
            west_part = pltpu.roll(west_part, slot * WIDE, 1)
        west = jnp.where(here, west_part, west)
        east = jnp.where(here, east_part, east)
    fill = jnp.zeros((128 - PAD_ROWS, 128), f32)
    sides[1] = jnp.concatenate([west, fill], axis=0).T[:STRIP, :]
    sides[0] = jnp.concatenate([east, fill], axis=0).T[:STRIP, :]
    for copy in fetch(((sides.at[odd], near_out), (sides.at[1 - odd], far_out)), out_sems):
        copy.wait()


def far_call(kernel, name, operands, results, scratch, work=None, here=(), near=(), near_out=()):
    placed = []
    specs = []
    out_spaces = [pltpu.VMEM if slot in near_out else pltpu.HBM for slot in range(len(results))]
    for slot, operand in enumerate(operands):
        if slot in here:
            space = pltpu.VMEM
        elif slot in near:
            space = pltpu.VMEM
            operand = pltpu.with_memory_space_constraint(operand, pltpu.VMEM)
        else:
            space = pltpu.HBM
            operand = pltpu.with_memory_space_constraint(operand, pltpu.HBM)
        placed.append(operand)
        specs.append(pl.BlockSpec(memory_space=space))
    return pl.pallas_call(
        kernel,
        out_shape=tuple(space(*result) for space, result in zip(out_spaces, results)),
        in_specs=specs,
        out_specs=tuple(pl.BlockSpec(memory_space=space) for space in out_spaces),
        scratch_shapes=scratch,
        compiler_params=pltpu.CompilerParams(vmem_limit_bytes=32 << 20),
        cost_estimate=work,
        name=name,
    )(*placed)


def cost(flops, moved):
    return pl.CostEstimate(flops=flops, bytes_accessed=moved, transcendentals=0)


def on_device(sea_height, trans_u, trans_v, depth, sea_mask, freshwater_flux, love_factor):
    north = jnp.asarray(north_tables())
    fields = (sea_height, trans_u, trans_v, depth, sea_mask, freshwater_flux)
    vmem = pltpu.VMEM
    copies = pltpu.SemaphoreType.DMA
    tile = ((ROWS, COLS), f32)
    strip = ((STRIP, COLS), f32)
    side = ((STRIP, 128), f32)
    messages = ((DEVS, 8, 128), f32)
    tiles = vmem((FIELDS, ROWS, COLS), f32)
    mask_tile = vmem((ROWS, COLS), jnp.int32)

    message, strip_near, strip_far, wave = far_call(
        forward_kernel,
        "forward",
        fields + (jnp.asarray(turn_tables()), jnp.asarray(step_tables()), jnp.asarray(area_table())),
        (messages, strip, strip, ((QUARTERS, 4, QUARTER, COLS), bf16)),
        [
            tiles,
            mask_tile,
            vmem((2, DEVS, COLS), f32),
            vmem((2, ORDERS, COLS), f32),
            vmem((ROWS, 128), f32),
            vmem(*messages),
            vmem((2, STRIP, COLS), f32),
            copies((9,)),
            copies((QUARTERS,)),
            copies((2,)),
        ],
        work=cost(6 * 2 * 1024 * 256 * 256, 3 << 20),
        near_out=(3,),
    )
    received = exchange(message)

    near_pairs = [(i, i ^ 1) for i in range(LATS)]
    far_pairs = [(i, ((i + 1) ^ 1) - 1) for i in range(1, LATS - 1)]
    from_near = lax.ppermute(strip_near, "lat", near_pairs)
    from_far = lax.ppermute(strip_far, "lat", far_pairs)

    gain_tiles = ((2 * len(PAIRS), ORDERS, TILE), f32)
    squares = ((ORDERS, DEG), f32)
    first_rows = ((ORDERS, HALF), f32)
    own_fields = ((FIELDS, ROWS, COLS), f32)
    gains, balance, start, own, bands = far_call(
        setup_kernel,
        "setup",
        fields
        + (
            jnp.asarray(row_tables()),
            love_factor.reshape(8, 128),
            jnp.asarray(balance_table()),
            jnp.asarray(seed_table()),
            north,
        ),
        (gain_tiles, squares, first_rows, own_fields, ((2, PAD_ROWS, 128), f32)),
        [
            mask_tile,
            vmem((8, 128), f32),
            vmem((ORDERS, DEVS), f32),
            vmem((3, 8, HALF), f32),
            copies((11,)),
        ],
        work=cost(2 << 20, 1 << 20),
        near_out=(0, 1, 2, 3, 4),
    )
    to_near, to_far, edges = far_call(
        column_kernel,
        "columns",
        (from_near, from_far, own),
        (side, side, ((FIELDS, 2 * WIDE, COLS), f32)),
        [vmem((2, STRIP, 128), f32), copies((2,))],
        here=(0, 1),
        near=(2,),
        near_out=(2,),
    )
    received, to_near, to_far = lax.optimization_barrier((received, to_near, to_far))
    table = ((2 * len(PAIRS) * TILE, HALF), bf16)
    (reply,) = far_call(
        legendre_kernel,
        "legendre",
        (received, gains, balance, start, north),
        (messages,),
        [vmem(*table), vmem(*table), vmem(*messages), copies((LATS,))],
        work=cost(6 * 2 * 64 * 8192 * 256, 9 << 20),
        here=(0, 4),
        near=(1, 2, 3),
    )
    answer = exchange(reply)

    near_lons = [(i, i ^ 1) for i in range(LONS)]
    far_lons = [(i, (((i + 1) ^ 1) - 1) % LONS) for i in range(LONS)]
    side_near = lax.ppermute(to_near, "lon", near_lons)
    side_far = lax.ppermute(to_far, "lon", far_lons)

    return far_call(
        finish_kernel,
        "finish",
        (answer, side_near, side_far, wave, own, edges, bands),
        (tile,) * 4,
        [
            vmem((FIELDS, PAD_ROWS, PAD_COLS), f32),
            vmem((4, ROWS, COLS), f32),
            copies((4,)),
        ],
        here=(0, 1, 2),
        near=(3, 4, 5, 6),
    )


def solution(mesh):
    tiles = P("lat", "lon")
    return jax.shard_map(
        on_device,
        mesh=mesh,
        in_specs=(tiles,) * 6 + (P(),),
        out_specs=(tiles,) * 4,
        check_vma=False,
    )
```
